128 devices in a mesh: dp: 32 (over x_hi, y, z), tensor: 4 (over x_lo, core).
Axes of the slice: x: 4 (x_hi: 2, x_lo: 2; x = x_hi * 2 + x_lo), y: 4, z: 4, core: 2. Of those that a mesh axis runs over, the one named last changes fastest.
Arguments:
- hidden_in: bfloat16 [32768, 1536], P(('dp', 'tensor')), may hold values from -6 to 6
- cotangent: bfloat16 [32768, 1536], P(('dp', 'tensor')), may hold values from -6 to 6
- norm_gain: float32 [1536], replicated, may hold values from 0.1 to 1.9
- w_z: bfloat16 [1536, 3072], P('dp', 'tensor'), may hold values from -0.15625 to 0.15625
- w_x: bfloat16 [1536, 3072], P('dp', 'tensor'), may hold values from -0.15625 to 0.15625
- w_bc: bfloat16 [1536, 256], P('dp'), may hold values from -0.15625 to 0.15625
- w_dt: bfloat16 [1536, 48], P('dp', 'tensor'), may hold values from -0.15625 to 0.15625
- conv_x: float32 [5, 3072], P(None, 'tensor'), may hold values from -3 to 3
- conv_bc: float32 [5, 256], replicated, may hold values from -3 to 3
- head_params: float32 [3, 48], P(None, 'tensor'), may hold values from -7 to 3, as said below
- gate_gain: float32 [3072], P('tensor'), may hold values from 0.1 to 1.9
- w_out: bfloat16 [3072, 1536], P('tensor', 'dp'), may hold values from -0.109375 to 0.109375
Outputs:
- output: bfloat16 [32768, 1536], P(('dp', 'tensor'))
- input_grad: float32 [32768, 1536], P(('dp', 'tensor'))
- grad_norm_gain: float32 [1536], replicated
- grad_w_z: float32 [1536, 3072], P('dp', 'tensor')
- grad_w_x: float32 [1536, 3072], P('dp', 'tensor')
- grad_w_bc: float32 [1536, 256], P('dp')
- grad_w_dt: float32 [1536, 48], P('dp', 'tensor')
- grad_conv_x: float32 [5, 3072], P(None, 'tensor')
- grad_conv_bc: float32 [5, 256], replicated
- grad_head: float32 [3, 48], P(None, 'tensor')
- grad_gate_gain: float32 [3072], P('tensor')
- grad_w_out: float32 [3072, 1536], P('tensor', 'dp')
The draws below stay inside these ranges and needn't reach their ends.
Inputs may be any that keep to these rules, and one draw needn't show every extreme that they name: `head_params`: row 0 holds logarithms of the heads' decay rates, row 1 the step-size biases, row 2 the skip weights.
All inputs are finite; a program needn't handle non-finite values.
Results may differ from the reference program's by a relative error of at most 0.0081.
Values may be sent and summed in bfloat16 or wider, within the bound.
No kernel may reach another device: no remote copies, remote signals or barrier semaphores. Data moves between devices by JAX's collectives and lax.ppermute only.
A program may use at most 128 MiB of HBM per device.

```python
import math
import jax
import jax.numpy as jnp
from jax import lax

D = 1536
H = 48
N = 128
K = 4
SPAN = 256
LEN = 1024
DI = 3072
TOKENS = 32768
N_DP = 32


def draw_head_params(key, part):
    key = jax.random.fold_in(key, 7)
    first, second, third = jax.random.split(key, 3)
    log_rates = jax.random.uniform(first, (H,), jnp.float32, 0.0, math.log(16.0))
    step_init = jnp.exp(jax.random.uniform(second, (H,), jnp.float32, math.log(0.001), math.log(0.1)))
    step_bias = step_init + jnp.log(-jnp.expm1(-step_init))
    skip_weight = jax.random.uniform(third, (H,), jnp.float32, 0.5, 1.5)
    return jnp.stack([log_rates, step_bias, skip_weight]).astype(jnp.float32)


def block_scale(rng, extent, shards, least, top_value):
    level, own = 1.0, jax.random.fold_in(rng, 6)
    for position, blocks in shards:
        heights = jnp.exp(jax.random.uniform(jax.random.fold_in(own, position), (blocks,), jnp.float32, least / len(shards), top_value / len(shards)))
        level = level * jnp.repeat(heights, extent[position] // blocks).reshape([-1 if axis == position else 1 for axis in range(len(extent))])
    return level


def gaussian(stream_key, shape, scale, reach, cuts=(), dtype=jnp.bfloat16):
    array = jax.random.normal(stream_key, shape, jnp.float32) * scale
    if len(cuts) > 0:
        array = block_scale(stream_key, shape, cuts, -0.22, 0.18) * array
    return jnp.clip(array, min=-reach, max=reach).astype(dtype)


def setup_inputs(seed: int = 0) -> dict:
    key_list = jax.random.split(jax.random.key(seed), 13)
    return {
        "hidden_in": gaussian(key_list[0], (TOKENS, D), 1.0, 6.0, ((0, 128),)),
        "cotangent": gaussian(key_list[1], (TOKENS, D), 1.0, 6.0, ((0, 128),)),
        "norm_gain": jnp.clip(1.0 + 0.18 * jax.random.normal(key_list[2], (D,), jnp.float32), 0.1, 1.9),
        "w_z": gaussian(key_list[3], (D, DI), D ** -0.5, 0.15625, ((0, 32), (1, 4))),
        "w_x": gaussian(key_list[4], (D, DI), D ** -0.5, 0.15625, ((0, 32), (1, 4))),
        "w_bc": gaussian(key_list[5], (D, 2 * N), D ** -0.5, 0.15625, ((0, 32),)),
        "w_dt": gaussian(key_list[6], (D, H), D ** -0.5, 0.15625, ((0, 32), (1, 4))),
        "conv_x": gaussian(key_list[7], (K + 1, DI), 0.5, 3.0, ((1, 4),), jnp.float32),
        "conv_bc": gaussian(key_list[8], (K + 1, 2 * N), 0.5, 3.0, (), jnp.float32),
        "head_params": draw_head_params(jax.random.fold_in(key_list[12], 71), 0),
        "gate_gain": jnp.clip(1.0 + 0.18 * jax.random.normal(key_list[10], (DI,), jnp.float32), 0.1, 1.9),
        "w_out": gaussian(key_list[11], (DI, D), DI ** -0.5, 0.109375, ((0, 4), (1, 32))),
    }


EPS = 1e-05

@jax.custom_vjp
def low(v):
    return lax.optimization_barrier(v.astype(jnp.bfloat16)).astype(jnp.float32)

@jax.custom_vjp
def low_back(v):
    return v

def low_keep(v):
    return (low(v), None)

def low_pass(kept, grad):
    return (grad,)

def back_keep(v):
    return (v, None)

def back_low(kept, grad):
    return (low(grad),)
low.defvjp(low_keep, low_pass)
low_back.defvjp(back_keep, back_low)

def matmul_hi(left, right):
    return jnp.dot(left, right, precision=lax.Precision.HIGHEST, preferred_element_type=jnp.float32)

def causal_conv(values, kernel):
    tap_count = kernel.shape[0] - 1
    length = values.shape[0]
    padded = jnp.pad(values, ((tap_count - 1, 0), (0, 0)))
    result = kernel[tap_count] + padded[0:length] * kernel[0]
    for offset in range(1, tap_count):
        result = result + padded[offset:offset + length] * kernel[offset]
    return result

def state_scan(inputs, steps_dt, rates, b_rows, c_rows):
    length = inputs.shape[0]
    head_count = steps_dt.shape[1]
    head_width = inputs.shape[1] // head_count
    state_width = b_rows.shape[1]
    block_count = length // SPAN
    x_blocks = inputs.reshape(block_count, SPAN, head_count, head_width)
    dt_blocks = steps_dt.reshape(block_count, SPAN, head_count)
    b_blocks = b_rows.reshape(block_count, SPAN, state_width)
    c_blocks = c_rows.reshape(block_count, SPAN, state_width)
    row_index = jnp.arange(SPAN)
    mask_3d = (row_index[:, None] >= row_index[None, :])[:, :, None]

    def one_block(carried, pieces):
        x_part, dt_part, b_part, c_part = pieces
        log_decay = jnp.cumsum(dt_part * rates, axis=0)
        spread = log_decay[:, None, :] - log_decay[None, :, :]
        decays = jnp.where(mask_3d, jnp.exp(jnp.where(mask_3d, spread, 0.0)), 0.0)
        scores = jnp.einsum('in,jn->ij', c_part, b_part, precision=lax.Precision.HIGHEST)
        weights = decays * scores[:, :, None] * dt_part[None, :, :]
        inside = jnp.einsum('ijh,jhp->ihp', weights, x_part, precision=lax.Precision.HIGHEST)
        carried_out = jnp.einsum('in,hnp->ihp', c_part, carried, precision=lax.Precision.HIGHEST) * jnp.exp(log_decay)[:, :, None]
        to_end = jnp.exp(log_decay[-1][None, :] - log_decay) * dt_part
        added_state = jnp.einsum('jn,jhp->hnp', b_part, x_part * to_end[:, :, None], precision=lax.Precision.HIGHEST)
        updated = carried * jnp.exp(log_decay[-1])[:, None, None] + added_state
        return (updated, inside + carried_out)
    initial = jnp.zeros((head_count, state_width, head_width), jnp.float32)
    last_state, y_blocks = lax.scan(jax.checkpoint(one_block), initial, (x_blocks, dt_blocks, b_blocks, c_blocks))
    return y_blocks.reshape(length, head_count * head_width)

def mixer_core(gate_pre, x_pre, bc_pre, dt_pre, conv_x, conv_bc, head_params):
    x_conv = jax.nn.silu(causal_conv(x_pre, conv_x))
    bc_conv = jax.nn.silu(causal_conv(bc_pre, conv_bc))
    state_width = bc_conv.shape[1] // 2
    steps_dt = jax.nn.softplus(dt_pre + head_params[1])
    rates = -jnp.exp(head_params[0])
    scanned = state_scan(x_conv, steps_dt, rates, bc_conv[:, :state_width], bc_conv[:, state_width:])
    head_count = steps_dt.shape[1]
    length = x_conv.shape[0]
    skipped = (x_conv.reshape(length, head_count, -1) * head_params[2][None, :, None]).reshape(length, -1)
    return (scanned + skipped) * jax.nn.silu(gate_pre)

def block_forward(resid, norm_gain, w_z, w_x, w_bc, w_dt, conv_x, conv_bc, head_params, gate_gain, w_out):
    inv_rms = lax.rsqrt(lax.optimization_barrier(jnp.mean(resid * resid, axis=1, keepdims=True)) + EPS)
    normed = low(resid * inv_rms * norm_gain)
    gate_pre = low_back(matmul_hi(normed, w_z))
    x_pre = low_back(matmul_hi(normed, w_x))
    bc_pre = low_back(matmul_hi(normed, w_bc))
    dt_pre = low_back(matmul_hi(normed, w_dt))
    gated = mixer_core(gate_pre, x_pre, bc_pre, dt_pre, conv_x, conv_bc, head_params)
    gate_rms = lax.rsqrt(lax.optimization_barrier(jnp.mean(gated * gated, axis=1, keepdims=True)) + EPS)
    normed_y = low(gated * gate_rms * gate_gain)
    return resid + matmul_hi(normed_y, w_out)

def reference(hidden_in, cotangent, norm_gain, w_z, w_x, w_bc, w_dt, conv_x, conv_bc, head_params, gate_gain, w_out):
    params = (norm_gain, w_z.astype(jnp.float32), w_x.astype(jnp.float32), w_bc.astype(jnp.float32), w_dt.astype(jnp.float32), conv_x, conv_bc, head_params, gate_gain, w_out.astype(jnp.float32))
    sequences = hidden_in.astype(jnp.float32).reshape(N_DP, LEN, D)
    cot_seqs = cotangent.astype(jnp.float32).reshape(N_DP, LEN, D)

    def one_sequence(totals, paired):
        resid, cot_rows = paired
        result, pull_back = jax.vjp(block_forward, resid, *params)
        grads = pull_back(cot_rows)
        summed = tuple((total + grad for total, grad in zip(totals, grads[1:])))
        return (summed, (result, grads[0]))
    zeros = tuple((jnp.zeros_like(param) for param in params))
    totals, (results, input_grads) = lax.scan(one_sequence, zeros, (sequences, cot_seqs))
    return (results.reshape(TOKENS, D).astype(jnp.bfloat16), input_grads.reshape(TOKENS, D), totals[0], totals[1], totals[2], totals[3], totals[4], totals[5], totals[6], totals[7], totals[8], totals[9])
```

```python
import jax
import jax.numpy as jnp
from jax import lax
from jax.sharding import Mesh, PartitionSpec as P

SPAN = 256
EPS = 1e-05
AXES = ("xh", "y", "z", "xl", "core")
DP = ("xh", "y", "z")
TN = ("xl", "core")
BF = jnp.bfloat16
F32 = jnp.float32


def causal_conv(values, kernel):
    tap_count = kernel.shape[0] - 1
    length = values.shape[0]
    padded = jnp.pad(values, ((tap_count - 1, 0), (0, 0)))
    result = kernel[tap_count] + padded[0:length] * kernel[0]
    for offset in range(1, tap_count):
        result = result + padded[offset : offset + length] * kernel[offset]
    return result


def state_scan(inputs, steps_dt, rates, b_rows, c_rows):
    length = inputs.shape[0]
    head_count = steps_dt.shape[1]
    head_width = inputs.shape[1] // head_count
    state_width = b_rows.shape[1]
    block_count = length // SPAN
    x_blocks = inputs.reshape(block_count, SPAN, head_count, head_width)
    dt_blocks = steps_dt.reshape(block_count, SPAN, head_count)
    b_blocks = b_rows.reshape(block_count, SPAN, state_width)
    c_blocks = c_rows.reshape(block_count, SPAN, state_width)
    row_index = jnp.arange(SPAN)
    mask_3d = (row_index[:, None] >= row_index[None, :])[:, :, None]

    def one_block(carried, pieces):
        x_part, dt_part, b_part, c_part = pieces
        log_decay = jnp.cumsum(dt_part * rates, axis=0)
        spread = log_decay[:, None, :] - log_decay[None, :, :]
        decays = jnp.where(mask_3d, jnp.exp(jnp.where(mask_3d, spread, 0.0)), 0.0)
        scores = jnp.einsum("in,jn->ij", c_part, b_part, precision=lax.Precision.HIGHEST)
        weights = decays * scores[:, :, None] * dt_part[None, :, :]
        inside = jnp.einsum("ijh,jhp->ihp", weights, x_part, precision=lax.Precision.HIGHEST)
        carried_out = (
            jnp.einsum("in,hnp->ihp", c_part, carried, precision=lax.Precision.HIGHEST)
            * jnp.exp(log_decay)[:, :, None]
        )
        to_end = jnp.exp(log_decay[-1][None, :] - log_decay) * dt_part
        added_state = jnp.einsum(
            "jn,jhp->hnp", b_part, x_part * to_end[:, :, None], precision=lax.Precision.HIGHEST
        )
        updated = carried * jnp.exp(log_decay[-1])[:, None, None] + added_state
        return (updated, inside + carried_out)

    initial = jnp.zeros((head_count, state_width, head_width), F32)
    last_state, y_blocks = lax.scan(
        jax.checkpoint(one_block), initial, (x_blocks, dt_blocks, b_blocks, c_blocks)
    )
    return y_blocks.reshape(length, head_count * head_width)


def mixer_inner(x_pre, bc_pre, dt_pre, conv_x, conv_bc, head_params):
    x_conv = jax.nn.silu(causal_conv(x_pre, conv_x))
    bc_conv = jax.nn.silu(causal_conv(bc_pre, conv_bc))
    state_width = bc_conv.shape[1] // 2
    steps_dt = jax.nn.softplus(dt_pre + head_params[1])
    rates = -jnp.exp(head_params[0])
    scanned = state_scan(
        x_conv, steps_dt, rates, bc_conv[:, :state_width], bc_conv[:, state_width:]
    )
    head_count = steps_dt.shape[1]
    length = x_conv.shape[0]
    skipped = (x_conv.reshape(length, head_count, -1) * head_params[2][None, :, None]).reshape(
        length, -1
    )
    return scanned + skipped


def contract(left, right, left_dim, right_dim):
    return lax.dot_general(
        left, right, (((left_dim,), (right_dim,)), ((), ())), preferred_element_type=F32
    )


def swap(value, axis):
    return lax.ppermute(value, axis, [(0, 1), (1, 0)])


def gather_dp(shard):
    count = lax.axis_size(DP)
    spread = jnp.broadcast_to(shard[None], (count,) + shard.shape)
    got = lax.all_to_all(spread, DP, 0, 0, tiled=True)
    return got.reshape((count * shard.shape[0],) + shard.shape[1:])


def scatter_dp(partial):
    count = lax.axis_size(DP)
    got = lax.all_to_all(partial, DP, 0, 0, tiled=True)
    return got.reshape((count, -1) + partial.shape[1:]).astype(F32).sum(axis=0)


def gather_tn(own):
    far = swap(own, "xl")
    first = lax.axis_index("xl") == 0
    pair = jnp.stack([jnp.where(first, own, far), jnp.where(first, far, own)])
    other = swap(pair, "core")
    even = lax.axis_index("core") == 0
    both = jnp.stack([jnp.where(even, pair, other), jnp.where(even, other, pair)], axis=1)
    return both.reshape((-1,) + own.shape[1:])


def sum_tn(value):
    total = value
    for mask in (1, 2, 3):
        total = total + lax.ppermute(value, TN, [(i, i ^ mask) for i in range(4)])
    return total


def scatter_tn(partial):
    rows = partial.shape[0] // 4
    split = partial.reshape((2, 2, rows) + partial.shape[1:])
    core, xl = lax.axis_index("core"), lax.axis_index("xl")
    keep = lax.dynamic_index_in_dim(split, core, 1, keepdims=False)
    send = lax.dynamic_index_in_dim(split, 1 - core, 1, keepdims=False).astype(BF)
    half = keep + swap(send, "core").astype(F32)
    keep = lax.dynamic_index_in_dim(half, xl, 0, keepdims=False)
    send = lax.dynamic_index_in_dim(half, 1 - xl, 0, keepdims=False).astype(BF)
    return keep + swap(send, "xl").astype(F32)


def on_device(
    hidden_in,
    cotangent,
    norm_gain,
    w_z,
    w_x,
    w_bc,
    w_dt,
    conv_x,
    conv_bc,
    head_params,
    gate_gain,
    w_out,
):
    wide = w_x.shape[1]
    states = w_bc.shape[1]
    quarter = states // 4
    heads = w_dt.shape[1]
    rank = lax.axis_index(TN)

    first = jnp.concatenate([w_x, w_bc, w_dt], axis=1)
    full_first = gather_dp(first)
    second = jnp.concatenate([w_z, w_out.T], axis=1)
    full_second = gather_dp(second)
    full_x = full_first[:, :wide]
    full_bc = full_first[:, wide : wide + states]
    full_dt = full_first[:, wide + states :]
    full_z = full_second[:, :wide]
    full_out = full_second[:, wide:]
    tokens = gather_tn(hidden_in).astype(F32)
    cot_all = gather_tn(cotangent)

    resid = hidden_in.astype(F32)
    inv_rms = lax.rsqrt(jnp.mean(resid * resid, axis=1, keepdims=True) + EPS)
    inv_all = lax.rsqrt(jnp.mean(tokens * tokens, axis=1, keepdims=True) + EPS)
    normed = (tokens * inv_all * norm_gain).astype(BF)

    x_pre = jnp.dot(normed, full_x, preferred_element_type=F32)
    bc_pre = jnp.dot(normed, full_bc, preferred_element_type=F32)
    dt_pre = jnp.dot(normed, full_dt, preferred_element_type=F32)
    mixed, mixer_back = jax.vjp(
        mixer_inner, x_pre, bc_pre, dt_pre, conv_x, conv_bc, head_params
    )
    gate_pre = jnp.dot(normed, full_z, preferred_element_type=F32)
    gate_sig = jax.nn.sigmoid(gate_pre)
    gate_act = gate_pre * gate_sig
    gated = mixed * gate_act
    d_normed_y = contract(cot_all, full_out, 1, 0)
    scaled = d_normed_y * gate_gain
    width_all = 4 * wide
    sums = sum_tn(jnp.stack([jnp.sum(gated * gated, axis=1), jnp.sum(gated * scaled, axis=1)]))
    gate_rms = lax.rsqrt(sums[0] / width_all + EPS)[:, None]
    inner = sums[1][:, None]
    normed_y = (gated * gate_rms * gate_gain).astype(BF)
    grad_gate_part = jnp.sum(d_normed_y * gated * gate_rms, axis=0)
    d_gated = gate_rms * scaled - gated * (gate_rms * gate_rms * gate_rms) * inner / width_all
    gate_low = (d_gated * mixed * (gate_sig * (1 + gate_pre * (1 - gate_sig)))).astype(BF)

    grad_z_full = contract(normed, gate_low, 0, 0)
    grad_out_full = contract(cot_all, normed_y, 0, 0)
    early = scatter_dp(jnp.concatenate([grad_z_full, grad_out_full], axis=1).astype(BF))
    grad_w_z = early[:, :wide]
    grad_w_out = early[:, wide:].T

    partial_out = contract(normed_y, full_out, 1, 1)
    output = (resid + scatter_tn(partial_out)).astype(BF)

    d_x, d_bc_part, d_dt, grad_conv_x_part, grad_conv_bc_part, grad_head_part = mixer_back(
        d_gated * gate_act
    )
    x_low = d_x.astype(BF)
    dt_low = d_dt.astype(BF)
    bc_part = d_bc_part.astype(BF)
    by_quarter = d_bc_part.reshape(-1, 4, quarter).transpose(1, 0, 2)
    bc_low = scatter_tn(by_quarter.reshape(-1, quarter)).astype(BF)

    late_low = jnp.concatenate([x_low, bc_low, dt_low], axis=1)
    grad_late = contract(normed, late_low, 0, 0)
    gain_part = jnp.sum(grad_z_full * full_z.astype(F32), axis=1) + jnp.sum(
        grad_late[:, :wide] * full_x.astype(F32), axis=1
    )
    own_bc = lax.dynamic_slice_in_dim(full_bc, rank * quarter, quarter, 1)
    gain_part = gain_part + jnp.sum(grad_late[:, wide : wide + quarter] * own_bc, axis=1)
    gain_part = gain_part + jnp.sum(grad_late[:, wide + quarter :] * full_dt, axis=1)
    gain_part = gain_part / norm_gain
    vector = jnp.concatenate(
        [
            gain_part,
            grad_conv_bc_part.reshape(-1),
            grad_conv_x_part.reshape(-1),
            grad_head_part.reshape(-1),
            grad_gate_part,
        ]
    )
    block = w_x.shape[0]
    columns = -(-vector.shape[0] // block)
    vector = jnp.pad(vector, (0, columns * block - vector.shape[0])).reshape(1, block, columns)
    count = lax.axis_size(DP)
    vector = jnp.broadcast_to(vector, (count, block, columns)).reshape(count * block, columns)
    late = scatter_dp(jnp.concatenate([grad_late, vector], axis=1).astype(BF))
    grad_w_x = late[:, :wide]
    bc_own = late[:, wide : wide + quarter]
    grad_w_dt = late[:, wide + quarter : wide + quarter + heads]
    vector = late[:, wide + quarter + heads :].reshape(-1)
    sizes = [norm_gain.size, conv_bc.size, conv_x.size, head_params.size, gate_gain.size]
    starts = [sum(sizes[:i]) for i in range(len(sizes) + 1)]
    shared = sum_tn(vector[: starts[2]])
    grad_norm_gain = shared[: starts[1]]
    grad_conv_bc = shared[starts[1] :].reshape(conv_bc.shape)
    grad_conv_x = vector[starts[2] : starts[3]].reshape(conv_x.shape)
    grad_head = vector[starts[3] : starts[4]].reshape(head_params.shape)
    grad_gate_gain = vector[starts[4] : starts[5]]
    parts = [bc_own] + [
        lax.ppermute(bc_own, TN, [(i, i ^ mask) for i in range(4)]) for mask in (1, 2, 3)
    ]
    stacked = jnp.stack(parts)
    order = jnp.arange(4) ^ rank
    grad_w_bc = jnp.take(stacked, order, axis=0).transpose(1, 0, 2).reshape(block, states)

    partial_in = contract(gate_low, full_z, 1, 1) + contract(
        late_low, jnp.concatenate([full_x, own_bc, full_dt], axis=1), 1, 1
    )
    d_normed = scatter_tn(partial_in)
    d_scaled = d_normed * norm_gain
    cubed = inv_rms * inv_rms * inv_rms
    input_grad = (
        inv_rms * d_scaled
        - resid * cubed * jnp.sum(resid * d_scaled, axis=1, keepdims=True) / resid.shape[1]
        + cotangent.astype(F32)
    )
    return (
        output,
        input_grad,
        grad_norm_gain,
        grad_w_z,
        grad_w_x,
        grad_w_bc,
        grad_w_dt,
        grad_conv_x,
        grad_conv_bc,
        grad_head,
        grad_gate_gain,
        grad_w_out,
    )


def solution(mesh):
    fine = Mesh(mesh.devices.reshape(2, 4, 4, 2, 2), AXES)
    placed = (
        P(AXES, None),
        P(AXES, None),
        P(),
        P(DP, TN),
        P(DP, TN),
        P(DP, None),
        P(DP, TN),
        P(None, TN),
        P(),
        P(None, TN),
        P(TN),
        P(TN, DP),
    )
    return jax.shard_map(
        on_device,
        mesh=fine,
        in_specs=placed,
        out_specs=(
            P(AXES, None),
            P(AXES, None),
            P(),
            P(DP, TN),
            P(DP, TN),
            P(DP, None),
            P(DP, TN),
            P(None, TN),
            P(),
            P(None, TN),
            P(TN),
            P(TN, DP),
        ),
        check_vma=False,
    )
```

```python
import functools
import jax
import jax.numpy as jnp
from jax import lax
from jax.experimental import pallas as pl
from jax.experimental.pallas import tpu as pltpu
from jax.sharding import Mesh, PartitionSpec as P

EPS = 1e-05
AXES = ("xh", "y", "z", "xl", "core")
DP = ("xh", "y", "z")
TN = ("xl", "core")
GROUP = ("xh", "xl", "core")
PLANE = ("y", "z")
BF = jnp.bfloat16
F32 = jnp.float32
HI = lax.Precision.HIGHEST
SPAN = 128
SCALE = 1.15e9
INNER = 768
VMEM_LIMIT = 50 * 1024 * 1024


def nn(left, right):
    return lax.dot_general(left, right, (((1,), (0,)), ((), ())), preferred_element_type=F32)


def nt(left, right):
    return lax.dot_general(left, right, (((1,), (1,)), ((), ())), preferred_element_type=F32)


def exact(left, right):
    return lax.dot_general(
        left, right, (((1,), (0,)), ((), ())), precision=HI, preferred_element_type=F32
    )


def exact_nt(left, right):
    return lax.dot_general(
        left, right, (((1,), (1,)), ((), ())), precision=HI, preferred_element_type=F32
    )


def halves(value):
    high = value.astype(BF)
    low = (value - high.astype(F32)).astype(BF)
    return high, low


def expand(value, spread):
    high, low = halves(value)
    return nn(jnp.concatenate([high, low], axis=1), spread)


def by_head(value, spread):
    width = spread.shape[0] // 2
    high, low = halves(value)
    return nt(high, spread[:width]) + nt(low, spread[:width])


def sigmoid(value):
    return 1.0 / (1.0 + jnp.exp(-value))


def softplus(value):
    return jnp.maximum(value, 0.0) + jnp.log1p(jnp.exp(-jnp.abs(value)))


def conv_rows(ext_ref, taps):
    total = taps[4:5] + ext_ref[5 : 5 + SPAN] * taps[0:1]
    for k in range(1, 4):
        total = total + ext_ref[5 + k : 5 + k + SPAN] * taps[k : k + 1]
    return total


def scan_parts(ext_ref, pre_dt, taps, head, spread, tri, inner):
    conv = conv_rows(ext_ref, taps)
    sig = sigmoid(conv)
    xbc = conv * sig
    raw = pre_dt + head[1:2]
    step = softplus(raw)
    decay = exact(tri, step * head[0:1])
    last = decay[SPAN - 1 : SPAN]
    grown = expand(jnp.concatenate([step, jnp.exp(decay), jnp.exp(last - decay)], axis=0), spread)
    step_x, start_x, end_x = grown[:SPAN], grown[SPAN : 2 * SPAN], grown[2 * SPAN :]
    return conv, sig, xbc, raw, step, decay, step_x, start_x, end_x


def forward_kernel(pre_ref, taps_ref, head_ref, skip_ref, spread_ref, y_ref, kept_ref, ext_ref, state_ref):
    inner = y_ref.shape[1]
    both = ext_ref.shape[1]

    @pl.when(pl.program_id(0) == 0)
    def _():
        ext_ref[0:8] = jnp.zeros((8, both), F32)
        state_ref[...] = jnp.zeros_like(state_ref)

    ext_ref[8 : 8 + SPAN] = pre_ref[:, :both]
    rows = lax.broadcasted_iota(jnp.int32, (SPAN, SPAN), 0)
    cols = lax.broadcasted_iota(jnp.int32, (SPAN, SPAN), 1)
    keep = rows >= cols
    tri = jnp.where(keep, 1.0, 0.0).astype(F32)
    spread = spread_ref[...]
    conv, sig, xbc, raw, step, decay, step_x, start_x, end_x = scan_parts(
        ext_ref, pre_ref[:, both:], taps_ref[...], head_ref[...], spread, tri, inner
    )
    ext_ref[0:8] = ext_ref[SPAN : SPAN + 8]
    state_width = (both - inner) // 2
    x = xbc[:, :inner]
    b = xbc[:, inner : inner + state_width]
    c = xbc[:, inner + state_width :]
    decay_t = decay.T
    scaled = x * step_x
    low = scaled.astype(BF)
    scores = exact_nt(c, b)
    state = state_ref[...]
    state_low = state.astype(BF)
    kept_ref[...] = state_low
    carried = nn(c.astype(BF), state_low) * start_x + x * skip_ref[...]
    left = cols < 64
    for pair in range(inner // 128):
        at = slice(128 * pair, 128 * pair + 128)
        x_pair = low[:, at]
        found = []
        for h in (2 * pair, 2 * pair + 1):
            gap = decay[:, h : h + 1] - decay_t[h : h + 1]
            weight = jnp.exp(jnp.where(keep, gap, -1e30)) * scores
            found.append(nn(weight.astype(BF), x_pair))
        y_ref[:, at] = jnp.where(left, found[0], found[1]) + carried[:, at]
    state_ref[...] = state * start_x[SPAN - 1 : SPAN] + nn(
        b.T.astype(BF), (scaled * end_x).astype(BF)
    )


def backward_kernel(
    pre_ref, before_ref, dy_ref, kept_ref, taps_ref, head_ref, skip_ref, spread_ref,
    late_ref, conv_grad_ref, head_grad_ref,
    ext_ref, dext_ref, dstate_ref, skip_sum_ref,
):
    inner = dy_ref.shape[1]
    both = ext_ref.shape[1]
    steps = pl.num_programs(0)
    at_step = pl.program_id(0)
    chunk = steps - 1 - at_step

    @pl.when(at_step == 0)
    def _():
        dext_ref[SPAN : SPAN + 8] = jnp.zeros((8, both), F32)
        dstate_ref[...] = jnp.zeros_like(dstate_ref)
        skip_sum_ref[...] = jnp.zeros_like(skip_sum_ref)
        conv_grad_ref[...] = jnp.zeros_like(conv_grad_ref)
        head_grad_ref[...] = jnp.zeros_like(head_grad_ref)

    ext_ref[8 : 8 + SPAN] = pre_ref[:, :both]
    ext_ref[0:8] = jnp.where(chunk == 0, 0.0, before_ref[:, :both])
    rows = lax.broadcasted_iota(jnp.int32, (SPAN, SPAN), 0)
    cols = lax.broadcasted_iota(jnp.int32, (SPAN, SPAN), 1)
    tri = jnp.where(rows >= cols, 1.0, 0.0).astype(F32)
    upper = jnp.where(cols >= rows, 1.0, 0.0).astype(F32)
    keep = cols >= rows
    spread = spread_ref[...]
    taps = taps_ref[...]
    head = head_ref[...]
    conv, sig, xbc, raw, step, decay, step_x, start_x, end_x = scan_parts(
        ext_ref, pre_ref[:, both:], taps, head, spread, tri, inner
    )
    state_width = (both - inner) // 2
    x = xbc[:, :inner]
    b = xbc[:, inner : inner + state_width]
    c = xbc[:, inner + state_width :]
    b_low, c_low = b.astype(BF), c.astype(BF)
    decay_t = decay.T
    scaled = x * step_x
    low = scaled.astype(BF)
    scores = exact_nt(b, c)
    dy = dy_ref[...].astype(F32)
    dy_low = dy.astype(BF)
    kept = kept_ref[...]
    dstate = dstate_ref[...]
    dstate_low = dstate.astype(BF)
    left = cols < 64
    wide_rows = lax.broadcasted_iota(jnp.int32, (SPAN, SPAN), 0)
    d_scores = jnp.zeros((SPAN, SPAN), F32)
    into = jnp.zeros((SPAN, SPAN), F32)
    out_of = jnp.zeros((SPAN, SPAN), F32)
    pieces = []
    none = jnp.zeros((SPAN, 128), BF)
    for pair in range(inner // 128):
        at = slice(128 * pair, 128 * pair + 128)
        x_pair = low[:, at]
        dy_pair = dy_low[:, at]
        found = []
        for side, h in enumerate((2 * pair, 2 * pair + 1)):
            gap = decay_t[h : h + 1] - decay[:, h : h + 1]
            fall = jnp.exp(jnp.where(keep, gap, -1e30))
            mine = jnp.where(left if side == 0 else ~left, dy_pair, none)
            back = nt(x_pair, mine) * fall
            d_scores = d_scores + back
            both_ways = back * scores
            into = jnp.where(wide_rows == h, jnp.sum(both_ways, axis=0, keepdims=True), into)
            out_of = jnp.where(cols == h, jnp.sum(both_ways, axis=1, keepdims=True), out_of)
            found.append(nn((fall * scores).astype(BF), dy_pair))
        pieces.append(jnp.where(left, found[0], found[1]))
    inside = jnp.concatenate(pieces, axis=1)
    dy_start = dy * start_x
    dy_start_low = dy_start.astype(BF)
    from_state = nn(c_low, kept)
    scaled_end = scaled * end_x
    d_end = nn(b_low, dstate_low)
    d_scaled = inside + d_end * end_x
    pair_start = by_head(dy_start * from_state, spread)
    pair_end = by_head(scaled_end * d_end, spread)
    d_scores_low = d_scores.astype(BF)
    d_c = nn(d_scores.T.astype(BF), b_low) + nt(dy_start_low, kept)
    d_b = nn(d_scores_low, c_low) + nt(scaled_end.astype(BF), dstate_low)
    through = jnp.sum(kept.astype(F32) * dstate, axis=0, keepdims=True)
    through = by_head(jnp.broadcast_to(through * start_x[SPAN - 1 : SPAN], (8, inner)), spread)[0:1]
    at_end = jnp.sum(pair_end, axis=0, keepdims=True) + through
    d_decay = into.T - out_of + pair_start - pair_end
    d_decay = d_decay + jnp.where(rows == SPAN - 1, at_end, 0.0)
    d_log = exact(upper, d_decay)
    d_step = by_head(d_scaled * x, spread) + d_log * head[0:1]
    d_raw = d_step * sigmoid(raw)
    dstate_ref[...] = dstate * start_x[SPAN - 1 : SPAN] + nn(c.T.astype(BF), dy_start_low)
    late_ref[:, both:] = d_raw.astype(BF)
    head_grad_ref[0:1] += jnp.sum(d_log * step, axis=0, keepdims=True) * head[0:1]
    head_grad_ref[1:2] += jnp.sum(d_raw, axis=0, keepdims=True)
    skip_sum_ref[0:1] += jnp.sum(dy * x, axis=0, keepdims=True)
    dx = d_scaled * step_x + dy * skip_ref[...]
    d_conv = jnp.concatenate([dx, d_b, d_c], axis=1) * (sig * (1.0 + conv * (1.0 - sig)))
    dext_ref[0:SPAN] = d_conv
    d_pre = dext_ref[3 : 3 + SPAN] * taps[0:1]
    for k in range(1, 4):
        d_pre = d_pre + dext_ref[3 - k : 3 - k + SPAN] * taps[k : k + 1]
    for k in range(4):
        conv_grad_ref[k : k + 1] += jnp.sum(
            d_conv * ext_ref[5 + k : 5 + k + SPAN], axis=0, keepdims=True
        )
    conv_grad_ref[4:5] += jnp.sum(d_conv, axis=0, keepdims=True)
    dext_ref[SPAN : SPAN + 8] = dext_ref[0:8]
    late_ref[:, :both] = d_pre.astype(BF)

    @pl.when(at_step == steps - 1)
    def _():
        head_grad_ref[2:3] += by_head(
            jnp.broadcast_to(skip_sum_ref[0:1], (8, inner)), spread
        )[0:1]


def whole(shape):
    return pl.BlockSpec(shape, lambda *_: (0,) * len(shape))


def column(rows, width, shift=0):
    return pl.BlockSpec((rows, width), lambda j, *_: (0, j + shift))


def shape_of(shape, dtype):
    return jax.ShapeDtypeStruct(shape, dtype)


def params(*semantics):
    return pltpu.CompilerParams(
        dimension_semantics=semantics or None, vmem_limit_bytes=VMEM_LIMIT
    )


def lasting(us):
    return pl.CostEstimate(flops=int(us * SCALE), bytes_accessed=1024, transcendentals=0)


def place_kernel(normalise, meta_ref, gain_ref, *refs):
    blocks, out_ref, flip_ref = refs[:4], refs[4], refs[5]
    rows, width = blocks[0].shape
    half = width // 2
    core = meta_ref[4]
    first = pl.multiple_of(core * half, 128)
    second = pl.multiple_of((1 - core) * half, 128)
    for k, block in enumerate(blocks):
        at = pl.multiple_of(meta_ref[k] * rows, rows)
        value = block[...].astype(F32)
        if normalise:
            scale = lax.rsqrt(jnp.mean(value * value, axis=1, keepdims=True) + EPS)
            value = value * scale * gain_ref[...]
        low = value.astype(BF)
        out_ref[pl.ds(at, rows), pl.ds(first, half)] = low[:, :half]
        out_ref[pl.ds(at, rows), pl.ds(second, half)] = low[:, half:]
        flip = value.T.astype(BF)
        flip_ref[pl.ds(first, half), pl.ds(at, rows)] = flip[:half]
        flip_ref[pl.ds(second, half), pl.ds(at, rows)] = flip[half:]


def place(meta, gain, blocks, normalise):
    rows, width = blocks[0].shape
    vmem = pl.BlockSpec(memory_space=pltpu.VMEM)
    return pl.pallas_call(
        functools.partial(place_kernel, normalise),
        in_specs=[pl.BlockSpec(memory_space=pltpu.SMEM)] + [vmem] * 5,
        out_specs=[vmem, vmem],
        out_shape=[shape_of((4 * rows, width), BF), shape_of((width, 4 * rows), BF)],
        compiler_params=params(),
        cost_estimate=lasting(6),
        name="place_normed" if normalise else "place_cotangent",
    )(meta, gain, *blocks)


def project_kernel(tokens_ref, mine_ref, other_ref, out_ref):
    half = mine_ref.shape[0]
    out_ref[...] = nn(tokens_ref[:, :half], mine_ref[...]) + nn(
        tokens_ref[:, half:], other_ref[...]
    )


def project(tokens, mine, other):
    half = mine.shape[0]
    length = tokens.shape[0]
    tile = 384
    skip = 2 * INNER // tile
    columns = mine.shape[1] - 2 * INNER
    return pl.pallas_call(
        project_kernel,
        grid=(columns // tile,),
        in_specs=[whole(tokens.shape), column(half, tile, skip), column(half, tile, skip)],
        out_specs=column(length, tile),
        out_shape=shape_of((length, columns), F32),
        compiler_params=params("arbitrary"),
        cost_estimate=lasting(6),
        name="project_in",
    )(tokens, mine, other)


def gate_sums_kernel(
    tokens_ref, cot_ref, zm_ref, zo_ref, om_ref, oo_ref, y_ref, gain_ref, z_ref, dy_ref, sums_ref
):
    half = zm_ref.shape[0]
    z = nn(tokens_ref[:, :half], zm_ref[...]) + nn(tokens_ref[:, half:], zo_ref[...])
    dy = nn(cot_ref[:, :half], om_ref[...]) + nn(cot_ref[:, half:], oo_ref[...])
    z_ref[...] = z
    dy_ref[...] = dy
    gated = y_ref[...] * (z * sigmoid(z))
    ones = jnp.ones((8, z.shape[1]), BF)
    found = []
    for value in (gated * gated, gated * (dy * gain_ref[...])):
        high, low = halves(value)
        found.append(nt(ones, high) + nt(ones, low))
    row = lax.broadcasted_iota(jnp.int32, found[0].shape, 0)
    total = jnp.where(row == 0, found[0], found[1])

    @pl.when(pl.program_id(0) == 0)
    def _():
        sums_ref[...] = total

    @pl.when(pl.program_id(0) > 0)
    def _():
        sums_ref[...] += total


def gate_sums(tokens, cot, mine, other, y, gain):
    length, inner = y.shape
    half = mine.shape[0]
    tile = 256
    steps = inner // tile
    return pl.pallas_call(
        gate_sums_kernel,
        grid=(steps,),
        in_specs=[
            whole(tokens.shape),
            whole(cot.shape),
            column(half, tile),
            column(half, tile),
            column(half, tile, steps),
            column(half, tile, steps),
            column(length, tile),
            column(1, tile),
        ],
        out_specs=[column(length, tile), column(length, tile), whole((8, length))],
        out_shape=[
            shape_of((length, inner), F32),
            shape_of((length, inner), F32),
            shape_of((8, length), F32),
        ],
        compiler_params=params("arbitrary"),
        cost_estimate=lasting(9),
        name="gate_sums",
    )(tokens, cot, mine, other, mine, other, y, gain)


def gate_back_kernel(
    width_all, s0, s1, s2, s3, z_ref, dy_ref, y_ref, gain_ref, tokens_t_ref, cot_t_ref,
    normed_ref, gate_ref, dscan_ref, gain_grad_ref, keep_ref, send_ref,
):
    sums = (s0[...] + s1[...]) + (s2[...] + s3[...])
    flat = sums.T
    rms = lax.rsqrt(flat[:, 0:1] / width_all + EPS)
    inner = flat[:, 1:2] * (rms * rms * rms / width_all)
    z = z_ref[...]
    y = y_ref[...]
    dy = dy_ref[...]
    gain = gain_ref[...]
    sig = sigmoid(z)
    act = z * sig
    gated = y * act
    unit = gated * rms
    normed = (unit * gain).astype(BF)
    normed_ref[...] = normed
    gain_grad_ref[...] = jnp.broadcast_to(
        jnp.sum(dy * unit, axis=0, keepdims=True), gain_grad_ref.shape
    )
    d_gated = rms * (dy * gain) - gated * inner
    dscan_ref[...] = d_gated * act
    gate = (d_gated * y * (sig * (1.0 + z * (1.0 - sig)))).astype(BF)
    gate_ref[...] = gate
    half = tokens_t_ref.shape[0] // 2
    keep_ref[0] = nn(tokens_t_ref[:half], gate)
    keep_ref[1] = nn(cot_t_ref[:half], normed)
    send_ref[0] = nn(tokens_t_ref[half:], gate).astype(BF)
    send_ref[1] = nn(cot_t_ref[half:], normed).astype(BF)


def gate_back(width_all, sums, z, dy, y, gain, tokens_t, cot_t):
    length, inner = y.shape
    half = tokens_t.shape[0] // 2
    tile = 256
    pile = pl.BlockSpec((2, half, tile), lambda j: (0, 0, j))
    return pl.pallas_call(
        functools.partial(gate_back_kernel, width_all),
        grid=(inner // tile,),
        in_specs=[whole((8, length))] * 4
        + [column(length, tile)] * 3
        + [column(1, tile), whole(tokens_t.shape), whole(cot_t.shape)],
        out_specs=[column(length, tile)] * 3 + [column(8, tile), pile, pile],
        out_shape=[
            shape_of((length, inner), BF),
            shape_of((length, inner), BF),
            shape_of((length, inner), F32),
            shape_of((8, inner), F32),
            shape_of((2, half, inner), F32),
            shape_of((2, half, inner), BF),
        ],
        compiler_params=params("arbitrary"),
        cost_estimate=lasting(12),
        name="gate_back",
    )(*sums, z, dy, y, gain, tokens_t, cot_t)


def project_out_kernel(meta_ref, normed_ref, om_ref, oo_ref, *outs):
    rows = outs[0].shape[0]
    half = om_ref.shape[0]
    for k, out in enumerate(outs):
        left = normed_ref[pl.ds(pl.multiple_of(meta_ref[k] * rows, rows), rows), :]
        out[:, :half] = nt(left, om_ref[...]).astype(BF)
        out[:, half:] = nt(left, oo_ref[...]).astype(BF)


def project_out(meta, normed_y, mine, other):
    length, inner = normed_y.shape
    half = mine.shape[0]
    rows = length // 4
    right = pl.BlockSpec((half, inner), lambda i: (0, 1))
    return pl.pallas_call(
        project_out_kernel,
        grid=(1,),
        in_specs=[pl.BlockSpec(memory_space=pltpu.SMEM), whole(normed_y.shape), right, right],
        out_specs=[whole((rows, 2 * half))] * 4,
        out_shape=[shape_of((rows, 2 * half), BF)] * 4,
        compiler_params=params("arbitrary"),
        cost_estimate=lasting(6),
        name="project_out",
    )(meta, normed_y, mine, other)


def project_back_kernel(meta_ref, late_ref, gate_ref, mine_ref, other_ref, tokens_ref, gain_ref, *outs):
    grad_ref = outs[4]
    rows = outs[0].shape[0]
    half = mine_ref.shape[0]
    inner = gate_ref.shape[1]
    core = meta_ref[4]
    sums = [jnp.zeros((1, half), F32), jnp.zeros((1, half), F32)]
    for k, out in enumerate(outs[:4]):
        at = pl.ds(pl.multiple_of(meta_ref[k] * rows, rows), rows)
        late, gate = late_ref[at, :], gate_ref[at, :]
        for side, right in enumerate((mine_ref, other_ref)):
            span = slice(side * half, side * half + half)
            found = nt(late, right[:, 2 * inner :]) + nt(gate, right[:, :inner])
            out[:, span] = found.astype(BF)
            sums[side] += jnp.sum(found * tokens_ref[at, span].astype(F32), axis=0, keepdims=True)
    for side in range(2):
        place = pl.multiple_of((core if side == 0 else 1 - core) * half, 128)
        grad_ref[:, pl.ds(place, half)] = jnp.broadcast_to(
            sums[side] / gain_ref[:, pl.ds(place, half)], (8, half)
        )


def project_back(meta, late, gate, mine, other, tokens, gain):
    length = late.shape[0]
    half = mine.shape[0]
    rows = length // 4
    return pl.pallas_call(
        project_back_kernel,
        grid=(1,),
        in_specs=[
            pl.BlockSpec(memory_space=pltpu.SMEM),
            whole(late.shape), whole(gate.shape), whole(mine.shape), whole(other.shape),
            whole(tokens.shape), whole(gain.shape),
        ],
        out_specs=[whole((rows, 2 * half))] * 4 + [whole((8, 2 * half))],
        out_shape=[shape_of((rows, 2 * half), BF)] * 4 + [shape_of((8, 2 * half), F32)],
        compiler_params=params("arbitrary"),
        cost_estimate=lasting(9),
        name="project_back",
    )(meta, late, gate, mine, other, tokens, gain)


def weight_grad_kernel(tokens_t_ref, late_ref, keep_ref, send_ref):
    half = keep_ref.shape[0]
    late = late_ref[...]
    keep_ref[...] = nn(tokens_t_ref[:half], late)
    send_ref[...] = nn(tokens_t_ref[half:], late).astype(BF)


def weight_grad(tokens_t, late):
    length, columns = late.shape
    half = tokens_t.shape[0] // 2
    tile = 384
    return pl.pallas_call(
        weight_grad_kernel,
        grid=(columns // tile,),
        in_specs=[whole(tokens_t.shape), column(length, tile)],
        out_specs=[column(half, tile)] * 2,
        out_shape=[shape_of((half, columns), F32), shape_of((half, columns), BF)],
        compiler_params=params("arbitrary"),
        cost_estimate=lasting(7),
        name="weight_grad",
    )(tokens_t, late)


def owner_total(xh_ref, blocks):
    total = sum(block[...].astype(F32) for block in blocks)
    half = total.shape[1] // 2
    turned = jnp.concatenate([total[:, half:], total[:, :half]], axis=1)
    return jnp.where(xh_ref[5] == 0, total, turned)


def output_kernel(meta_ref, b0, b1, b2, b3, hidden_ref, out_ref):
    mixed = owner_total(meta_ref, (b0, b1, b2, b3))
    out_ref[...] = (hidden_ref[...].astype(F32) + mixed).astype(BF)


def finish_output(meta, blocks, hidden):
    vmem = pl.BlockSpec(memory_space=pltpu.VMEM)
    return pl.pallas_call(
        output_kernel,
        in_specs=[pl.BlockSpec(memory_space=pltpu.SMEM)] + [vmem] * 5,
        out_specs=vmem,
        out_shape=shape_of(hidden.shape, BF),
        compiler_params=params(),
        cost_estimate=lasting(3),
        name="finish_output",
    )(meta, *blocks, hidden)


def input_kernel(meta_ref, b0, b1, b2, b3, hidden_ref, cot_ref, gain_ref, out_ref):
    scaled = owner_total(meta_ref, (b0, b1, b2, b3)) * gain_ref[...]
    resid = hidden_ref[...].astype(F32)
    inv = lax.rsqrt(jnp.mean(resid * resid, axis=1, keepdims=True) + EPS)
    along = jnp.mean(resid * scaled, axis=1, keepdims=True) * (inv * inv * inv)
    out_ref[...] = inv * scaled - resid * along + cot_ref[...].astype(F32)


def finish_input(meta, blocks, hidden, cot, gain):
    vmem = pl.BlockSpec(memory_space=pltpu.VMEM)
    return pl.pallas_call(
        input_kernel,
        in_specs=[pl.BlockSpec(memory_space=pltpu.SMEM)] + [vmem] * 7,
        out_specs=vmem,
        out_shape=shape_of(hidden.shape, F32),
        compiler_params=params(),
        cost_estimate=lasting(3),
        name="finish_input",
    )(meta, *blocks, hidden, cot, gain)


def mixer_tables(conv_x, conv_bc, head_params):
    heads = head_params.shape[1]
    inner = conv_x.shape[1]
    taps = jnp.pad(jnp.concatenate([conv_x, conv_bc], axis=1), ((0, 3), (0, 0)))
    head = jnp.stack([-jnp.exp(head_params[0]), head_params[1]])
    head = jnp.pad(head, ((0, 6), (0, 128 - heads)))
    skip = jnp.repeat(head_params[2], inner // heads)[None]
    owner = lax.broadcasted_iota(jnp.int32, (256, inner), 1) // (inner // heads)
    one = owner == lax.broadcasted_iota(jnp.int32, (256, inner), 0) % 128
    return taps, head, skip, one.astype(BF)


def mixer_forward(pre, taps, head, skip, spread):
    length, columns = pre.shape
    both = taps.shape[1]
    inner = skip.shape[1]
    steps = length // SPAN
    return pl.pallas_call(
        forward_kernel,
        grid=(steps,),
        in_specs=[
            pl.BlockSpec((SPAN, columns), lambda i: (i, 0)),
            whole(taps.shape), whole(head.shape), whole(skip.shape), whole(spread.shape),
        ],
        out_specs=[
            pl.BlockSpec((SPAN, inner), lambda i: (i, 0)),
            pl.BlockSpec((128, inner), lambda i: (i, 0)),
        ],
        out_shape=[shape_of((length, inner), F32), shape_of((steps * 128, inner), BF)],
        scratch_shapes=[pltpu.VMEM((SPAN + 8, both), F32), pltpu.VMEM((128, inner), F32)],
        compiler_params=params("arbitrary"),
        cost_estimate=lasting(13),
        name="mixer_forward",
    )(pre, taps, head, skip, spread)


def mixer_backward(pre, dy, kept, taps, head, skip, spread):
    length, columns = pre.shape
    both = taps.shape[1]
    inner = skip.shape[1]
    steps = length // SPAN
    last = steps - 1
    per = SPAN // 8
    return pl.pallas_call(
        backward_kernel,
        grid=(steps,),
        in_specs=[
            pl.BlockSpec((SPAN, columns), lambda i: (last - i, 0)),
            pl.BlockSpec((8, columns), lambda i: (jnp.maximum((last - i) * per - 1, 0), 0)),
            pl.BlockSpec((SPAN, inner), lambda i: (last - i, 0)),
            pl.BlockSpec((128, inner), lambda i: (last - i, 0)),
            whole(taps.shape), whole(head.shape), whole(skip.shape), whole(spread.shape),
        ],
        out_specs=[
            pl.BlockSpec((SPAN, columns), lambda i: (last - i, 0)),
            whole((8, both)),
            whole((8, 128)),
        ],
        out_shape=[
            shape_of((length, columns), BF),
            shape_of((8, both), F32),
            shape_of((8, 128), F32),
        ],
        scratch_shapes=[
            pltpu.VMEM((SPAN + 8, both), F32),
            pltpu.VMEM((SPAN + 8, both), F32),
            pltpu.VMEM((128, inner), F32),
            pltpu.VMEM((8, inner), F32),
        ],
        compiler_params=params("arbitrary"),
        cost_estimate=lasting(30),
        name="mixer_backward",
    )(pre, pre, dy, kept, taps, head, skip, spread)


CELLS = [(xh, xl, core) for xh in range(2) for xl in range(2) for core in range(2)]
TURNS = [(a, b) for a in range(2) for b in range(2)]


def moves(rule):
    return [(4 * c[0] + 2 * c[1] + c[2], 4 * d[0] + 2 * d[1] + d[2]) for c in CELLS for d in [rule(*c)]]


def permute(value, rule):
    return lax.ppermute(value, GROUP, moves(rule))


def trade(value):
    return permute(
        value, lambda xh, xl, core: (xh, xl, core) if xh == core else (1 - xh, xl, 1 - core)
    )


def swap_core(value):
    return lax.ppermute(value, "core", [(0, 1), (1, 0)])


def to_workers(value):
    return [
        permute(value, lambda xh, xl, core, a=a, b=b: (core ^ a, xl ^ b, xh)) for a, b in TURNS
    ]


def to_owners(blocks):
    return [
        permute(block, lambda xh, xl, core, a=a, b=b: (core, xl ^ b, xh ^ a))
        for block, (a, b) in zip(blocks, TURNS)
    ]


def around(value):
    return [value] + [
        permute(value, lambda xh, xl, core, a=a, b=b: (xh ^ a, xl ^ b, core)) for a, b in TURNS[1:]
    ]


def gather_plane(shard):
    count = lax.axis_size(PLANE)
    spread = jnp.broadcast_to(shard[None], (count,) + shard.shape)
    got = lax.all_to_all(spread, PLANE, 0, 0, tiled=True)
    return got.reshape((count * shard.shape[0],) + shard.shape[1:])


def exchange(blocks):
    return lax.all_to_all(blocks, PLANE, 0, 0, tiled=True)


def after(*values):
    return lax.optimization_barrier(values)


def on_device(
    hidden_in,
    cotangent,
    norm_gain,
    w_z,
    w_x,
    w_bc,
    w_dt,
    conv_x,
    conv_bc,
    head_params,
    gate_gain,
    w_out,
):
    block, wide = w_x.shape
    states = w_bc.shape[1]
    heads = w_dt.shape[1]
    both = wide + states
    xh, xl, core = (lax.axis_index(axis) for axis in GROUP)
    meta = jnp.stack([(xl ^ b) * 2 + (xh ^ a) for a, b in TURNS] + [core, xh]).astype(jnp.int32)
    gain = norm_gain[None]

    weights = trade(
        jnp.concatenate(
            [w_z, w_out.T, w_x, w_bc, jnp.pad(w_dt, ((0, 0), (0, 128 - heads)))], axis=1
        )
    )
    small = jnp.concatenate(
        [conv_x, gate_gain[None], jnp.pad(head_params, ((0, 0), (0, wide - heads)))[:2]]
    )
    small = trade(jnp.concatenate([small, jnp.pad(head_params[2:], ((0, 7), (0, wide - heads)))]))
    conv_x, gate_row, head_params = small[:5], small[5:6], small[6:9, :heads]
    taps, head, skip, spread = mixer_tables(conv_x, conv_bc, head_params)

    mine = gather_plane(weights)
    hidden, weights = after(hidden_in, weights)
    hidden_blocks = to_workers(hidden)
    mine, hidden_blocks, cot = after(mine, hidden_blocks, cotangent)
    cot_blocks = to_workers(cot)
    tokens, tokens_t = place(meta, gain, hidden_blocks, True)
    other = swap_core(mine)

    pre = project(tokens, mine, other)
    y, kept = mixer_forward(pre, taps, head, skip, spread)
    y, cot_blocks = after(y, cot_blocks)
    cot, cot_t = place(meta, gain, cot_blocks, False)
    z, dy, sums = gate_sums(tokens, cot, mine, other, y, gate_row)
    normed_y, gate, dscan, gain_grad, keep, send = gate_back(
        4.0 * wide, around(sums), z, dy, y, gate_row, tokens_t, cot_t
    )

    early = (keep + swap_core(send).astype(F32)).astype(BF)
    early = early.reshape(2, -1, block, wide).transpose(1, 0, 2, 3)
    out_blocks = project_out(meta, normed_y, mine, other)
    dscan, early, out_blocks = after(dscan, early, out_blocks)
    early = exchange(early)
    out_blocks = to_owners(out_blocks)
    late, conv_grad, head_grad = mixer_backward(pre, dscan, kept, taps, head, skip, spread)
    *back_blocks, norm_part = project_back(
        meta, late, gate, mine, other, tokens, gain
    )
    late, back_blocks = after(late, back_blocks)
    back_blocks = to_owners(back_blocks)
    input_grad = finish_input(meta, back_blocks, hidden_in, cotangent, gain)

    keep, send = weight_grad(tokens_t, late)
    send, early, out_blocks = after(send, early, out_blocks)
    output = finish_output(meta, out_blocks, hidden_in)
    rest = jnp.pad(
        jnp.concatenate([norm_part[:1, :wide], norm_part[:1, wide:], gain_grad[:1]]),
        ((0, 0), (0, both - wide)),
    )
    vector = jnp.concatenate(
        [jnp.concatenate([conv_grad[:5], rest]), head_grad], axis=1
    )
    vector = (vector + swap_core(vector)).astype(BF)
    late_sum = (keep + swap_core(send).astype(F32)).astype(BF).reshape(-1, block, both + 128)
    vector = jnp.broadcast_to(vector[None], (late_sum.shape[0],) + vector.shape)
    late_sum = jnp.concatenate([late_sum, vector], axis=1)
    total = exchange(late_sum).astype(F32).sum(axis=0)
    early = trade(early.astype(F32).sum(axis=0))

    shared = jnp.concatenate(
        [total[: block + 5, wide:both], total[block + 5 : block + 7, :wide].reshape(-1, states)]
    )
    shared = sum(
        permute(shared, lambda xh, xl, core, a=a, b=b: (core, xl ^ b, xh ^ a)) for a, b in TURNS
    )
    own = trade(jnp.concatenate([total[:, :wide], total[:, both:]], axis=1))
    return (
        output,
        input_grad,
        shared[block + 5 :].reshape(-1),
        early[0],
        own[:block, :wide],
        shared[:block],
        own[:block, wide : wide + heads],
        own[block : block + 5, :wide],
        shared[block : block + 5],
        own[block : block + 3, wide : wide + heads],
        own[block + 7, :wide],
        early[1].T,
    )


def solution(mesh):
    fine = Mesh(mesh.devices.reshape(2, 4, 4, 2, 2), AXES)
    rows, both, lanes = P(AXES, None), P(DP, TN), P(None, TN)
    return jax.shard_map(
        on_device,
        mesh=fine,
        in_specs=(rows, rows, P(), both, both, P(DP, None), both, lanes, P(), lanes, P(TN), P(TN, DP)),
        out_specs=(
            rows, rows, P(), both, both, P(DP, None), both, lanes, P(), lanes, P(TN), P(TN, DP)
        ),
        check_vma=False,
    )
```

```python
import functools
import jax
import jax.numpy as jnp
from jax import lax
from jax.experimental import pallas as pl
from jax.experimental.pallas import tpu as pltpu
from jax.sharding import Mesh, PartitionSpec as P

EPS = 1e-05
AXES = ("xh", "y", "z", "xl", "core")
DP = ("xh", "y", "z")
TN = ("xl", "core")
GROUP = ("xh", "xl", "core")
PLANE = ("y", "z")
BF = jnp.bfloat16
F32 = jnp.float32
HI = lax.Precision.HIGHEST
SPAN = 128
SCALE = 1.15e9


def nn(left, right):
    return lax.dot_general(left, right, (((1,), (0,)), ((), ())), preferred_element_type=F32)


def nt(left, right):
    return lax.dot_general(left, right, (((1,), (1,)), ((), ())), preferred_element_type=F32)


def exact(left, right):
    return lax.dot_general(
        left, right, (((1,), (0,)), ((), ())), precision=HI, preferred_element_type=F32
    )


def exact_nt(left, right):
    return lax.dot_general(
        left, right, (((1,), (1,)), ((), ())), precision=HI, preferred_element_type=F32
    )


def halves(value):
    high = value.astype(BF)
    low = (value - high.astype(F32)).astype(BF)
    return high, low


def expand(value, spread):
    high, low = halves(value)
    return nn(jnp.concatenate([high, low], axis=1), spread)


def by_head(value, spread):
    width = spread.shape[0] // 2
    high, low = halves(value)
    return nt(high, spread[:width]) + nt(low, spread[:width])


def logistic(value):
    return 1.0 / (1.0 + jnp.exp(-value))


def sigmoid(value):
    return 0.5 * jnp.tanh(0.5 * value) + 0.5


def softplus(value):
    return jnp.maximum(value, 0.0) + jnp.log1p(jnp.exp(-jnp.abs(value)))


def conv_rows(ext_ref, taps):
    total = taps[4:5] + ext_ref[5 : 5 + SPAN] * taps[0:1]
    for k in range(1, 4):
        total = total + ext_ref[5 + k : 5 + k + SPAN] * taps[k : k + 1]
    return total


def scan_parts(conv, pre_dt, head, spread, tri):
    sig = sigmoid(conv)
    xbc = conv * sig
    raw = pre_dt + head[1:2]
    step = softplus(raw)
    decay = exact(tri, step * head[0:1])
    last = decay[SPAN - 1 : SPAN]
    grown = expand(jnp.concatenate([step, jnp.exp(decay), jnp.exp(last - decay)], axis=0), spread)
    step_x, start_x, end_x = grown[:SPAN], grown[SPAN : 2 * SPAN], grown[2 * SPAN :]
    return sig, xbc, raw, step, decay, step_x, start_x, end_x


def forward_kernel(
    pre_ref, taps_ref, head_ref, skip_ref, spread_ref, y_ref, kept_ref, conv_ref, ext_ref, state_ref
):
    inner = y_ref.shape[1]
    both = ext_ref.shape[1]

    @pl.when(pl.program_id(0) == 0)
    def _():
        ext_ref[0:8] = jnp.zeros((8, both), F32)
        state_ref[...] = jnp.zeros_like(state_ref)

    ext_ref[8 : 8 + SPAN] = pre_ref[:, :both]
    rows = lax.broadcasted_iota(jnp.int32, (SPAN, SPAN), 0)
    cols = lax.broadcasted_iota(jnp.int32, (SPAN, SPAN), 1)
    keep = rows >= cols
    tri = jnp.where(keep, 1.0, 0.0).astype(F32)
    spread = spread_ref[...]
    conv = conv_rows(ext_ref, taps_ref[...])
    conv_ref[...] = conv
    sig, xbc, raw, step, decay, step_x, start_x, end_x = scan_parts(
        conv, pre_ref[:, both:], head_ref[...], spread, tri
    )
    ext_ref[0:8] = ext_ref[SPAN : SPAN + 8]
    state_width = (both - inner) // 2
    x = xbc[:, :inner]
    b = xbc[:, inner : inner + state_width]
    c = xbc[:, inner + state_width :]
    decay_t = decay.T
    scaled = x * step_x
    low = scaled.astype(BF)
    scores = exact_nt(c, b)
    state = state_ref[...]
    state_low = state.astype(BF)
    kept_ref[...] = state_low
    carried = nn(c.astype(BF), state_low) * start_x + x * skip_ref[...]
    left = cols < 64
    for pair in range(inner // 128):
        at = slice(128 * pair, 128 * pair + 128)
        x_pair = low[:, at]
        found = []
        for h in (2 * pair, 2 * pair + 1):
            gap = decay[:, h : h + 1] - decay_t[h : h + 1]
            weight = jnp.exp(jnp.where(keep, gap, -1e30)) * scores
            found.append(nn(weight.astype(BF), x_pair))
        y_ref[:, at] = jnp.where(left, found[0], found[1]) + carried[:, at]
    state_ref[...] = state * start_x[SPAN - 1 : SPAN] + nn(
        b.T.astype(BF), (scaled * end_x).astype(BF)
    )


def backward_kernel(
    pre_ref, conv_ref, dy_ref, kept_ref, taps_ref, head_ref, skip_ref, spread_ref,
    late_ref, conv_grad_ref, head_grad_ref,
    dext_ref, dstate_ref, skip_sum_ref,
):
    inner = dy_ref.shape[1]
    both = dext_ref.shape[1]
    steps = pl.num_programs(0)
    at_step = pl.program_id(0)

    @pl.when(at_step == 0)
    def _():
        dext_ref[SPAN : SPAN + 8] = jnp.zeros((8, both), F32)
        dstate_ref[...] = jnp.zeros_like(dstate_ref)
        skip_sum_ref[...] = jnp.zeros_like(skip_sum_ref)
        conv_grad_ref[...] = jnp.zeros_like(conv_grad_ref)
        head_grad_ref[...] = jnp.zeros_like(head_grad_ref)

    rows = lax.broadcasted_iota(jnp.int32, (SPAN, SPAN), 0)
    cols = lax.broadcasted_iota(jnp.int32, (SPAN, SPAN), 1)
    tri = jnp.where(rows >= cols, 1.0, 0.0).astype(F32)
    upper = jnp.where(cols >= rows, 1.0, 0.0).astype(F32)
    keep = cols >= rows
    spread = spread_ref[...]
    taps = taps_ref[...]
    head = head_ref[...]
    conv = conv_ref[...]
    sig, xbc, raw, step, decay, step_x, start_x, end_x = scan_parts(
        conv, pre_ref[:, both:], head, spread, tri
    )
    state_width = (both - inner) // 2
    x = xbc[:, :inner]
    b = xbc[:, inner : inner + state_width]
    c = xbc[:, inner + state_width :]
    b_low, c_low = b.astype(BF), c.astype(BF)
    decay_t = decay.T
    scaled = x * step_x
    low = scaled.astype(BF)
    scores = exact_nt(b, c)
    dy = dy_ref[...].astype(F32)
    dy_low = dy.astype(BF)
    kept = kept_ref[...]
    dstate = dstate_ref[...]
    dstate_low = dstate.astype(BF)
    left = cols < 64
    wide_rows = lax.broadcasted_iota(jnp.int32, (SPAN, SPAN), 0)
    d_scores = jnp.zeros((SPAN, SPAN), F32)
    into = jnp.zeros((SPAN, SPAN), F32)
    out_of = jnp.zeros((SPAN, SPAN), F32)
    pieces = []
    none = jnp.zeros((SPAN, 128), BF)
    for pair in range(inner // 128):
        at = slice(128 * pair, 128 * pair + 128)
        x_pair = low[:, at]
        dy_pair = dy_low[:, at]
        found = []
        for side, h in enumerate((2 * pair, 2 * pair + 1)):
            gap = decay_t[h : h + 1] - decay[:, h : h + 1]
            fall = jnp.exp(jnp.where(keep, gap, -1e30))
            mine = jnp.where(left if side == 0 else ~left, dy_pair, none)
            back = nt(x_pair, mine) * fall
            d_scores = d_scores + back
            both_ways = back * scores
            into = jnp.where(wide_rows == h, jnp.sum(both_ways, axis=0, keepdims=True), into)
            out_of = jnp.where(cols == h, jnp.sum(both_ways, axis=1, keepdims=True), out_of)
            found.append(nn((fall * scores).astype(BF), dy_pair))
        pieces.append(jnp.where(left, found[0], found[1]))
    inside = jnp.concatenate(pieces, axis=1)
    dy_start = dy * start_x
    dy_start_low = dy_start.astype(BF)
    from_state = nn(c_low, kept)
    scaled_end = scaled * end_x
    d_end = nn(b_low, dstate_low)
    d_scaled = inside + d_end * end_x
    pair_start = by_head(dy_start * from_state, spread)
    pair_end = by_head(scaled_end * d_end, spread)
    d_scores_low = d_scores.astype(BF)
    d_c = nn(d_scores.T.astype(BF), b_low) + nt(dy_start_low, kept)
    d_b = nn(d_scores_low, c_low) + nt(scaled_end.astype(BF), dstate_low)
    through = jnp.sum(kept.astype(F32) * dstate, axis=0, keepdims=True)
    through = by_head(jnp.broadcast_to(through * start_x[SPAN - 1 : SPAN], (8, inner)), spread)[0:1]
    at_end = jnp.sum(pair_end, axis=0, keepdims=True) + through
    d_decay = into.T - out_of + pair_start - pair_end
    d_decay = d_decay + jnp.where(rows == SPAN - 1, at_end, 0.0)
    d_log = exact(upper, d_decay)
    d_step = by_head(d_scaled * x, spread) + d_log * head[0:1]
    d_raw = d_step * logistic(raw)
    dstate_ref[...] = dstate * start_x[SPAN - 1 : SPAN] + nn(c.T.astype(BF), dy_start_low)
    late_ref[:, both:] = d_raw.astype(BF)
    head_grad_ref[0:1] += jnp.sum(d_log * step, axis=0, keepdims=True) * head[0:1]
    head_grad_ref[1:2] += jnp.sum(d_raw, axis=0, keepdims=True)
    skip_sum_ref[0:1] += jnp.sum(dy * x, axis=0, keepdims=True)
    dx = d_scaled * step_x + dy * skip_ref[...]
    d_conv = jnp.concatenate([dx, d_b, d_c], axis=1) * (sig * (1.0 + conv * (1.0 - sig)))
    dext_ref[0:SPAN] = d_conv
    values = pre_ref[:, :both]
    d_pre = d_conv * taps[3:4]
    conv_grad_ref[3:4] += jnp.sum(d_conv * values, axis=0, keepdims=True)
    for k in range(3):
        moved = dext_ref[3 - k : 3 - k + SPAN]
        d_pre = d_pre + moved * taps[k : k + 1]
        conv_grad_ref[k : k + 1] += jnp.sum(moved * values, axis=0, keepdims=True)
    conv_grad_ref[4:5] += jnp.sum(d_conv, axis=0, keepdims=True)
    dext_ref[SPAN : SPAN + 8] = dext_ref[0:8]
    late_ref[:, :both] = d_pre.astype(BF)

    @pl.when(at_step == steps - 1)
    def _():
        head_grad_ref[2:3] += by_head(
            jnp.broadcast_to(skip_sum_ref[0:1], (8, inner)), spread
        )[0:1]


def whole(shape):
    return pl.BlockSpec(shape, lambda *_: (0,) * len(shape))


def column(rows, width, shift=0):
    return pl.BlockSpec((rows, width), lambda j, *_: (0, j + shift))


def shape_of(shape, dtype):
    return jax.ShapeDtypeStruct(shape, dtype)


def params(limit, *semantics):
    return pltpu.CompilerParams(
        dimension_semantics=semantics or None, vmem_limit_bytes=52 * 1024 * 1024
    )


def lasting(us):
    return pl.CostEstimate(flops=int(us * SCALE), bytes_accessed=1024, transcendentals=0)


def place_kernel(normalise, meta_ref, gain_ref, *refs):
    blocks, out_ref, flip_ref = refs[:4], refs[4], refs[5]
    rows, width = blocks[0].shape
    half = width // 2
    core = meta_ref[4]
    first = pl.multiple_of(core * half, 128)
    second = pl.multiple_of((1 - core) * half, 128)
    for k, block in enumerate(blocks):
        at = pl.multiple_of(meta_ref[k] * rows, rows)
        value = block[...].astype(F32)
        if normalise:
            scale = lax.rsqrt(jnp.mean(value * value, axis=1, keepdims=True) + EPS)
            value = value * scale * gain_ref[...]
        low = value.astype(BF)
        out_ref[pl.ds(at, rows), pl.ds(first, half)] = low[:, :half]
        out_ref[pl.ds(at, rows), pl.ds(second, half)] = low[:, half:]
        flip = value.T.astype(BF)
        flip_ref[pl.ds(first, half), pl.ds(at, rows)] = flip[:half]
        flip_ref[pl.ds(second, half), pl.ds(at, rows)] = flip[half:]


def place(meta, gain, blocks, normalise):
    rows, width = blocks[0].shape
    vmem = pl.BlockSpec()
    return pl.pallas_call(
        functools.partial(place_kernel, normalise),
        in_specs=[pl.BlockSpec(memory_space=pltpu.SMEM)] + [vmem] * 5,
        out_specs=[vmem, vmem],
        out_shape=[shape_of((4 * rows, width), BF), shape_of((width, 4 * rows), BF)],
        compiler_params=params(24),
        cost_estimate=lasting(6),
        name="place_normed" if normalise else "place_cotangent",
    )(meta, gain, *blocks)


def project_kernel(tokens_ref, mine_ref, other_ref, out_ref):
    half = mine_ref.shape[0]
    out_ref[...] = nn(tokens_ref[:, :half], mine_ref[...]) + nn(
        tokens_ref[:, half:], other_ref[...]
    )


def project(tokens, mine, other, inner):
    half = mine.shape[0]
    length = tokens.shape[0]
    tile = 384
    columns = mine.shape[1] - 2 * inner
    return pl.pallas_call(
        project_kernel,
        grid=(columns // tile,),
        in_specs=[whole(tokens.shape)] + [column(half, tile, 2 * inner // tile)] * 2,
        out_specs=column(length, tile),
        out_shape=shape_of((length, columns), F32),
        compiler_params=params(20, "arbitrary"),
        cost_estimate=lasting(6),
        name="project_in",
    )(tokens, mine, other)


def gate_sums_kernel(
    tokens_ref, cot_ref, zm_ref, zo_ref, om_ref, oo_ref, y_ref, gain_ref, z_ref, dy_ref, sums_ref
):
    half = zm_ref.shape[0]
    z = nn(tokens_ref[:, :half], zm_ref[...]) + nn(tokens_ref[:, half:], zo_ref[...])
    dy = nn(cot_ref[:, :half], om_ref[...]) + nn(cot_ref[:, half:], oo_ref[...])
    z_ref[...] = z
    dy_ref[...] = dy
    gated = y_ref[...] * (z * sigmoid(z))
    ones = jnp.ones((8, z.shape[1]), BF)
    found = []
    for value in (gated * gated, gated * (dy * gain_ref[...])):
        high, low = halves(value)
        found.append(nt(ones, high) + nt(ones, low))
    row = lax.broadcasted_iota(jnp.int32, found[0].shape, 0)
    total = jnp.where(row == 0, found[0], found[1])

    @pl.when(pl.program_id(0) == 0)
    def _():
        sums_ref[...] = total

    @pl.when(pl.program_id(0) > 0)
    def _():
        sums_ref[...] += total


def gate_sums(tokens, cot, mine, other, y, gain):
    length, inner = y.shape
    half = mine.shape[0]
    tile = 256
    steps = inner // tile
    return pl.pallas_call(
        gate_sums_kernel,
        grid=(steps,),
        in_specs=[
            whole(tokens.shape),
            whole(cot.shape),
            column(half, tile),
            column(half, tile),
            column(half, tile, steps),
            column(half, tile, steps),
            column(length, tile),
            column(1, tile),
        ],
        out_specs=[column(length, tile), column(length, tile), whole((8, length))],
        out_shape=[
            shape_of((length, inner), F32),
            shape_of((length, inner), F32),
            shape_of((8, length), F32),
        ],
        compiler_params=params(36, "arbitrary"),
        cost_estimate=lasting(9),
        name="gate_sums",
    )(tokens, cot, mine, other, mine, other, y, gain)


def gate_back_kernel(
    width_all, s0, s1, s2, s3, z_ref, dy_ref, y_ref, gain_ref, tokens_t_ref, cot_t_ref,
    normed_ref, gate_ref, dscan_ref, gain_grad_ref, keep_ref, send_ref,
):
    sums = (s0[...] + s1[...]) + (s2[...] + s3[...])
    flat = sums.T
    rms = lax.rsqrt(flat[:, 0:1] / width_all + EPS)
    inner = flat[:, 1:2] * (rms * rms * rms / width_all)
    z = z_ref[...]
    y = y_ref[...]
    dy = dy_ref[...]
    gain = gain_ref[...]
    sig = sigmoid(z)
    act = z * sig
    gated = y * act
    unit = gated * rms
    normed = (unit * gain).astype(BF)
    normed_ref[...] = normed
    gain_grad_ref[...] = jnp.broadcast_to(
        jnp.sum(dy * unit, axis=0, keepdims=True), gain_grad_ref.shape
    )
    d_gated = rms * (dy * gain) - gated * inner
    dscan_ref[...] = d_gated * act
    gate = (d_gated * y * (sig * (1.0 + z * (1.0 - sig)))).astype(BF)
    gate_ref[...] = gate
    half = tokens_t_ref.shape[0] // 2
    for side, (left, right) in enumerate(((tokens_t_ref, gate), (cot_t_ref, normed))):
        for out, at in ((keep_ref, slice(0, half)), (send_ref, slice(half, 2 * half))):
            found = nn(left[at], right).astype(BF)
            out[:, side] = found.reshape(out.shape[0], out.shape[2], found.shape[1])


def gate_back(block, width_all, sums, z, dy, y, gain, tokens_t, cot_t):
    length, inner = y.shape
    half = tokens_t.shape[0] // 2
    tile = 256
    pile = pl.BlockSpec((half // block, 2, block, tile), lambda j: (0, 0, 0, j))
    return pl.pallas_call(
        functools.partial(gate_back_kernel, width_all),
        grid=(inner // tile,),
        in_specs=[whole((8, length))] * 4
        + [column(length, tile)] * 3
        + [column(1, tile), whole(tokens_t.shape), whole(cot_t.shape)],
        out_specs=[column(length, tile)] * 3 + [column(8, tile), pile, pile],
        out_shape=[
            shape_of((length, inner), BF),
            shape_of((length, inner), BF),
            shape_of((length, inner), F32),
            shape_of((8, inner), F32),
            shape_of((half // block, 2, block, inner), BF),
            shape_of((half // block, 2, block, inner), BF),
        ],
        compiler_params=params(44, "arbitrary"),
        cost_estimate=lasting(12),
        name="gate_back",
    )(*sums, z, dy, y, gain, tokens_t, cot_t)


def scatter_rows(meta_ref, found, scratch, outs):
    rows = outs[0].shape[0]
    scratch[...] = found
    for k, out in enumerate(outs):
        out[...] = scratch[pl.ds(pl.multiple_of(meta_ref[k] * rows, rows), rows), :].astype(BF)


def project_out_kernel(meta_ref, normed_ref, om_ref, oo_ref, *refs):
    outs, scratch = refs[:4], refs[4]

    def step(right):
        scatter_rows(meta_ref, nt(normed_ref[...], right[...]), scratch, outs)

    first = pl.program_id(0) < pl.num_programs(0) // 2
    pl.when(first)(lambda: step(om_ref))
    pl.when(jnp.logical_not(first))(lambda: step(oo_ref))


def sides(tile, columns, shift):
    return [
        pl.BlockSpec((pl.Element(tile), pl.Element(columns)), lambda j: (jnp.minimum(j, 1) * tile, shift)),
        pl.BlockSpec((pl.Element(tile), pl.Element(columns)), lambda j: (jnp.maximum(j - 2, 0) * tile, shift)),
    ]


def project_out(meta, normed_y, mine, other):
    length, inner = normed_y.shape
    half = mine.shape[0]
    rows = length // 4
    tile = half // 2
    return pl.pallas_call(
        project_out_kernel,
        grid=(4,),
        in_specs=[pl.BlockSpec(memory_space=pltpu.SMEM), whole(normed_y.shape)]
        + sides(tile, inner, inner),
        out_specs=[column(rows, tile)] * 4,
        out_shape=[shape_of((rows, 2 * half), BF)] * 4,
        scratch_shapes=[pltpu.VMEM((length, tile), F32)],
        compiler_params=params(24, "arbitrary"),
        cost_estimate=lasting(6),
        name="project_out",
    )(meta, normed_y, mine, other)


def project_back_kernel(
    meta_ref, late_ref, gate_ref, xm_ref, xo_ref, zm_ref, zo_ref, tokens_ref, gain_ref, *refs
):
    outs, grad_ref, scratch = refs[:4], refs[4], refs[5]
    tile = scratch.shape[1]
    j = pl.program_id(0)
    side, within = j // 2, j % 2
    core = meta_ref[4]

    def step(x_ref, z_ref):
        found = nt(late_ref[...], x_ref[...]) + nt(gate_ref[...], z_ref[...])
        total = jnp.sum(found * tokens_ref[...].astype(F32), axis=0, keepdims=True)
        owner = side + core - 2 * side * core
        place = pl.ds(pl.multiple_of((2 * owner + within) * tile, 128), tile)
        grad_ref[:, place] = jnp.broadcast_to(total / gain_ref[:, place], (8, tile))
        scatter_rows(meta_ref, found, scratch, outs)

    pl.when(side == 0)(lambda: step(xm_ref, zm_ref))
    pl.when(side == 1)(lambda: step(xo_ref, zo_ref))


def project_back(meta, late, gate, mine1, other1, mine2, other2, tokens, gain):
    length, columns = late.shape
    inner = gate.shape[1]
    half = mine1.shape[0]
    rows = length // 4
    tile = half // 2
    return pl.pallas_call(
        project_back_kernel,
        grid=(4,),
        in_specs=[pl.BlockSpec(memory_space=pltpu.SMEM), whole(late.shape), whole(gate.shape)]
        + sides(tile, columns, 2 * inner)
        + sides(tile, inner, 0)
        + [column(length, tile), whole(gain.shape)],
        out_specs=[column(rows, tile)] * 4 + [whole((8, 2 * half))],
        out_shape=[shape_of((rows, 2 * half), BF)] * 4 + [shape_of((8, 2 * half), F32)],
        scratch_shapes=[pltpu.VMEM((length, tile), F32)],
        compiler_params=params(32, "arbitrary"),
        cost_estimate=lasting(0.5),
        name="project_back",
    )(meta, late, gate, mine1, other1, mine2, other2, tokens, gain)


def weight_grad_kernel(tokens_t_ref, late_ref, vector_ref, keep_ref, send_ref):
    half = keep_ref.shape[0]
    late = late_ref[...]
    keep_ref[...] = nn(tokens_t_ref[:half], late)
    send_ref[:half] = nn(tokens_t_ref[half:], late).astype(BF)
    send_ref[half:] = vector_ref[...].astype(BF)


def weight_grad(tokens_t, late, vector):
    length, columns = late.shape
    half = tokens_t.shape[0] // 2
    rows = half + vector.shape[0]
    tile = 384
    return pl.pallas_call(
        weight_grad_kernel,
        grid=(columns // tile,),
        in_specs=[whole(tokens_t.shape), column(length, tile), column(vector.shape[0], tile)],
        out_specs=[column(half, tile), column(rows, tile)],
        out_shape=[shape_of((half, columns), F32), shape_of((rows, columns), BF)],
        compiler_params=params(24, "arbitrary"),
        cost_estimate=lasting(0.5),
        name="weight_grad",
    )(tokens_t, late, vector)


def pack_kernel(z_ref, out_ref, x_ref, bc_ref, dt_ref, packed_ref):
    at = 0
    for ref in (z_ref, out_ref, x_ref, bc_ref):
        packed_ref[:, at : at + ref.shape[1]] = ref[...]
        at += ref.shape[1]
    heads, rows = dt_ref.shape
    tall = jnp.concatenate([dt_ref[...].astype(F32), jnp.zeros((128 - heads, rows), F32)], axis=0)
    packed_ref[:, at:] = tall.T.astype(BF)


def pack(*parts):
    vmem = pl.BlockSpec()
    return pl.pallas_call(
        pack_kernel,
        in_specs=[vmem] * 5,
        out_specs=vmem,
        out_shape=shape_of(
            (parts[0].shape[0], sum(part.shape[1] for part in parts[:4]) + 128), BF
        ),
        compiler_params=params(8),
        cost_estimate=lasting(1),
        name="pack_weights",
    )(*parts)


def total_kernel(states, got_ref, own_ref, shared_ref):
    total = jnp.sum(got_ref[...].astype(F32), axis=0)
    rows = total.shape[0]
    inner = own_ref.shape[1] - 128
    both = inner + states
    own_ref[:, :inner] = total[:, :inner]
    own_ref[:, inner:] = total[:, both:]
    shared_ref[:rows] = total[:, inner:both]
    per = inner // states
    for k in range(2 * per):
        line = rows - 3 + k // per
        at = states * (k % per)
        shared_ref[rows + k : rows + k + 1] = total[line : line + 1, at : at + states]


def total_of(got, states):
    count, rows, columns = got.shape
    vmem = pl.BlockSpec()
    extra = rows + 2 * ((columns - states - 128) // states)
    return pl.pallas_call(
        functools.partial(total_kernel, states),
        in_specs=[vmem],
        out_specs=[vmem, vmem],
        out_shape=[shape_of((rows, columns - states), F32), shape_of((extra, states), F32)],
        compiler_params=params(16),
        cost_estimate=lasting(3),
        name="late_total",
    )(got)


def deliver_kernel(
    own_ref, s0, s1, s2, s3,
    norm_ref, x_ref, bc_ref, dt_ref, conv_x_ref, conv_bc_ref, head_ref, gate_ref,
):
    shared = (s0[...] + s1[...]) + (s2[...] + s3[...])
    own = own_ref[...]
    block, inner = x_ref.shape
    heads = dt_ref.shape[0]
    x_ref[...] = own[:block, :inner]
    dt_ref[...] = own[:block, inner:].T[:heads]
    conv_x_ref[...] = own[block : block + 5, :inner]
    head_ref[...] = own[block : block + 3, inner : inner + heads]
    gate_ref[...] = own[block + 7, :inner]
    bc_ref[...] = shared[:block]
    conv_bc_ref[...] = shared[block : block + 5]
    states = bc_ref.shape[1]
    for k in range(norm_ref.shape[0] // states):
        norm_ref[states * k : states * k + states] = shared[block + 8 + k]


def deliver(own, shared, block, heads):
    vmem = pl.BlockSpec()
    inner = own.shape[1] - 128
    states = shared[0].shape[1]
    shapes = [
        (2 * inner,), (block, inner), (block, states), (heads, block),
        (5, inner), (5, states), (3, heads), (inner,),
    ]
    return pl.pallas_call(
        deliver_kernel,
        in_specs=[vmem] * 5,
        out_specs=[vmem] * 8,
        out_shape=[shape_of(shape, F32) for shape in shapes],
        compiler_params=params(16),
        cost_estimate=lasting(2),
        name="deliver_late",
    )(own, *shared)


def owner_total(xh_ref, blocks):
    total = sum(block[...].astype(F32) for block in blocks)
    half = total.shape[1] // 2
    turned = jnp.concatenate([total[:, half:], total[:, :half]], axis=1)
    return jnp.where(xh_ref[5] == 0, total, turned)


def output_kernel(meta_ref, b0, b1, b2, b3, hidden_ref, out_ref):
    mixed = owner_total(meta_ref, (b0, b1, b2, b3))
    out_ref[...] = (hidden_ref[...].astype(F32) + mixed).astype(BF)


def finish_output(meta, blocks, hidden):
    vmem = pl.BlockSpec()
    return pl.pallas_call(
        output_kernel,
        in_specs=[pl.BlockSpec(memory_space=pltpu.SMEM)] + [vmem] * 5,
        out_specs=vmem,
        out_shape=shape_of(hidden.shape, BF),
        compiler_params=params(16),
        cost_estimate=lasting(3),
        name="finish_output",
    )(meta, *blocks, hidden)


def input_kernel(meta_ref, b0, b1, b2, b3, hidden_ref, cot_ref, gain_ref, out_ref):
    scaled = owner_total(meta_ref, (b0, b1, b2, b3)) * gain_ref[...]
    resid = hidden_ref[...].astype(F32)
    inv = lax.rsqrt(jnp.mean(resid * resid, axis=1, keepdims=True) + EPS)
    along = jnp.mean(resid * scaled, axis=1, keepdims=True) * (inv * inv * inv)
    out_ref[...] = inv * scaled - resid * along + cot_ref[...].astype(F32)


def finish_input(meta, blocks, hidden, cot, gain):
    vmem = pl.BlockSpec()
    return pl.pallas_call(
        input_kernel,
        in_specs=[pl.BlockSpec(memory_space=pltpu.SMEM)] + [vmem] * 7,
        out_specs=vmem,
        out_shape=shape_of(hidden.shape, F32),
        compiler_params=params(16),
        cost_estimate=lasting(3),
        name="finish_input",
    )(meta, *blocks, hidden, cot, gain)


def mixer_tables(conv_x, conv_bc, head_params):
    heads = head_params.shape[1]
    inner = conv_x.shape[1]
    taps = jnp.pad(jnp.concatenate([conv_x, conv_bc], axis=1), ((0, 3), (0, 0)))
    head = jnp.stack([-jnp.exp(head_params[0]), head_params[1]])
    head = jnp.pad(head, ((0, 6), (0, 128 - heads)))
    skip = jnp.repeat(head_params[2], inner // heads)[None]
    owner = lax.broadcasted_iota(jnp.int32, (256, inner), 1) // (inner // heads)
    one = owner == lax.broadcasted_iota(jnp.int32, (256, inner), 0) % 128
    return taps, head, skip, one.astype(BF)


def mixer_forward(pre, taps, head, skip, spread):
    length, columns = pre.shape
    both = taps.shape[1]
    inner = skip.shape[1]
    steps = length // SPAN
    return pl.pallas_call(
        forward_kernel,
        grid=(steps,),
        in_specs=[
            pl.BlockSpec((SPAN, columns), lambda i: (i, 0)),
            whole(taps.shape), whole(head.shape), whole(skip.shape), whole(spread.shape),
        ],
        out_specs=[
            pl.BlockSpec((SPAN, inner), lambda i: (i, 0)),
            pl.BlockSpec((128, inner), lambda i: (i, 0)),
            pl.BlockSpec((SPAN, both), lambda i: (i, 0)),
        ],
        out_shape=[
            shape_of((length, inner), F32),
            shape_of((steps * 128, inner), BF),
            shape_of((length, both), F32),
        ],
        scratch_shapes=[pltpu.VMEM((SPAN + 8, both), F32), pltpu.VMEM((128, inner), F32)],
        compiler_params=params(20, "arbitrary"),
        cost_estimate=lasting(13),
        name="mixer_forward",
    )(pre, taps, head, skip, spread)


def mixer_backward(pre, conv, dy, kept, taps, head, skip, spread):
    length, columns = pre.shape
    both = taps.shape[1]
    inner = skip.shape[1]
    steps = length // SPAN
    last = steps - 1
    return pl.pallas_call(
        backward_kernel,
        grid=(steps,),
        in_specs=[
            pl.BlockSpec((SPAN, columns), lambda i: (last - i, 0)),
            pl.BlockSpec((SPAN, both), lambda i: (last - i, 0)),
            pl.BlockSpec((SPAN, inner), lambda i: (last - i, 0)),
            pl.BlockSpec((128, inner), lambda i: (last - i, 0)),
            whole(taps.shape), whole(head.shape), whole(skip.shape), whole(spread.shape),
        ],
        out_specs=[
            pl.BlockSpec((SPAN, columns), lambda i: (last - i, 0)),
            whole((8, both)),
            whole((8, 128)),
        ],
        out_shape=[
            shape_of((length, columns), BF),
            shape_of((8, both), F32),
            shape_of((8, 128), F32),
        ],
        scratch_shapes=[
            pltpu.VMEM((SPAN + 8, both), F32),
            pltpu.VMEM((128, inner), F32),
            pltpu.VMEM((8, inner), F32),
        ],
        compiler_params=params(24, "arbitrary"),
        cost_estimate=lasting(30),
        name="mixer_backward",
    )(pre, conv, dy, kept, taps, head, skip, spread)


CELLS = [(xh, xl, core) for xh in range(2) for xl in range(2) for core in range(2)]
TURNS = [(a, b) for a in range(2) for b in range(2)]


def moves(rule):
    return [(4 * c[0] + 2 * c[1] + c[2], 4 * d[0] + 2 * d[1] + d[2]) for c in CELLS for d in [rule(*c)]]


def permute(value, rule):
    return lax.ppermute(value, GROUP, moves(rule))


def trade(value):
    return permute(
        value, lambda xh, xl, core: (xh, xl, core) if xh == core else (1 - xh, xl, 1 - core)
    )


def swap_core(value):
    return lax.ppermute(value, "core", [(0, 1), (1, 0)])


def to_workers(value):
    return [
        permute(value, lambda xh, xl, core, a=a, b=b: (core ^ a, xl ^ b, xh)) for a, b in TURNS
    ]


def to_owners(blocks):
    return [
        permute(block, lambda xh, xl, core, a=a, b=b: (core, xl ^ b, xh ^ a))
        for block, (a, b) in zip(blocks, TURNS)
    ]


def around(value):
    return [value] + [
        permute(value, lambda xh, xl, core, a=a, b=b: (xh ^ a, xl ^ b, core)) for a, b in TURNS[1:]
    ]


def gather_plane(shard):
    count = lax.axis_size(PLANE)
    spread = jnp.broadcast_to(shard[None], (count,) + shard.shape)
    got = lax.all_to_all(spread, PLANE, 0, 0, tiled=True)
    return got.reshape((count * shard.shape[0],) + shard.shape[1:])


def exchange(blocks):
    return lax.all_to_all(blocks, PLANE, 0, 0, tiled=True)


def after(*values):
    return lax.optimization_barrier(values)


def on_device(
    hidden_in,
    cotangent,
    norm_gain,
    w_z,
    w_x,
    w_bc,
    w_dt,
    conv_x,
    conv_bc,
    head_params,
    gate_gain,
    w_out,
):
    block, wide = w_x.shape
    states = w_bc.shape[1]
    heads = w_dt.shape[1]
    both = wide + states
    xh, xl, core = (lax.axis_index(axis) for axis in GROUP)
    meta = jnp.stack([(xl ^ b) * 2 + (xh ^ a) for a, b in TURNS] + [core, xh]).astype(jnp.int32)
    gain = norm_gain[None]

    weights = trade(pack(w_z, w_out.T, w_x, w_bc, w_dt.T))
    small = jnp.concatenate(
        [conv_x, gate_gain[None], jnp.pad(head_params, ((0, 0), (0, wide - heads)))[:2]]
    )
    small = jnp.concatenate([small, jnp.pad(head_params[2:], ((0, 7), (0, wide - heads)))])
    small, weights = after(small, weights)
    small = jnp.where(core == xh, small, swap_core(small))

    mine = gather_plane(weights)
    hidden, weights = after(hidden_in, weights)
    hidden_blocks = to_workers(hidden)
    first_half, cot, small = after(hidden_blocks[:2], cotangent, small)
    hidden_blocks = first_half + hidden_blocks[2:]
    cot_blocks = to_workers(cot)
    tokens, tokens_t = place(meta, gain, hidden_blocks, True)
    tokens, mine, cot_first = after(tokens, mine, cot_blocks[0])
    cot_blocks = [cot_first] + cot_blocks[1:]
    other = swap_core(mine)

    conv_x, gate_row, head_params = small[:5], small[5:6], small[6:9, :heads]
    taps, head, skip, spread = mixer_tables(conv_x, conv_bc, head_params)
    pre = project(tokens, mine, other, wide)
    y, kept, conv = mixer_forward(pre, taps, head, skip, spread)
    y, cot_blocks = after(y, cot_blocks)
    cot, cot_t = place(meta, gain, cot_blocks, False)
    z, dy, sums = gate_sums(tokens, cot, mine, other, y, gate_row)
    normed_y, gate, dscan, gain_grad, keep, send = gate_back(
        block, 4.0 * wide, around(sums), z, dy, y, gate_row, tokens_t, cot_t
    )

    early = (keep.astype(F32) + swap_core(send).astype(F32)).astype(BF)
    out_blocks = project_out(meta, normed_y, mine, other)
    dscan, early, out_blocks = after(dscan, early, out_blocks)
    early = exchange(early)
    out_blocks = to_owners(out_blocks)
    late, conv_grad, head_grad = mixer_backward(pre, conv, dscan, kept, taps, head, skip, spread)
    *back_blocks, norm_part = project_back(
        meta, late, gate, mine, other, mine, other, tokens, gain
    )
    late, back_blocks, out_blocks = after(late, back_blocks, out_blocks)
    back_blocks = to_owners(back_blocks)

    rest = jnp.pad(
        jnp.concatenate([norm_part[:1, :wide], norm_part[:1, wide:], gain_grad[:1]]),
        ((0, 0), (0, states)),
    )
    vector = jnp.concatenate([jnp.concatenate([conv_grad[:5], rest]), head_grad], axis=1)
    vector = jnp.pad(vector, ((0, 8), (0, 0)))
    keep, send = weight_grad(tokens_t, late, vector)
    send, early, back_first = after(send, early, back_blocks[0])
    output = finish_output(meta, out_blocks, hidden_in)
    got = swap_core(send).astype(F32)
    half = keep.shape[0]
    late_sum = (keep + got[:half]).astype(BF).reshape(-1, block, both + 128)
    vector = (vector[:8] + got[half : half + 8]).astype(BF)
    vector = jnp.broadcast_to(vector[None], (late_sum.shape[0],) + vector.shape)
    late_sum = jnp.concatenate([late_sum, vector], axis=1)
    back_blocks = [back_first] + back_blocks[1:]
    input_grad = finish_input(meta, back_blocks, hidden_in, cotangent, gain)
    early = trade(early.astype(F32).sum(axis=0))
    got, input_grad, early, output = after(exchange(late_sum), input_grad, early, output)
    own, shared = total_of(got, states)

    shared = [
        permute(shared, lambda xh, xl, core, a=a, b=b: (core, xl ^ b, xh ^ a)) for a, b in TURNS
    ]
    norm_grad, x_grad, bc_grad, dt_grad, conv_x_grad, conv_bc_grad, head_part, gate_part = deliver(
        trade(own), shared, block, heads
    )
    return (
        output,
        input_grad,
        norm_grad,
        early[0],
        x_grad,
        bc_grad,
        dt_grad.T,
        conv_x_grad,
        conv_bc_grad,
        head_part,
        gate_part,
        early[1].T,
    )


def solution(mesh):
    fine = Mesh(mesh.devices.reshape(2, 4, 4, 2, 2), AXES)
    rows, both, lanes = P(AXES, None), P(DP, TN), P(None, TN)
    return jax.shard_map(
        on_device,
        mesh=fine,
        in_specs=(rows, rows, P(), both, both, P(DP, None), both, lanes, P(), lanes, P(TN), P(TN, DP)),
        out_specs=(
            rows, rows, P(), both, both, P(DP, None), both, lanes, P(), lanes, P(TN), P(TN, DP)
        ),
        check_vma=False,
    )
```

```python
import functools
import jax
import jax.numpy as jnp
from jax import lax
from jax.experimental import pallas as pl
from jax.experimental.pallas import tpu as pltpu
from jax.sharding import Mesh, PartitionSpec as P

EPS = 1e-05
AXES = ("xh", "y", "z", "xl", "core")
DP = ("xh", "y", "z")
TN = ("xl", "core")
GROUP = ("xh", "xl", "core")
PLANE = ("y", "z")
BF = jnp.bfloat16
F32 = jnp.float32
HI = lax.Precision.HIGHEST
SPAN = 128
LIMIT = 36


def near(value):
    return pltpu.with_memory_space_constraint(value, pltpu.VMEM)


def far(value):
    return pltpu.with_memory_space_constraint(value, pltpu.HBM)


ROWS = 512
SCALE = 1.15e9


def nn(left, right):
    return lax.dot_general(left, right, (((1,), (0,)), ((), ())), preferred_element_type=F32)


def nt(left, right):
    return lax.dot_general(left, right, (((1,), (1,)), ((), ())), preferred_element_type=F32)


def exact(left, right):
    return lax.dot_general(
        left, right, (((1,), (0,)), ((), ())), precision=HI, preferred_element_type=F32
    )


def exact_nt(left, right):
    return lax.dot_general(
        left, right, (((1,), (1,)), ((), ())), precision=HI, preferred_element_type=F32
    )


def halves(value):
    high = value.astype(BF)
    low = (value - high.astype(F32)).astype(BF)
    return high, low


def expand(value, spread):
    high, low = halves(value)
    return nn(jnp.concatenate([high, low], axis=1), spread)


def by_head(value, spread):
    width = spread.shape[0] // 2
    high, low = halves(value)
    return nt(high, spread[:width]) + nt(low, spread[:width])


def logistic(value):
    return 1.0 / (1.0 + jnp.exp(-value))


def sigmoid(value):
    return 0.5 * jnp.tanh(0.5 * value) + 0.5


def softplus(value):
    return jnp.maximum(value, 0.0) + jnp.log1p(jnp.exp(-jnp.abs(value)))


def conv_rows(ext_ref, taps):
    total = taps[4:5] + ext_ref[5 : 5 + SPAN] * taps[0:1]
    for k in range(1, 4):
        total = total + ext_ref[5 + k : 5 + k + SPAN] * taps[k : k + 1]
    return total


def scan_parts(conv, pre_dt, head, spread, tri):
    sig = sigmoid(conv)
    xbc = conv * sig
    raw = pre_dt + head[1:2]
    step = softplus(raw)
    decay = exact(tri, step * head[0:1])
    last = decay[SPAN - 1 : SPAN]
    grown = expand(jnp.concatenate([step, jnp.exp(decay), jnp.exp(last - decay)], axis=0), spread)
    step_x, start_x, end_x = grown[:SPAN], grown[SPAN : 2 * SPAN], grown[2 * SPAN :]
    return sig, xbc, raw, step, decay, step_x, start_x, end_x


def forward_kernel(
    pre_ref, taps_ref, head_ref, skip_ref, spread_ref, y_ref, kept_ref, conv_ref, ext_ref, state_ref
):
    inner = y_ref.shape[1]
    both = ext_ref.shape[1]

    @pl.when(pl.program_id(0) == 0)
    def _():
        ext_ref[0:8] = jnp.zeros((8, both), F32)
        state_ref[...] = jnp.zeros_like(state_ref)

    ext_ref[8 : 8 + SPAN] = pre_ref[:, :both]
    rows = lax.broadcasted_iota(jnp.int32, (SPAN, SPAN), 0)
    cols = lax.broadcasted_iota(jnp.int32, (SPAN, SPAN), 1)
    keep = rows >= cols
    tri = jnp.where(keep, 1.0, 0.0).astype(F32)
    spread = spread_ref[...]
    conv = conv_rows(ext_ref, taps_ref[...])
    conv_ref[...] = conv
    sig, xbc, raw, step, decay, step_x, start_x, end_x = scan_parts(
        conv, pre_ref[:, both:], head_ref[...], spread, tri
    )
    ext_ref[0:8] = ext_ref[SPAN : SPAN + 8]
    state_width = (both - inner) // 2
    x = xbc[:, :inner]
    b = xbc[:, inner : inner + state_width]
    c = xbc[:, inner + state_width :]
    decay_t = decay.T
    scaled = x * step_x
    low = scaled.astype(BF)
    scores = exact_nt(c, b)
    state = state_ref[...]
    state_low = state.astype(BF)
    kept_ref[...] = state_low
    carried = nn(c.astype(BF), state_low) * start_x + x * skip_ref[...]
    left = cols < 64
    for pair in range(inner // 128):
        at = slice(128 * pair, 128 * pair + 128)
        x_pair = low[:, at]
        found = []
        for h in (2 * pair, 2 * pair + 1):
            gap = decay[:, h : h + 1] - decay_t[h : h + 1]
            weight = jnp.exp(jnp.where(keep, gap, -1e30)) * scores
            found.append(nn(weight.astype(BF), x_pair))
        y_ref[:, at] = jnp.where(left, found[0], found[1]) + carried[:, at]
    state_ref[...] = state * start_x[SPAN - 1 : SPAN] + nn(
        b.T.astype(BF), (scaled * end_x).astype(BF)
    )


def backward_kernel(
    pre_ref, conv_ref, dy_ref, kept_ref, taps_ref, head_ref, skip_ref, spread_ref,
    late_ref, conv_grad_ref, head_grad_ref,
    dext_ref, dstate_ref, skip_sum_ref,
):
    inner = dy_ref.shape[1]
    both = dext_ref.shape[1]
    steps = pl.num_programs(0)
    at_step = pl.program_id(0)

    @pl.when(at_step == 0)
    def _():
        dext_ref[SPAN : SPAN + 8] = jnp.zeros((8, both), F32)
        dstate_ref[...] = jnp.zeros_like(dstate_ref)
        skip_sum_ref[...] = jnp.zeros_like(skip_sum_ref)
        conv_grad_ref[...] = jnp.zeros_like(conv_grad_ref)
        head_grad_ref[...] = jnp.zeros_like(head_grad_ref)

    rows = lax.broadcasted_iota(jnp.int32, (SPAN, SPAN), 0)
    cols = lax.broadcasted_iota(jnp.int32, (SPAN, SPAN), 1)
    tri = jnp.where(rows >= cols, 1.0, 0.0).astype(F32)
    upper = jnp.where(cols >= rows, 1.0, 0.0).astype(F32)
    keep = cols >= rows
    spread = spread_ref[...]
    taps = taps_ref[...]
    head = head_ref[...]
    conv = conv_ref[...]
    sig, xbc, raw, step, decay, step_x, start_x, end_x = scan_parts(
        conv, pre_ref[:, both:], head, spread, tri
    )
    state_width = (both - inner) // 2
    x = xbc[:, :inner]
    b = xbc[:, inner : inner + state_width]
    c = xbc[:, inner + state_width :]
    b_low, c_low = b.astype(BF), c.astype(BF)
    decay_t = decay.T
    scaled = x * step_x
    low = scaled.astype(BF)
    scores = exact_nt(b, c)
    dy = dy_ref[...].astype(F32)
    dy_low = dy.astype(BF)
    kept = kept_ref[...]
    dstate = dstate_ref[...]
    dstate_low = dstate.astype(BF)
    left = cols < 64
    wide_rows = lax.broadcasted_iota(jnp.int32, (SPAN, SPAN), 0)
    d_scores = jnp.zeros((SPAN, SPAN), F32)
    into = jnp.zeros((SPAN, SPAN), F32)
    out_of = jnp.zeros((SPAN, SPAN), F32)
    pieces = []
    none = jnp.zeros((SPAN, 128), BF)
    for pair in range(inner // 128):
        at = slice(128 * pair, 128 * pair + 128)
        x_pair = low[:, at]
        dy_pair = dy_low[:, at]
        found = []
        for side, h in enumerate((2 * pair, 2 * pair + 1)):
            gap = decay_t[h : h + 1] - decay[:, h : h + 1]
            fall = jnp.exp(jnp.where(keep, gap, -1e30))
            mine = jnp.where(left if side == 0 else ~left, dy_pair, none)
            back = nt(x_pair, mine) * fall
            d_scores = d_scores + back
            both_ways = back * scores
            into = jnp.where(wide_rows == h, jnp.sum(both_ways, axis=0, keepdims=True), into)
            out_of = jnp.where(cols == h, jnp.sum(both_ways, axis=1, keepdims=True), out_of)
            found.append(nn((fall * scores).astype(BF), dy_pair))
        pieces.append(jnp.where(left, found[0], found[1]))
    inside = jnp.concatenate(pieces, axis=1)
    dy_start = dy * start_x
    dy_start_low = dy_start.astype(BF)
    from_state = nn(c_low, kept)
    scaled_end = scaled * end_x
    d_end = nn(b_low, dstate_low)
    d_scaled = inside + d_end * end_x
    pair_start = by_head(dy_start * from_state, spread)
    pair_end = by_head(scaled_end * d_end, spread)
    d_scores_low = d_scores.astype(BF)
    d_c = nn(d_scores.T.astype(BF), b_low) + nt(dy_start_low, kept)
    d_b = nn(d_scores_low, c_low) + nt(scaled_end.astype(BF), dstate_low)
    through = jnp.sum(kept.astype(F32) * dstate, axis=0, keepdims=True)
    through = by_head(jnp.broadcast_to(through * start_x[SPAN - 1 : SPAN], (8, inner)), spread)[0:1]
    at_end = jnp.sum(pair_end, axis=0, keepdims=True) + through
    d_decay = into.T - out_of + pair_start - pair_end
    d_decay = d_decay + jnp.where(rows == SPAN - 1, at_end, 0.0)
    d_log = exact(upper, d_decay)
    d_step = by_head(d_scaled * x, spread) + d_log * head[0:1]
    d_raw = d_step * logistic(raw)
    dstate_ref[...] = dstate * start_x[SPAN - 1 : SPAN] + nn(c.T.astype(BF), dy_start_low)
    late_ref[:, both:] = d_raw.astype(BF)
    head_grad_ref[0:1] += jnp.sum(d_log * step, axis=0, keepdims=True) * head[0:1]
    head_grad_ref[1:2] += jnp.sum(d_raw, axis=0, keepdims=True)
    skip_sum_ref[0:1] += jnp.sum(dy * x, axis=0, keepdims=True)
    dx = d_scaled * step_x + dy * skip_ref[...]
    d_conv = jnp.concatenate([dx, d_b, d_c], axis=1) * (sig * (1.0 + conv * (1.0 - sig)))
    dext_ref[0:SPAN] = d_conv
    values = pre_ref[:, :both]
    d_pre = d_conv * taps[3:4]
    conv_grad_ref[3:4] += jnp.sum(d_conv * values, axis=0, keepdims=True)
    for k in range(3):
        moved = dext_ref[3 - k : 3 - k + SPAN]
        d_pre = d_pre + moved * taps[k : k + 1]
        conv_grad_ref[k : k + 1] += jnp.sum(moved * values, axis=0, keepdims=True)
    conv_grad_ref[4:5] += jnp.sum(d_conv, axis=0, keepdims=True)
    dext_ref[SPAN : SPAN + 8] = dext_ref[0:8]
    late_ref[:, :both] = d_pre.astype(BF)

    @pl.when(at_step == steps - 1)
    def _():
        head_grad_ref[2:3] += by_head(
            jnp.broadcast_to(skip_sum_ref[0:1], (8, inner)), spread
        )[0:1]


def whole(shape):
    return pl.BlockSpec(shape, lambda *_: (0,) * len(shape))


def column(rows, width, shift=0):
    return pl.BlockSpec((rows, width), lambda j, *_: (0, j + shift))


def shape_of(shape, dtype):
    return jax.ShapeDtypeStruct(shape, dtype)


def stored(shape, dtype):
    return pltpu.HBM(shape, dtype)


def held_near(shape, dtype):
    return pltpu.VMEM(shape, dtype)


def params(limit, *semantics):
    return pltpu.CompilerParams(
        dimension_semantics=semantics or None, vmem_limit_bytes=LIMIT * 1024 * 1024
    )


def lasting(us):
    return pl.CostEstimate(flops=int(us * SCALE), bytes_accessed=1024, transcendentals=0)


def place_kernel(normalise, meta_ref, gain_ref, *refs):
    blocks, out_ref, flip_ref = refs[:4], refs[4], refs[5]
    rows, width = blocks[0].shape
    half = width // 2
    core = meta_ref[4]
    first = pl.multiple_of(core * half, 128)
    second = pl.multiple_of((1 - core) * half, 128)
    for k, block in enumerate(blocks):
        at = pl.multiple_of(meta_ref[k] * rows, rows)
        value = block[...].astype(F32)
        if normalise:
            scale = lax.rsqrt(jnp.mean(value * value, axis=1, keepdims=True) + EPS)
            value = value * scale * gain_ref[...]
        low = value.astype(BF)
        out_ref[pl.ds(at, rows), pl.ds(first, half)] = low[:, :half]
        out_ref[pl.ds(at, rows), pl.ds(second, half)] = low[:, half:]
        flip = value.T.astype(BF)
        flip_ref[pl.ds(first, half), pl.ds(at, rows)] = flip[:half]
        flip_ref[pl.ds(second, half), pl.ds(at, rows)] = flip[half:]


def place(meta, gain, blocks, normalise):
    rows, width = blocks[0].shape
    vmem = pl.BlockSpec()
    return pl.pallas_call(
        functools.partial(place_kernel, normalise),
        in_specs=[pl.BlockSpec(memory_space=pltpu.SMEM)] + [vmem] * 5,
        out_specs=[vmem, vmem],
        out_shape=[
            (stored if normalise else shape_of)((4 * rows, width), BF),
            shape_of((width, 4 * rows), BF),
        ],
        compiler_params=params(24),
        cost_estimate=lasting(6),
        name="place_normed" if normalise else "place_cotangent",
    )(meta, gain, *[far(block) for block in blocks])


def project_kernel(tokens_ref, mine_ref, other_ref, out_ref):
    half = mine_ref.shape[0]
    out_ref[...] = nn(tokens_ref[:, :half], mine_ref[...]) + nn(
        tokens_ref[:, half:], other_ref[...]
    )


def project(tokens, mine, other, inner):
    half = mine.shape[0]
    length = tokens.shape[0]
    columns = mine.shape[1] - 2 * inner
    rows = ROWS
    part = pl.BlockSpec((pl.Element(half), pl.Element(columns)), lambda i: (0, 2 * inner))
    return pl.pallas_call(
        project_kernel,
        grid=(length // rows,),
        in_specs=[pl.BlockSpec((rows, 2 * half), lambda i: (i, 0)), part, part],
        out_specs=pl.BlockSpec((rows, columns), lambda i: (i, 0)),
        out_shape=shape_of((length, columns), F32),
        compiler_params=params(20, "arbitrary"),
        cost_estimate=lasting(6),
        name="project_in",
    )(far(tokens), far(mine), far(other))


def gate_sums_kernel(
    tokens_ref, cot_ref, zm_ref, zo_ref, om_ref, oo_ref, y_ref, gain_ref, z_ref, dy_ref, sums_ref
):
    half = zm_ref.shape[0]
    z = nn(tokens_ref[:, :half], zm_ref[...]) + nn(tokens_ref[:, half:], zo_ref[...])
    dy = nn(cot_ref[:, :half], om_ref[...]) + nn(cot_ref[:, half:], oo_ref[...])
    z_ref[...] = z
    dy_ref[...] = dy
    gated = y_ref[...] * (z * sigmoid(z))
    ones = jnp.ones((8, z.shape[1]), BF)
    found = []
    for value in (gated * gated, gated * (dy * gain_ref[...])):
        high, low = halves(value)
        found.append(nt(ones, high) + nt(ones, low))
    row = lax.broadcasted_iota(jnp.int32, found[0].shape, 0)
    total = jnp.where(row == 0, found[0], found[1])

    @pl.when(pl.program_id(0) == 0)
    def _():
        sums_ref[...] = total

    @pl.when(pl.program_id(0) > 0)
    def _():
        sums_ref[...] += total


def gate_sums(tokens, cot, mine, other, y, gain):
    length, inner = y.shape
    half = mine.shape[0]
    tile = 256
    steps = inner // tile
    return pl.pallas_call(
        gate_sums_kernel,
        grid=(steps,),
        in_specs=[
            whole(tokens.shape),
            whole(cot.shape),
            column(half, tile),
            column(half, tile),
            column(half, tile, steps),
            column(half, tile, steps),
            column(length, tile),
            column(1, tile),
        ],
        out_specs=[column(length, tile), column(length, tile), whole((8, length))],
        out_shape=[
            shape_of((length, inner), F32),
            shape_of((length, inner), F32),
            shape_of((8, length), F32),
        ],
        compiler_params=params(36, "arbitrary"),
        cost_estimate=lasting(9),
        name="gate_sums",
    )(near(tokens), near(cot), far(mine), far(other), far(mine), far(other), near(y), gain)


def gate_back_kernel(
    width_all, s0, s1, s2, s3, z_ref, dy_ref, y_ref, gain_ref, tokens_t_ref, cot_t_ref,
    normed_ref, gate_ref, dscan_ref, gain_grad_ref, keep_ref, send_ref,
):
    sums = (s0[...] + s1[...]) + (s2[...] + s3[...])
    flat = sums.T
    rms = lax.rsqrt(flat[:, 0:1] / width_all + EPS)
    inner = flat[:, 1:2] * (rms * rms * rms / width_all)
    z = z_ref[...]
    y = y_ref[...]
    dy = dy_ref[...]
    gain = gain_ref[...]
    sig = sigmoid(z)
    act = z * sig
    gated = y * act
    unit = gated * rms
    normed = (unit * gain).astype(BF)
    normed_ref[...] = normed
    gain_grad_ref[...] = jnp.broadcast_to(
        jnp.sum(dy * unit, axis=0, keepdims=True), gain_grad_ref.shape
    )
    d_gated = rms * (dy * gain) - gated * inner
    dscan_ref[...] = d_gated * act
    gate = (d_gated * y * (sig * (1.0 + z * (1.0 - sig)))).astype(BF)
    gate_ref[...] = gate
    half = tokens_t_ref.shape[0] // 2
    for side, (left, right) in enumerate(((tokens_t_ref, gate), (cot_t_ref, normed))):
        for out, at in ((keep_ref, slice(0, half)), (send_ref, slice(half, 2 * half))):
            found = nn(left[at], right).astype(BF)
            out[:, side] = found.reshape(out.shape[0], out.shape[2], found.shape[1])


def gate_back(block, width_all, sums, z, dy, y, gain, tokens_t, cot_t):
    length, inner = y.shape
    half = tokens_t.shape[0] // 2
    tile = 256
    pile = pl.BlockSpec((half // block, 2, block, tile), lambda j: (0, 0, 0, j))
    return pl.pallas_call(
        functools.partial(gate_back_kernel, width_all),
        grid=(inner // tile,),
        in_specs=[whole((8, length))] * 4
        + [column(length, tile)] * 3
        + [column(1, tile), whole(tokens_t.shape), whole(cot_t.shape)],
        out_specs=[column(length, tile)] * 3 + [column(8, tile), pile, pile],
        out_shape=[
            stored((length, inner), BF),
            stored((length, inner), BF),
            stored((length, inner), F32),
            shape_of((8, inner), F32),
            shape_of((half // block, 2, block, inner), BF),
            shape_of((half // block, 2, block, inner), BF),
        ],
        compiler_params=params(44, "arbitrary"),
        cost_estimate=lasting(12),
        name="gate_back",
    )(*sums, near(z), near(dy), near(y), gain, near(tokens_t), near(cot_t))


def scatter_rows(meta_ref, found, scratch, outs):
    rows = outs[0].shape[0]
    scratch[...] = found
    for k, out in enumerate(outs):
        out[...] = scratch[pl.ds(pl.multiple_of(meta_ref[k] * rows, rows), rows), :].astype(BF)


def project_out_kernel(meta_ref, normed_ref, om_ref, oo_ref, *refs):
    outs, scratch = refs[:4], refs[4]

    def step(right):
        scatter_rows(meta_ref, nt(normed_ref[...], right[...]), scratch, outs)

    first = pl.program_id(0) < pl.num_programs(0) // 2
    pl.when(first)(lambda: step(om_ref))
    pl.when(jnp.logical_not(first))(lambda: step(oo_ref))


def sides(tile, columns, shift, per):
    return [
        pl.BlockSpec(
            (pl.Element(tile), pl.Element(columns)),
            lambda j: (jnp.minimum(j, per - 1) * tile, shift),
        ),
        pl.BlockSpec(
            (pl.Element(tile), pl.Element(columns)),
            lambda j: (jnp.maximum(j - per, 0) * tile, shift),
        ),
    ]


def project_out(meta, normed_y, mine, other):
    length, inner = normed_y.shape
    half = mine.shape[0]
    rows = length // 4
    per = 3
    tile = half // per
    return pl.pallas_call(
        project_out_kernel,
        grid=(2 * per,),
        in_specs=[pl.BlockSpec(memory_space=pltpu.SMEM), whole(normed_y.shape)]
        + sides(tile, inner, inner, per),
        out_specs=[column(rows, tile)] * 4,
        out_shape=[stored((rows, 2 * half), BF)] * 4,
        scratch_shapes=[pltpu.VMEM((length, tile), F32)],
        compiler_params=params(24, "arbitrary"),
        cost_estimate=lasting(6),
        name="project_out",
    )(meta, far(normed_y), far(mine), far(other))


def project_back_kernel(
    meta_ref, late_ref, gate_ref, xm_ref, xo_ref, zm_ref, zo_ref, tokens_ref, gain_ref, *refs
):
    outs, grad_ref, scratch = refs[:4], refs[4], refs[5]
    tile = scratch.shape[1]
    j = pl.program_id(0)
    per = pl.num_programs(0) // 2
    side, within = j // per, j % per
    core = meta_ref[4]

    def step(x_ref, z_ref):
        found = nt(late_ref[...], x_ref[...]) + nt(gate_ref[...], z_ref[...])
        total = jnp.sum(found * tokens_ref[...].astype(F32), axis=0, keepdims=True)
        owner = side + core - 2 * side * core
        place = pl.ds(pl.multiple_of((per * owner + within) * tile, 128), tile)
        grad_ref[:, place] = jnp.broadcast_to(total / gain_ref[:, place], (8, tile))
        scatter_rows(meta_ref, found, scratch, outs)

    pl.when(side == 0)(lambda: step(xm_ref, zm_ref))
    pl.when(side == 1)(lambda: step(xo_ref, zo_ref))


def project_back(meta, late, gate, mine1, other1, mine2, other2, tokens, gain):
    length, columns = late.shape
    inner = gate.shape[1]
    half = mine1.shape[0]
    rows = length // 4
    per = 3
    tile = half // per
    return pl.pallas_call(
        project_back_kernel,
        grid=(2 * per,),
        in_specs=[pl.BlockSpec(memory_space=pltpu.SMEM), whole(late.shape), whole(gate.shape)]
        + sides(tile, columns, 2 * inner, per)
        + sides(tile, inner, 0, per)
        + [column(length, tile), whole(gain.shape)],
        out_specs=[column(rows, tile)] * 4 + [whole((8, 2 * half))],
        out_shape=[stored((rows, 2 * half), BF)] * 4 + [shape_of((8, 2 * half), F32)],
        scratch_shapes=[pltpu.VMEM((length, tile), F32)],
        compiler_params=params(32, "arbitrary"),
        cost_estimate=lasting(0.5),
        name="project_back",
    )(
        meta, near(late), far(gate), far(mine1), far(other1), far(mine2), far(other2), far(tokens), gain
    )


def weight_grad_kernel(tokens_t_ref, late_ref, vector_ref, keep_ref, send_ref):
    half = keep_ref.shape[0]
    late = late_ref[...]
    keep_ref[...] = nn(tokens_t_ref[:half], late)
    send_ref[:half] = nn(tokens_t_ref[half:], late).astype(BF)
    send_ref[half:] = vector_ref[...].astype(BF)


def weight_grad(tokens_t, late, vector):
    length, columns = late.shape
    half = tokens_t.shape[0] // 2
    rows = half + vector.shape[0]
    tile = 384
    return pl.pallas_call(
        weight_grad_kernel,
        grid=(columns // tile,),
        in_specs=[whole(tokens_t.shape), column(length, tile), column(vector.shape[0], tile)],
        out_specs=[column(half, tile), column(rows, tile)],
        out_shape=[stored((half, columns), F32), stored((rows, columns), BF)],
        compiler_params=params(24, "arbitrary"),
        cost_estimate=lasting(0.5),
        name="weight_grad",
    )(far(tokens_t), near(late), vector)


def pack_kernel(z_ref, out_ref, x_ref, bc_ref, dt_ref, packed_ref):
    at = 0
    for ref in (z_ref, out_ref, x_ref, bc_ref):
        packed_ref[:, at : at + ref.shape[1]] = ref[...]
        at += ref.shape[1]
    heads, rows = dt_ref.shape
    tall = jnp.concatenate([dt_ref[...].astype(F32), jnp.zeros((128 - heads, rows), F32)], axis=0)
    packed_ref[:, at:] = tall.T.astype(BF)


def pack(*parts):
    vmem = pl.BlockSpec()
    return pl.pallas_call(
        pack_kernel,
        in_specs=[vmem] * 5,
        out_specs=vmem,
        out_shape=shape_of(
            (parts[0].shape[0], sum(part.shape[1] for part in parts[:4]) + 128), BF
        ),
        compiler_params=params(8),
        cost_estimate=lasting(1),
        name="pack_weights",
    )(*[far(part) for part in parts])


def total_kernel(states, got_ref, own_ref, shared_ref):
    total = jnp.sum(got_ref[...].astype(F32), axis=0)
    rows = total.shape[0]
    inner = own_ref.shape[1] - 128
    both = inner + states
    own_ref[:, :inner] = total[:, :inner]
    own_ref[:, inner:] = total[:, both:]
    shared_ref[:rows] = total[:, inner:both]
    per = inner // states
    for k in range(2 * per):
        line = rows - 3 + k // per
        at = states * (k % per)
        shared_ref[rows + k : rows + k + 1] = total[line : line + 1, at : at + states]


def total_of(got, states):
    count, rows, columns = got.shape
    vmem = pl.BlockSpec()
    extra = rows + 2 * ((columns - states - 128) // states)
    return pl.pallas_call(
        functools.partial(total_kernel, states),
        in_specs=[vmem],
        out_specs=[vmem, vmem],
        out_shape=[shape_of((rows, columns - states), F32), shape_of((extra, states), F32)],
        compiler_params=params(16),
        cost_estimate=lasting(3),
        name="late_total",
    )(got)


def deliver_kernel(
    own_ref, s0, s1, s2, s3,
    norm_ref, x_ref, bc_ref, dt_ref, conv_x_ref, conv_bc_ref, head_ref, gate_ref,
):
    shared = (s0[...] + s1[...]) + (s2[...] + s3[...])
    own = own_ref[...]
    block, inner = x_ref.shape
    heads = dt_ref.shape[0]
    x_ref[...] = own[:block, :inner]
    dt_ref[...] = own[:block, inner:].T[:heads]
    conv_x_ref[...] = own[block : block + 5, :inner]
    head_ref[...] = own[block : block + 3, inner : inner + heads]
    gate_ref[...] = own[block + 7, :inner]
    bc_ref[...] = shared[:block]
    conv_bc_ref[...] = shared[block : block + 5]
    states = bc_ref.shape[1]
    for k in range(norm_ref.shape[0] // states):
        norm_ref[states * k : states * k + states] = shared[block + 8 + k]


def deliver(own, shared, block, heads):
    vmem = pl.BlockSpec()
    inner = own.shape[1] - 128
    states = shared[0].shape[1]
    shapes = [
        (2 * inner,), (block, inner), (block, states), (heads, block),
        (5, inner), (5, states), (3, heads), (inner,),
    ]
    return pl.pallas_call(
        deliver_kernel,
        in_specs=[vmem] * 5,
        out_specs=[vmem] * 8,
        out_shape=[shape_of(shape, F32) for shape in shapes],
        compiler_params=params(16),
        cost_estimate=lasting(2),
        name="deliver_late",
    )(own, *shared)


def owner_total(xh_ref, blocks):
    total = sum(block[...].astype(F32) for block in blocks)
    half = total.shape[1] // 2
    turned = jnp.concatenate([total[:, half:], total[:, :half]], axis=1)
    return jnp.where(xh_ref[5] == 0, total, turned)


def output_kernel(meta_ref, b0, b1, b2, b3, hidden_ref, out_ref):
    mixed = owner_total(meta_ref, (b0, b1, b2, b3))
    out_ref[...] = (hidden_ref[...].astype(F32) + mixed).astype(BF)


def finish_output(meta, blocks, hidden):
    vmem = pl.BlockSpec()
    return pl.pallas_call(
        output_kernel,
        in_specs=[pl.BlockSpec(memory_space=pltpu.SMEM)] + [vmem] * 5,
        out_specs=vmem,
        out_shape=shape_of(hidden.shape, BF),
        compiler_params=params(16),
        cost_estimate=lasting(3),
        name="finish_output",
    )(meta, *[far(block) for block in blocks], far(hidden))


def input_kernel(meta_ref, b0, b1, b2, b3, hidden_ref, cot_ref, gain_ref, out_ref):
    scaled = owner_total(meta_ref, (b0, b1, b2, b3)) * gain_ref[...]
    resid = hidden_ref[...].astype(F32)
    inv = lax.rsqrt(jnp.mean(resid * resid, axis=1, keepdims=True) + EPS)
    along = jnp.mean(resid * scaled, axis=1, keepdims=True) * (inv * inv * inv)
    out_ref[...] = inv * scaled - resid * along + cot_ref[...].astype(F32)


def finish_input(meta, blocks, hidden, cot, gain):
    vmem = pl.BlockSpec()
    return pl.pallas_call(
        input_kernel,
        in_specs=[pl.BlockSpec(memory_space=pltpu.SMEM)] + [vmem] * 7,
        out_specs=vmem,
        out_shape=shape_of(hidden.shape, F32),
        compiler_params=params(16),
        cost_estimate=lasting(3),
        name="finish_input",
    )(meta, *blocks, far(hidden), far(cot), gain)


def mixer_tables(conv_x, conv_bc, head_params):
    heads = head_params.shape[1]
    inner = conv_x.shape[1]
    taps = jnp.pad(jnp.concatenate([conv_x, conv_bc], axis=1), ((0, 3), (0, 0)))
    head = jnp.stack([-jnp.exp(head_params[0]), head_params[1]])
    head = jnp.pad(head, ((0, 6), (0, 128 - heads)))
    skip = jnp.repeat(head_params[2], inner // heads)[None]
    owner = lax.broadcasted_iota(jnp.int32, (256, inner), 1) // (inner // heads)
    one = owner == lax.broadcasted_iota(jnp.int32, (256, inner), 0) % 128
    return taps, head, skip, one.astype(BF)


def mixer_forward(pre, taps, head, skip, spread):
    length, columns = pre.shape
    both = taps.shape[1]
    inner = skip.shape[1]
    steps = length // SPAN
    return pl.pallas_call(
        forward_kernel,
        grid=(steps,),
        in_specs=[
            pl.BlockSpec((SPAN, columns), lambda i: (i, 0)),
            whole(taps.shape), whole(head.shape), whole(skip.shape), whole(spread.shape),
        ],
        out_specs=[
            pl.BlockSpec((SPAN, inner), lambda i: (i, 0)),
            pl.BlockSpec((128, inner), lambda i: (i, 0)),
            pl.BlockSpec((SPAN, both), lambda i: (i, 0)),
        ],
        out_shape=[
            shape_of((length, inner), F32),
            stored((steps * 128, inner), BF),
            stored((length, both), F32),
        ],
        scratch_shapes=[pltpu.VMEM((SPAN + 8, both), F32), pltpu.VMEM((128, inner), F32)],
        compiler_params=params(20, "arbitrary"),
        cost_estimate=lasting(13),
        name="mixer_forward",
    )(near(pre), taps, head, skip, spread)


def mixer_backward(pre, conv, dy, kept, taps, head, skip, spread):
    length, columns = pre.shape
    both = taps.shape[1]
    inner = skip.shape[1]
    steps = length // SPAN
    last = steps - 1
    return pl.pallas_call(
        backward_kernel,
        grid=(steps,),
        in_specs=[
            pl.BlockSpec((SPAN, columns), lambda i: (last - i, 0)),
            pl.BlockSpec((SPAN, both), lambda i: (last - i, 0)),
            pl.BlockSpec((SPAN, inner), lambda i: (last - i, 0)),
            pl.BlockSpec((128, inner), lambda i: (last - i, 0)),
            whole(taps.shape), whole(head.shape), whole(skip.shape), whole(spread.shape),
        ],
        out_specs=[
            pl.BlockSpec((SPAN, columns), lambda i: (last - i, 0)),
            whole((8, both)),
            whole((8, 128)),
        ],
        out_shape=[
            held_near((length, columns), BF),
            shape_of((8, both), F32),
            shape_of((8, 128), F32),
        ],
        scratch_shapes=[
            pltpu.VMEM((SPAN + 8, both), F32),
            pltpu.VMEM((128, inner), F32),
            pltpu.VMEM((8, inner), F32),
        ],
        compiler_params=params(24, "arbitrary"),
        cost_estimate=lasting(30),
        name="mixer_backward",
    )(far(pre), far(conv), far(dy), far(kept), taps, head, skip, spread)


CELLS = [(xh, xl, core) for xh in range(2) for xl in range(2) for core in range(2)]
TURNS = [(a, b) for a in range(2) for b in range(2)]


def moves(rule):
    return [(4 * c[0] + 2 * c[1] + c[2], 4 * d[0] + 2 * d[1] + d[2]) for c in CELLS for d in [rule(*c)]]


def permute(value, rule):
    return lax.ppermute(value, GROUP, moves(rule))


def trade(value):
    return permute(
        value, lambda xh, xl, core: (xh, xl, core) if xh == core else (1 - xh, xl, 1 - core)
    )


def swap_core(value):
    return lax.ppermute(value, "core", [(0, 1), (1, 0)])


def to_workers(value):
    return [
        permute(value, lambda xh, xl, core, a=a, b=b: (core ^ a, xl ^ b, xh)) for a, b in TURNS
    ]


def to_owners(blocks):
    return [
        permute(block, lambda xh, xl, core, a=a, b=b: (core, xl ^ b, xh ^ a))
        for block, (a, b) in zip(blocks, TURNS)
    ]


def around(value):
    return [value] + [
        permute(value, lambda xh, xl, core, a=a, b=b: (xh ^ a, xl ^ b, core)) for a, b in TURNS[1:]
    ]


def gather_plane(shard):
    count = lax.axis_size(PLANE)
    spread = jnp.broadcast_to(shard[None], (count,) + shard.shape)
    got = lax.all_to_all(spread, PLANE, 0, 0, tiled=True)
    return got.reshape((count * shard.shape[0],) + shard.shape[1:])


def exchange(blocks):
    return lax.all_to_all(blocks, PLANE, 0, 0, tiled=True)


def after(*values):
    return lax.optimization_barrier(values)


def on_device(
    hidden_in,
    cotangent,
    norm_gain,
    w_z,
    w_x,
    w_bc,
    w_dt,
    conv_x,
    conv_bc,
    head_params,
    gate_gain,
    w_out,
):
    block, wide = w_x.shape
    states = w_bc.shape[1]
    heads = w_dt.shape[1]
    both = wide + states
    xh, xl, core = (lax.axis_index(axis) for axis in GROUP)
    meta = jnp.stack([(xl ^ b) * 2 + (xh ^ a) for a, b in TURNS] + [core, xh]).astype(jnp.int32)
    gain = norm_gain[None]

    weights = trade(pack(w_z, w_out.T, w_x, w_bc, w_dt.T))
    small = jnp.concatenate(
        [conv_x, gate_gain[None], jnp.pad(head_params, ((0, 0), (0, wide - heads)))[:2]]
    )
    small = jnp.concatenate([small, jnp.pad(head_params[2:], ((0, 7), (0, wide - heads)))])
    small, weights = after(small, weights)
    small = jnp.where(core == xh, small, swap_core(small))

    mine = gather_plane(weights)
    hidden, weights = after(hidden_in, weights)
    hidden_blocks = to_workers(hidden)
    first_half, cot, small = after(hidden_blocks[:2], cotangent, small)
    hidden_blocks = first_half + hidden_blocks[2:]
    cot_blocks = to_workers(cot)
    tokens, tokens_t = place(meta, gain, hidden_blocks, True)
    tokens, mine, cot_first = after(tokens, mine, cot_blocks[0])
    cot_blocks = [cot_first] + cot_blocks[1:]
    other = swap_core(mine)

    conv_x, gate_row, head_params = small[:5], small[5:6], small[6:9, :heads]
    taps, head, skip, spread = mixer_tables(conv_x, conv_bc, head_params)
    pre = project(tokens, mine, other, wide)
    y, kept, conv = mixer_forward(pre, taps, head, skip, spread)
    y, cot_blocks = after(y, cot_blocks)
    cot, cot_t = place(meta, gain, cot_blocks, False)
    z, dy, sums = gate_sums(tokens, cot, mine, other, y, gate_row)
    normed_y, gate, dscan, gain_grad, keep, send = gate_back(
        block, 4.0 * wide, around(sums), z, dy, y, gate_row, tokens_t, cot_t
    )

    early = (keep.astype(F32) + swap_core(send).astype(F32)).astype(BF)
    out_blocks = project_out(meta, normed_y, mine, other)
    dscan, early, out_blocks = after(dscan, early, out_blocks)
    early = exchange(early)
    out_blocks = to_owners(out_blocks)
    late, conv_grad, head_grad = mixer_backward(pre, conv, dscan, kept, taps, head, skip, spread)
    *back_blocks, norm_part = project_back(
        meta, late, gate, mine, other, mine, other, tokens, gain
    )
    late, back_blocks, out_blocks = after(late, back_blocks, out_blocks)
    back_blocks = to_owners(back_blocks)

    rest = jnp.pad(
        jnp.concatenate([norm_part[:1, :wide], norm_part[:1, wide:], gain_grad[:1]]),
        ((0, 0), (0, states)),
    )
    vector = jnp.concatenate([jnp.concatenate([conv_grad[:5], rest]), head_grad], axis=1)
    vector = jnp.pad(vector, ((0, 8), (0, 0)))
    keep, send = weight_grad(tokens_t, late, vector)
    send, early, back_first = after(send, early, back_blocks[0])
    output = finish_output(meta, out_blocks, hidden_in)
    got = swap_core(send).astype(F32)
    half = keep.shape[0]
    late_sum = (keep + got[:half]).astype(BF).reshape(-1, block, both + 128)
    vector = (vector[:8] + got[half : half + 8]).astype(BF)
    vector = jnp.broadcast_to(vector[None], (late_sum.shape[0],) + vector.shape)
    late_sum = jnp.concatenate([late_sum, vector], axis=1)
    back_blocks = [back_first] + back_blocks[1:]
    input_grad = finish_input(meta, back_blocks, hidden_in, cotangent, gain)
    early = trade(early.astype(F32).sum(axis=0))
    got, input_grad, early, output = after(exchange(late_sum), input_grad, early, output)
    own, shared = total_of(got, states)

    shared = [
        permute(shared, lambda xh, xl, core, a=a, b=b: (core, xl ^ b, xh ^ a)) for a, b in TURNS
    ]
    norm_grad, x_grad, bc_grad, dt_grad, conv_x_grad, conv_bc_grad, head_part, gate_part = deliver(
        trade(own), shared, block, heads
    )
    return (
        output,
        input_grad,
        norm_grad,
        early[0],
        x_grad,
        bc_grad,
        dt_grad.T,
        conv_x_grad,
        conv_bc_grad,
        head_part,
        gate_part,
        early[1].T,
    )


def solution(mesh):
    fine = Mesh(mesh.devices.reshape(2, 4, 4, 2, 2), AXES)
    rows, both, lanes = P(AXES, None), P(DP, TN), P(None, TN)
    return jax.shard_map(
        on_device,
        mesh=fine,
        in_specs=(rows, rows, P(), both, both, P(DP, None), both, lanes, P(), lanes, P(TN), P(TN, DP)),
        out_specs=(
            rows, rows, P(), both, both, P(DP, None), both, lanes, P(), lanes, P(TN), P(TN, DP)
        ),
        check_vma=False,
    )
```

```python
import functools
import jax
import jax.numpy as jnp
from jax import lax
from jax.experimental import pallas as pl
from jax.experimental.pallas import tpu as pltpu
from jax.sharding import Mesh, PartitionSpec as P

EPS = 1e-05
AXES = ("xh", "y", "z", "xl", "core")
DP = ("xh", "y", "z")
TN = ("xl", "core")
GROUP = ("xh", "xl", "core")
PLANE = ("y", "z")
BF = jnp.bfloat16
F32 = jnp.float32
HI = lax.Precision.HIGHEST
SPAN = 128
LIMIT = 36


def near(value):
    return pltpu.with_memory_space_constraint(value, pltpu.VMEM)


def far(value):
    return pltpu.with_memory_space_constraint(value, pltpu.HBM)


ROWS = 512
SCALE = 1.15e9


def nn(left, right):
    return lax.dot_general(left, right, (((1,), (0,)), ((), ())), preferred_element_type=F32)


def nt(left, right):
    return lax.dot_general(left, right, (((1,), (1,)), ((), ())), preferred_element_type=F32)


def exact(left, right):
    return lax.dot_general(
        left, right, (((1,), (0,)), ((), ())), precision=HI, preferred_element_type=F32
    )


def exact_nt(left, right):
    return lax.dot_general(
        left, right, (((1,), (1,)), ((), ())), precision=HI, preferred_element_type=F32
    )


def halves(value):
    high = value.astype(BF)
    low = (value - high.astype(F32)).astype(BF)
    return high, low


def expand(value, spread):
    high, low = halves(value)
    return nn(jnp.concatenate([high, low], axis=1), spread)


def by_head(value, spread):
    width = spread.shape[0] // 2
    high, low = halves(value)
    return nt(high, spread[:width]) + nt(low, spread[:width])


def logistic(value):
    return 1.0 / (1.0 + jnp.exp(-value))


def sigmoid(value):
    return 0.5 * jnp.tanh(0.5 * value) + 0.5


def softplus(value):
    return jnp.maximum(value, 0.0) + jnp.log1p(jnp.exp(-jnp.abs(value)))


def conv_rows(ext_ref, taps):
    total = taps[4:5] + ext_ref[5 : 5 + SPAN] * taps[0:1]
    for k in range(1, 4):
        total = total + ext_ref[5 + k : 5 + k + SPAN] * taps[k : k + 1]
    return total


def scan_parts(conv, pre_dt, head, spread, tri):
    sig = sigmoid(conv)
    xbc = conv * sig
    raw = pre_dt + head[1:2]
    step = softplus(raw)
    decay = exact(tri, step * head[0:1])
    last = decay[SPAN - 1 : SPAN]
    grown = expand(jnp.concatenate([step, jnp.exp(decay), jnp.exp(last - decay)], axis=0), spread)
    step_x, start_x, end_x = grown[:SPAN], grown[SPAN : 2 * SPAN], grown[2 * SPAN :]
    return sig, xbc, raw, step, decay, step_x, start_x, end_x


def forward_kernel(
    pre_ref, taps_ref, head_ref, skip_ref, spread_ref, y_ref, kept_ref, conv_ref, ext_ref, state_ref
):
    inner = y_ref.shape[1]
    both = ext_ref.shape[1]

    @pl.when(pl.program_id(0) == 0)
    def _():
        ext_ref[0:8] = jnp.zeros((8, both), F32)
        state_ref[...] = jnp.zeros_like(state_ref)

    ext_ref[8 : 8 + SPAN] = pre_ref[:, :both]
    rows = lax.broadcasted_iota(jnp.int32, (SPAN, SPAN), 0)
    cols = lax.broadcasted_iota(jnp.int32, (SPAN, SPAN), 1)
    keep = rows >= cols
    tri = jnp.where(keep, 1.0, 0.0).astype(F32)
    spread = spread_ref[...]
    conv = conv_rows(ext_ref, taps_ref[...])
    conv_ref[...] = conv
    sig, xbc, raw, step, decay, step_x, start_x, end_x = scan_parts(
        conv, pre_ref[:, both:], head_ref[...], spread, tri
    )
    ext_ref[0:8] = ext_ref[SPAN : SPAN + 8]
    state_width = (both - inner) // 2
    x = xbc[:, :inner]
    b = xbc[:, inner : inner + state_width]
    c = xbc[:, inner + state_width :]
    decay_t = decay.T
    scaled = x * step_x
    low = scaled.astype(BF)
    scores = exact_nt(c, b)
    state = state_ref[...]
    state_low = state.astype(BF)
    kept_ref[...] = state_low
    carried = nn(c.astype(BF), state_low) * start_x + x * skip_ref[...]
    left = cols < 64
    for pair in range(inner // 128):
        at = slice(128 * pair, 128 * pair + 128)
        x_pair = low[:, at]
        found = []
        for h in (2 * pair, 2 * pair + 1):
            gap = decay[:, h : h + 1] - decay_t[h : h + 1]
            weight = jnp.exp(jnp.where(keep, gap, -1e30)) * scores
            found.append(nn(weight.astype(BF), x_pair))
        y_ref[:, at] = jnp.where(left, found[0], found[1]) + carried[:, at]
    state_ref[...] = state * start_x[SPAN - 1 : SPAN] + nn(
        b.T.astype(BF), (scaled * end_x).astype(BF)
    )


def backward_kernel(
    pre_ref, conv_ref, dy_ref, kept_ref, taps_ref, head_ref, skip_ref, spread_ref,
    late_ref, conv_grad_ref, head_grad_ref,
    dext_ref, dstate_ref, skip_sum_ref,
):
    inner = dy_ref.shape[1]
    both = dext_ref.shape[1]
    steps = pl.num_programs(0)
    at_step = pl.program_id(0)

    @pl.when(at_step == 0)
    def _():
        dext_ref[SPAN : SPAN + 8] = jnp.zeros((8, both), F32)
        dstate_ref[...] = jnp.zeros_like(dstate_ref)
        skip_sum_ref[...] = jnp.zeros_like(skip_sum_ref)
        conv_grad_ref[...] = jnp.zeros_like(conv_grad_ref)
        head_grad_ref[...] = jnp.zeros_like(head_grad_ref)

    rows = lax.broadcasted_iota(jnp.int32, (SPAN, SPAN), 0)
    cols = lax.broadcasted_iota(jnp.int32, (SPAN, SPAN), 1)
    tri = jnp.where(rows >= cols, 1.0, 0.0).astype(F32)
    upper = jnp.where(cols >= rows, 1.0, 0.0).astype(F32)
    keep = cols >= rows
    spread = spread_ref[...]
    taps = taps_ref[...]
    head = head_ref[...]
    conv = conv_ref[...]
    sig, xbc, raw, step, decay, step_x, start_x, end_x = scan_parts(
        conv, pre_ref[:, both:], head, spread, tri
    )
    state_width = (both - inner) // 2
    x = xbc[:, :inner]
    b = xbc[:, inner : inner + state_width]
    c = xbc[:, inner + state_width :]
    b_low, c_low = b.astype(BF), c.astype(BF)
    decay_t = decay.T
    scaled = x * step_x
    low = scaled.astype(BF)
    scores = exact_nt(b, c)
    dy = dy_ref[...].astype(F32)
    dy_low = dy.astype(BF)
    kept = kept_ref[...]
    dstate = dstate_ref[...]
    dstate_low = dstate.astype(BF)
    left = cols < 64
    wide_rows = lax.broadcasted_iota(jnp.int32, (SPAN, SPAN), 0)
    d_scores = jnp.zeros((SPAN, SPAN), F32)
    into = jnp.zeros((SPAN, SPAN), F32)
    out_of = jnp.zeros((SPAN, SPAN), F32)
    pieces = []
    none = jnp.zeros((SPAN, 128), BF)
    for pair in range(inner // 128):
        at = slice(128 * pair, 128 * pair + 128)
        x_pair = low[:, at]
        dy_pair = dy_low[:, at]
        found = []
        for side, h in enumerate((2 * pair, 2 * pair + 1)):
            gap = decay_t[h : h + 1] - decay[:, h : h + 1]
            fall = jnp.exp(jnp.where(keep, gap, -1e30))
            mine = jnp.where(left if side == 0 else ~left, dy_pair, none)
            back = nt(x_pair, mine) * fall
            d_scores = d_scores + back
            both_ways = back * scores
            into = jnp.where(wide_rows == h, jnp.sum(both_ways, axis=0, keepdims=True), into)
            out_of = jnp.where(cols == h, jnp.sum(both_ways, axis=1, keepdims=True), out_of)
            found.append(nn((fall * scores).astype(BF), dy_pair))
        pieces.append(jnp.where(left, found[0], found[1]))
    inside = jnp.concatenate(pieces, axis=1)
    dy_start = dy * start_x
    dy_start_low = dy_start.astype(BF)
    from_state = nn(c_low, kept)
    scaled_end = scaled * end_x
    d_end = nn(b_low, dstate_low)
    d_scaled = inside + d_end * end_x
    pair_start = by_head(dy_start * from_state, spread)
    pair_end = by_head(scaled_end * d_end, spread)
    d_scores_low = d_scores.astype(BF)
    d_c = nn(d_scores.T.astype(BF), b_low) + nt(dy_start_low, kept)
    d_b = nn(d_scores_low, c_low) + nt(scaled_end.astype(BF), dstate_low)
    through = jnp.sum(kept.astype(F32) * dstate, axis=0, keepdims=True)
    through = by_head(jnp.broadcast_to(through * start_x[SPAN - 1 : SPAN], (8, inner)), spread)[0:1]
    at_end = jnp.sum(pair_end, axis=0, keepdims=True) + through
    d_decay = into.T - out_of + pair_start - pair_end
    d_decay = d_decay + jnp.where(rows == SPAN - 1, at_end, 0.0)
    d_log = exact(upper, d_decay)
    d_step = by_head(d_scaled * x, spread) + d_log * head[0:1]
    d_raw = d_step * logistic(raw)
    dstate_ref[...] = dstate * start_x[SPAN - 1 : SPAN] + nn(c.T.astype(BF), dy_start_low)
    late_ref[:, both:] = d_raw.astype(BF)
    head_grad_ref[0:1] += jnp.sum(d_log * step, axis=0, keepdims=True) * head[0:1]
    head_grad_ref[1:2] += jnp.sum(d_raw, axis=0, keepdims=True)
    skip_sum_ref[0:1] += jnp.sum(dy * x, axis=0, keepdims=True)
    dx = d_scaled * step_x + dy * skip_ref[...]
    d_conv = jnp.concatenate([dx, d_b, d_c], axis=1) * (sig * (1.0 + conv * (1.0 - sig)))
    dext_ref[0:SPAN] = d_conv
    values = pre_ref[:, :both]
    d_pre = d_conv * taps[3:4]
    conv_grad_ref[3:4] += jnp.sum(d_conv * values, axis=0, keepdims=True)
    for k in range(3):
        moved = dext_ref[3 - k : 3 - k + SPAN]
        d_pre = d_pre + moved * taps[k : k + 1]
        conv_grad_ref[k : k + 1] += jnp.sum(moved * values, axis=0, keepdims=True)
    conv_grad_ref[4:5] += jnp.sum(d_conv, axis=0, keepdims=True)
    dext_ref[SPAN : SPAN + 8] = dext_ref[0:8]
    late_ref[:, :both] = d_pre.astype(BF)

    @pl.when(at_step == steps - 1)
    def _():
        head_grad_ref[2:3] += by_head(
            jnp.broadcast_to(skip_sum_ref[0:1], (8, inner)), spread
        )[0:1]


def whole(shape):
    return pl.BlockSpec(shape, lambda *_: (0,) * len(shape))


def column(rows, width, shift=0):
    return pl.BlockSpec((rows, width), lambda j, *_: (0, j + shift))


def shape_of(shape, dtype):
    return jax.ShapeDtypeStruct(shape, dtype)


def stored(shape, dtype):
    return pltpu.HBM(shape, dtype)


def held_near(shape, dtype):
    return pltpu.VMEM(shape, dtype)


def params(limit, *semantics):
    return pltpu.CompilerParams(
        dimension_semantics=semantics or None, vmem_limit_bytes=LIMIT * 1024 * 1024
    )


def lasting(us):
    return pl.CostEstimate(flops=int(us * SCALE), bytes_accessed=1024, transcendentals=0)


def place_kernel(normalise, meta_ref, gain_ref, *refs):
    blocks, out_ref, flip_ref = refs[:4], refs[4], refs[5]
    rows, width = blocks[0].shape
    half = width // 2
    core = meta_ref[4]
    first = pl.multiple_of(core * half, 128)
    second = pl.multiple_of((1 - core) * half, 128)
    for k, block in enumerate(blocks):
        at = pl.multiple_of(meta_ref[k] * rows, rows)
        value = block[...].astype(F32)
        if normalise:
            scale = lax.rsqrt(jnp.mean(value * value, axis=1, keepdims=True) + EPS)
            value = value * scale * gain_ref[...]
        low = value.astype(BF)
        out_ref[pl.ds(at, rows), pl.ds(first, half)] = low[:, :half]
        out_ref[pl.ds(at, rows), pl.ds(second, half)] = low[:, half:]
        flip = value.T.astype(BF)
        flip_ref[pl.ds(first, half), pl.ds(at, rows)] = flip[:half]
        flip_ref[pl.ds(second, half), pl.ds(at, rows)] = flip[half:]


def place(meta, gain, blocks, normalise):
    rows, width = blocks[0].shape
    vmem = pl.BlockSpec()
    return pl.pallas_call(
        functools.partial(place_kernel, normalise),
        in_specs=[pl.BlockSpec(memory_space=pltpu.SMEM)] + [vmem] * 5,
        out_specs=[vmem, vmem],
        out_shape=[
            (stored if normalise else shape_of)((4 * rows, width), BF),
            shape_of((width, 4 * rows), BF),
        ],
        compiler_params=params(24),
        cost_estimate=lasting(6),
        name="place_normed" if normalise else "place_cotangent",
    )(meta, gain, *[far(block) for block in blocks])


def project_kernel(tokens_ref, xm_ref, xo_ref, zm_ref, zo_ref, pre_ref, z_ref):
    half = xm_ref.shape[0]
    for first, second, out in ((xm_ref, xo_ref, pre_ref), (zm_ref, zo_ref, z_ref)):
        out[...] = nn(tokens_ref[:, :half], first[...]) + nn(tokens_ref[:, half:], second[...])


def project(tokens, mine, other, inner):
    half = mine.shape[0]
    length = tokens.shape[0]
    columns = mine.shape[1] - 2 * inner
    rows = ROWS

    def part(width, shift):
        return pl.BlockSpec(
            (pl.Element(half), pl.Element(width)),
            lambda i: (0, shift),
            pipeline_mode=pl.Buffered(1),
        )

    return pl.pallas_call(
        project_kernel,
        grid=(length // rows,),
        in_specs=[pl.BlockSpec((rows, 2 * half), lambda i: (i, 0))]
        + [part(columns, 2 * inner)] * 2
        + [part(inner, 0)] * 2,
        out_specs=[
            pl.BlockSpec((rows, columns), lambda i: (i, 0)),
            pl.BlockSpec((rows, inner), lambda i: (i, 0)),
        ],
        out_shape=[shape_of((length, columns), F32), shape_of((length, inner), F32)],
        compiler_params=params(20, "arbitrary"),
        cost_estimate=lasting(6),
        name="project_in",
    )(far(tokens), far(mine), other, far(mine), other)


def gate_sums_kernel(
    cot_ref, om_ref, oo_ref, y_ref, z_ref, gain_ref, dy_ref, sums_ref
):
    half = om_ref.shape[0]
    z = z_ref[...]
    dy = nn(cot_ref[:, :half], om_ref[...]) + nn(cot_ref[:, half:], oo_ref[...])
    dy_ref[...] = dy
    gated = y_ref[...] * (z * sigmoid(z))
    ones = jnp.ones((8, z.shape[1]), BF)
    found = []
    for value in (gated * gated, gated * (dy * gain_ref[...])):
        high, low = halves(value)
        found.append(nt(ones, high) + nt(ones, low))
    row = lax.broadcasted_iota(jnp.int32, found[0].shape, 0)
    total = jnp.where(row == 0, found[0], found[1])

    @pl.when(pl.program_id(0) == 0)
    def _():
        sums_ref[...] = total

    @pl.when(pl.program_id(0) > 0)
    def _():
        sums_ref[...] += total


def gate_sums(cot, mine, other, y, z, gain):
    length, inner = y.shape
    half = mine.shape[0]
    tile = 256
    steps = inner // tile
    return pl.pallas_call(
        gate_sums_kernel,
        grid=(steps,),
        in_specs=[
            whole(cot.shape),
            column(half, tile, steps),
            column(half, tile, steps),
            column(length, tile),
            column(length, tile),
            column(1, tile),
        ],
        out_specs=[column(length, tile), whole((8, length))],
        out_shape=[shape_of((length, inner), F32), shape_of((8, length), F32)],
        compiler_params=params(36, "arbitrary"),
        cost_estimate=lasting(6),
        name="gate_sums",
    )(near(cot), far(mine), far(other), near(y), near(z), gain)


def gate_back_kernel(
    width_all, s0, s1, s2, s3, z_ref, dy_ref, y_ref, gain_ref, tokens_t_ref, cot_t_ref,
    normed_ref, gate_ref, dscan_ref, gain_grad_ref, keep_ref, send_ref,
):
    sums = (s0[...] + s1[...]) + (s2[...] + s3[...])
    flat = sums.T
    rms = lax.rsqrt(flat[:, 0:1] / width_all + EPS)
    inner = flat[:, 1:2] * (rms * rms * rms / width_all)
    z = z_ref[...]
    y = y_ref[...]
    dy = dy_ref[...]
    gain = gain_ref[...]
    sig = sigmoid(z)
    act = z * sig
    gated = y * act
    unit = gated * rms
    normed = (unit * gain).astype(BF)
    normed_ref[...] = normed
    gain_grad_ref[...] = jnp.broadcast_to(
        jnp.sum(dy * unit, axis=0, keepdims=True), gain_grad_ref.shape
    )
    d_gated = rms * (dy * gain) - gated * inner
    dscan_ref[...] = d_gated * act
    gate = (d_gated * y * (sig * (1.0 + z * (1.0 - sig)))).astype(BF)
    gate_ref[...] = gate
    half = tokens_t_ref.shape[0] // 2
    for side, (left, right) in enumerate(((tokens_t_ref, gate), (cot_t_ref, normed))):
        for out, at in ((keep_ref, slice(0, half)), (send_ref, slice(half, 2 * half))):
            found = nn(left[at], right).astype(BF)
            out[:, side] = found.reshape(out.shape[0], out.shape[2], found.shape[1])


def gate_back(block, width_all, sums, z, dy, y, gain, tokens_t, cot_t):
    length, inner = y.shape
    half = tokens_t.shape[0] // 2
    tile = 256
    pile = pl.BlockSpec((half // block, 2, block, tile), lambda j: (0, 0, 0, j))
    return pl.pallas_call(
        functools.partial(gate_back_kernel, width_all),
        grid=(inner // tile,),
        in_specs=[whole((8, length))] * 4
        + [column(length, tile)] * 3
        + [column(1, tile), whole(tokens_t.shape), whole(cot_t.shape)],
        out_specs=[column(length, tile)] * 3 + [column(8, tile), pile, pile],
        out_shape=[
            stored((length, inner), BF),
            stored((length, inner), BF),
            stored((length, inner), F32),
            shape_of((8, inner), F32),
            shape_of((half // block, 2, block, inner), BF),
            shape_of((half // block, 2, block, inner), BF),
        ],
        compiler_params=params(44, "arbitrary"),
        cost_estimate=lasting(12),
        name="gate_back",
    )(*sums, near(z), near(dy), near(y), gain, near(tokens_t), near(cot_t))


def scatter_rows(meta_ref, found, scratch, outs):
    rows = outs[0].shape[0]
    scratch[...] = found
    for k, out in enumerate(outs):
        out[...] = scratch[pl.ds(pl.multiple_of(meta_ref[k] * rows, rows), rows), :].astype(BF)


def project_out_kernel(meta_ref, normed_ref, om_ref, oo_ref, *refs):
    outs, scratch = refs[:4], refs[4]

    def step(right):
        scatter_rows(meta_ref, nt(normed_ref[...], right[...]), scratch, outs)

    first = pl.program_id(0) < pl.num_programs(0) // 2
    pl.when(first)(lambda: step(om_ref))
    pl.when(jnp.logical_not(first))(lambda: step(oo_ref))


def sides(tile, columns, shift, per):
    return [
        pl.BlockSpec(
            (pl.Element(tile), pl.Element(columns)),
            lambda j: (jnp.minimum(j, per - 1) * tile, shift),
        ),
        pl.BlockSpec(
            (pl.Element(tile), pl.Element(columns)),
            lambda j: (jnp.maximum(j - per, 0) * tile, shift),
        ),
    ]


def project_out(meta, normed_y, mine, other):
    length, inner = normed_y.shape
    half = mine.shape[0]
    rows = length // 4
    per = 3
    tile = half // per
    return pl.pallas_call(
        project_out_kernel,
        grid=(2 * per,),
        in_specs=[pl.BlockSpec(memory_space=pltpu.SMEM), whole(normed_y.shape)]
        + sides(tile, inner, inner, per),
        out_specs=[column(rows, tile)] * 4,
        out_shape=[stored((rows, 2 * half), BF)] * 4,
        scratch_shapes=[pltpu.VMEM((length, tile), F32)],
        compiler_params=params(24, "arbitrary"),
        cost_estimate=lasting(6),
        name="project_out",
    )(meta, far(normed_y), far(mine), far(other))


def project_back_kernel(
    meta_ref, late_ref, gate_ref, xm_ref, xo_ref, zm_ref, zo_ref, tokens_ref, gain_ref, *refs
):
    outs, grad_ref, scratch = refs[:4], refs[4], refs[5]
    tile = scratch.shape[1]
    j = pl.program_id(0)
    per = pl.num_programs(0) // 2
    side, within = j // per, j % per
    core = meta_ref[4]

    def step(x_ref, z_ref):
        found = nt(late_ref[...], x_ref[...]) + nt(gate_ref[...], z_ref[...])
        total = jnp.sum(found * tokens_ref[...].astype(F32), axis=0, keepdims=True)
        owner = side + core - 2 * side * core
        place = pl.ds(pl.multiple_of((per * owner + within) * tile, 128), tile)
        grad_ref[:, place] = jnp.broadcast_to(total / gain_ref[:, place], (8, tile))
        scatter_rows(meta_ref, found, scratch, outs)

    pl.when(side == 0)(lambda: step(xm_ref, zm_ref))
    pl.when(side == 1)(lambda: step(xo_ref, zo_ref))


def project_back(meta, late, gate, mine1, other1, mine2, other2, tokens, gain):
    length, columns = late.shape
    inner = gate.shape[1]
    half = mine1.shape[0]
    rows = length // 4
    per = 3
    tile = half // per
    return pl.pallas_call(
        project_back_kernel,
        grid=(2 * per,),
        in_specs=[pl.BlockSpec(memory_space=pltpu.SMEM), whole(late.shape), whole(gate.shape)]
        + sides(tile, columns, 2 * inner, per)
        + sides(tile, inner, 0, per)
        + [column(length, tile), whole(gain.shape)],
        out_specs=[column(rows, tile)] * 4 + [whole((8, 2 * half))],
        out_shape=[stored((rows, 2 * half), BF)] * 4 + [shape_of((8, 2 * half), F32)],
        scratch_shapes=[pltpu.VMEM((length, tile), F32)],
        compiler_params=params(32, "arbitrary"),
        cost_estimate=lasting(0.5),
        name="project_back",
    )(
        meta, near(late), far(gate), far(mine1), far(other1), far(mine2), far(other2), far(tokens), gain
    )


def weight_grad_kernel(tokens_t_ref, late_ref, vector_ref, keep_ref, send_ref):
    half = keep_ref.shape[0]
    late = late_ref[...]
    keep_ref[...] = nn(tokens_t_ref[:half], late)
    send_ref[:half] = nn(tokens_t_ref[half:], late).astype(BF)
    send_ref[half:] = vector_ref[...].astype(BF)


def weight_grad(tokens_t, late, vector):
    length, columns = late.shape
    half = tokens_t.shape[0] // 2
    rows = half + vector.shape[0]
    tile = 384
    return pl.pallas_call(
        weight_grad_kernel,
        grid=(columns // tile,),
        in_specs=[whole(tokens_t.shape), column(length, tile), column(vector.shape[0], tile)],
        out_specs=[column(half, tile), column(rows, tile)],
        out_shape=[stored((half, columns), F32), stored((rows, columns), BF)],
        compiler_params=params(24, "arbitrary"),
        cost_estimate=lasting(0.5),
        name="weight_grad",
    )(far(tokens_t), near(late), vector)


def pack_kernel(z_ref, out_ref, x_ref, bc_ref, dt_ref, packed_ref):
    at = 0
    for ref in (z_ref, out_ref, x_ref, bc_ref):
        packed_ref[:, at : at + ref.shape[1]] = ref[...]
        at += ref.shape[1]
    heads, rows = dt_ref.shape
    tall = jnp.concatenate([dt_ref[...].astype(F32), jnp.zeros((128 - heads, rows), F32)], axis=0)
    packed_ref[:, at:] = tall.T.astype(BF)


def pack(*parts):
    vmem = pl.BlockSpec()
    return pl.pallas_call(
        pack_kernel,
        in_specs=[vmem] * 5,
        out_specs=vmem,
        out_shape=shape_of(
            (parts[0].shape[0], sum(part.shape[1] for part in parts[:4]) + 128), BF
        ),
        compiler_params=params(8),
        cost_estimate=lasting(1),
        name="pack_weights",
    )(*[far(part) for part in parts])


def total_kernel(states, got_ref, own_ref, shared_ref):
    total = jnp.sum(got_ref[...].astype(F32), axis=0)
    rows = total.shape[0]
    inner = own_ref.shape[1] - 128
    both = inner + states
    own_ref[:, :inner] = total[:, :inner]
    own_ref[:, inner:] = total[:, both:]
    shared_ref[:rows] = total[:, inner:both]
    per = inner // states
    for k in range(2 * per):
        line = rows - 3 + k // per
        at = states * (k % per)
        shared_ref[rows + k : rows + k + 1] = total[line : line + 1, at : at + states]


def total_of(got, states):
    count, rows, columns = got.shape
    vmem = pl.BlockSpec()
    extra = rows + 2 * ((columns - states - 128) // states)
    return pl.pallas_call(
        functools.partial(total_kernel, states),
        in_specs=[vmem],
        out_specs=[vmem, vmem],
        out_shape=[shape_of((rows, columns - states), F32), shape_of((extra, states), F32)],
        compiler_params=params(16),
        cost_estimate=lasting(3),
        name="late_total",
    )(got)


def deliver_kernel(
    own_ref, s0, s1, s2, s3,
    norm_ref, x_ref, bc_ref, dt_ref, conv_x_ref, conv_bc_ref, head_ref, gate_ref,
):
    shared = (s0[...] + s1[...]) + (s2[...] + s3[...])
    own = own_ref[...]
    block, inner = x_ref.shape
    heads = dt_ref.shape[0]
    x_ref[...] = own[:block, :inner]
    dt_ref[...] = own[:block, inner:].T[:heads]
    conv_x_ref[...] = own[block : block + 5, :inner]
    head_ref[...] = own[block : block + 3, inner : inner + heads]
    gate_ref[...] = own[block + 7, :inner]
    bc_ref[...] = shared[:block]
    conv_bc_ref[...] = shared[block : block + 5]
    states = bc_ref.shape[1]
    for k in range(norm_ref.shape[0] // states):
        norm_ref[states * k : states * k + states] = shared[block + 8 + k]


def deliver(own, shared, block, heads):
    vmem = pl.BlockSpec()
    inner = own.shape[1] - 128
    states = shared[0].shape[1]
    shapes = [
        (2 * inner,), (block, inner), (block, states), (heads, block),
        (5, inner), (5, states), (3, heads), (inner,),
    ]
    return pl.pallas_call(
        deliver_kernel,
        in_specs=[vmem] * 5,
        out_specs=[vmem] * 8,
        out_shape=[shape_of(shape, F32) for shape in shapes],
        compiler_params=params(16),
        cost_estimate=lasting(2),
        name="deliver_late",
    )(own, *shared)


def owner_total(xh_ref, blocks):
    total = sum(block[...].astype(F32) for block in blocks)
    half = total.shape[1] // 2
    turned = jnp.concatenate([total[:, half:], total[:, :half]], axis=1)
    return jnp.where(xh_ref[5] == 0, total, turned)


def output_kernel(meta_ref, b0, b1, b2, b3, hidden_ref, out_ref):
    mixed = owner_total(meta_ref, (b0, b1, b2, b3))
    out_ref[...] = (hidden_ref[...].astype(F32) + mixed).astype(BF)


def finish_output(meta, blocks, hidden):
    vmem = pl.BlockSpec()
    return pl.pallas_call(
        output_kernel,
        in_specs=[pl.BlockSpec(memory_space=pltpu.SMEM)] + [vmem] * 5,
        out_specs=vmem,
        out_shape=shape_of(hidden.shape, BF),
        compiler_params=params(16),
        cost_estimate=lasting(3),
        name="finish_output",
    )(meta, *[far(block) for block in blocks], far(hidden))


def input_kernel(meta_ref, b0, b1, b2, b3, hidden_ref, cot_ref, gain_ref, out_ref):
    scaled = owner_total(meta_ref, (b0, b1, b2, b3)) * gain_ref[...]
    resid = hidden_ref[...].astype(F32)
    inv = lax.rsqrt(jnp.mean(resid * resid, axis=1, keepdims=True) + EPS)
    along = jnp.mean(resid * scaled, axis=1, keepdims=True) * (inv * inv * inv)
    out_ref[...] = inv * scaled - resid * along + cot_ref[...].astype(F32)


def finish_input(meta, blocks, hidden, cot, gain):
    vmem = pl.BlockSpec()
    return pl.pallas_call(
        input_kernel,
        in_specs=[pl.BlockSpec(memory_space=pltpu.SMEM)] + [vmem] * 7,
        out_specs=vmem,
        out_shape=shape_of(hidden.shape, F32),
        compiler_params=params(16),
        cost_estimate=lasting(3),
        name="finish_input",
    )(meta, *blocks, far(hidden), far(cot), gain)


def mixer_tables(conv_x, conv_bc, head_params):
    heads = head_params.shape[1]
    inner = conv_x.shape[1]
    taps = jnp.pad(jnp.concatenate([conv_x, conv_bc], axis=1), ((0, 3), (0, 0)))
    head = jnp.stack([-jnp.exp(head_params[0]), head_params[1]])
    head = jnp.pad(head, ((0, 6), (0, 128 - heads)))
    skip = jnp.repeat(head_params[2], inner // heads)[None]
    owner = lax.broadcasted_iota(jnp.int32, (256, inner), 1) // (inner // heads)
    one = owner == lax.broadcasted_iota(jnp.int32, (256, inner), 0) % 128
    return taps, head, skip, one.astype(BF)


def mixer_forward(pre, taps, head, skip, spread):
    length, columns = pre.shape
    both = taps.shape[1]
    inner = skip.shape[1]
    steps = length // SPAN
    return pl.pallas_call(
        forward_kernel,
        grid=(steps,),
        in_specs=[
            pl.BlockSpec((SPAN, columns), lambda i: (i, 0)),
            whole(taps.shape), whole(head.shape), whole(skip.shape), whole(spread.shape),
        ],
        out_specs=[
            pl.BlockSpec((SPAN, inner), lambda i: (i, 0)),
            pl.BlockSpec((128, inner), lambda i: (i, 0)),
            pl.BlockSpec((SPAN, both), lambda i: (i, 0)),
        ],
        out_shape=[
            shape_of((length, inner), F32),
            stored((steps * 128, inner), BF),
            stored((length, both), F32),
        ],
        scratch_shapes=[pltpu.VMEM((SPAN + 8, both), F32), pltpu.VMEM((128, inner), F32)],
        compiler_params=params(20, "arbitrary"),
        cost_estimate=lasting(13),
        name="mixer_forward",
    )(near(pre), taps, head, skip, spread)


def mixer_backward(pre, conv, dy, kept, taps, head, skip, spread):
    length, columns = pre.shape
    both = taps.shape[1]
    inner = skip.shape[1]
    steps = length // SPAN
    last = steps - 1
    return pl.pallas_call(
        backward_kernel,
        grid=(steps,),
        in_specs=[
            pl.BlockSpec((SPAN, columns), lambda i: (last - i, 0)),
            pl.BlockSpec((SPAN, both), lambda i: (last - i, 0)),
            pl.BlockSpec((SPAN, inner), lambda i: (last - i, 0)),
            pl.BlockSpec((128, inner), lambda i: (last - i, 0)),
            whole(taps.shape), whole(head.shape), whole(skip.shape), whole(spread.shape),
        ],
        out_specs=[
            pl.BlockSpec((SPAN, columns), lambda i: (last - i, 0)),
            whole((8, both)),
            whole((8, 128)),
        ],
        out_shape=[
            held_near((length, columns), BF),
            shape_of((8, both), F32),
            shape_of((8, 128), F32),
        ],
        scratch_shapes=[
            pltpu.VMEM((SPAN + 8, both), F32),
            pltpu.VMEM((128, inner), F32),
            pltpu.VMEM((8, inner), F32),
        ],
        compiler_params=params(24, "arbitrary"),
        cost_estimate=lasting(30),
        name="mixer_backward",
    )(far(pre), far(conv), far(dy), far(kept), taps, head, skip, spread)


CELLS = [(xh, xl, core) for xh in range(2) for xl in range(2) for core in range(2)]
TURNS = [(a, b) for a in range(2) for b in range(2)]


def moves(rule):
    return [(4 * c[0] + 2 * c[1] + c[2], 4 * d[0] + 2 * d[1] + d[2]) for c in CELLS for d in [rule(*c)]]


def permute(value, rule):
    return lax.ppermute(value, GROUP, moves(rule))


def trade(value):
    return permute(
        value, lambda xh, xl, core: (xh, xl, core) if xh == core else (1 - xh, xl, 1 - core)
    )


def swap_core(value):
    return lax.ppermute(value, "core", [(0, 1), (1, 0)])


def to_workers(value):
    return [
        permute(value, lambda xh, xl, core, a=a, b=b: (core ^ a, xl ^ b, xh)) for a, b in TURNS
    ]


def to_owners(blocks):
    return [
        permute(block, lambda xh, xl, core, a=a, b=b: (core, xl ^ b, xh ^ a))
        for block, (a, b) in zip(blocks, TURNS)
    ]


def around(value):
    return [value] + [
        permute(value, lambda xh, xl, core, a=a, b=b: (xh ^ a, xl ^ b, core)) for a, b in TURNS[1:]
    ]


def gather_plane(shard):
    count = lax.axis_size(PLANE)
    spread = jnp.broadcast_to(shard[None], (count,) + shard.shape)
    got = lax.all_to_all(spread, PLANE, 0, 0, tiled=True)
    return got.reshape((count * shard.shape[0],) + shard.shape[1:])


def exchange(blocks):
    return lax.all_to_all(blocks, PLANE, 0, 0, tiled=True)


def after(*values):
    return lax.optimization_barrier(values)


def on_device(
    hidden_in,
    cotangent,
    norm_gain,
    w_z,
    w_x,
    w_bc,
    w_dt,
    conv_x,
    conv_bc,
    head_params,
    gate_gain,
    w_out,
):
    block, wide = w_x.shape
    states = w_bc.shape[1]
    heads = w_dt.shape[1]
    both = wide + states
    xh, xl, core = (lax.axis_index(axis) for axis in GROUP)
    meta = jnp.stack([(xl ^ b) * 2 + (xh ^ a) for a, b in TURNS] + [core, xh]).astype(jnp.int32)
    gain = norm_gain[None]

    weights = trade(pack(w_z, w_out.T, w_x, w_bc, w_dt.T))
    small = jnp.concatenate(
        [conv_x, gate_gain[None], jnp.pad(head_params, ((0, 0), (0, wide - heads)))[:2]]
    )
    small = jnp.concatenate([small, jnp.pad(head_params[2:], ((0, 7), (0, wide - heads)))])
    small, weights = after(small, weights)
    small = jnp.where(core == xh, small, swap_core(small))

    mine = gather_plane(weights)
    hidden, weights = after(hidden_in, weights)
    hidden_blocks = to_workers(hidden)
    conv_x, gate_row, head_params = small[:5], small[5:6], small[6:9, :heads]
    taps, head, skip, spread = mixer_tables(conv_x, conv_bc, head_params)
    first_half, cot, taps, head, skip, spread, gate_row, meta, gain = after(
        hidden_blocks[:2], cotangent, taps, head, skip, spread, gate_row, meta, gain
    )
    hidden_blocks = first_half + hidden_blocks[2:]
    cot_blocks = to_workers(cot)
    tokens, tokens_t = place(meta, gain, hidden_blocks, True)
    tokens, mine, cot_first = after(tokens, mine, cot_blocks[0])
    cot_blocks = [cot_first] + cot_blocks[1:]
    other = swap_core(mine)

    pre, z = project(tokens, mine, other, wide)
    y, kept, conv = mixer_forward(pre, taps, head, skip, spread)
    y, cot_blocks = after(y, cot_blocks)
    cot, cot_t = place(meta, gain, cot_blocks, False)
    dy, sums = gate_sums(cot, mine, other, y, z, gate_row)
    normed_y, gate, dscan, gain_grad, keep, send = gate_back(
        block, 4.0 * wide, around(sums), z, dy, y, gate_row, tokens_t, cot_t
    )

    early = (keep.astype(F32) + swap_core(send).astype(F32)).astype(BF)
    out_blocks = project_out(meta, normed_y, mine, other)
    dscan, early, out_blocks = after(dscan, early, out_blocks)
    early = exchange(early)
    out_blocks = to_owners(out_blocks)
    late, conv_grad, head_grad = mixer_backward(pre, conv, dscan, kept, taps, head, skip, spread)
    *back_blocks, norm_part = project_back(
        meta, late, gate, mine, other, mine, other, tokens, gain
    )
    late, back_blocks, out_blocks = after(late, back_blocks, out_blocks)
    back_blocks = to_owners(back_blocks)

    rest = jnp.pad(
        jnp.concatenate([norm_part[:1, :wide], norm_part[:1, wide:], gain_grad[:1]]),
        ((0, 0), (0, states)),
    )
    vector = jnp.concatenate([jnp.concatenate([conv_grad[:5], rest]), head_grad], axis=1)
    vector = jnp.pad(vector, ((0, 8), (0, 0)))
    keep, send = weight_grad(tokens_t, late, vector)
    send, early, back_first = after(send, early, back_blocks[0])
    output = finish_output(meta, out_blocks, hidden_in)
    got = swap_core(send).astype(F32)
    half = keep.shape[0]
    late_sum = (keep + got[:half]).astype(BF).reshape(-1, block, both + 128)
    vector = (vector[:8] + got[half : half + 8]).astype(BF)
    vector = jnp.broadcast_to(vector[None], (late_sum.shape[0],) + vector.shape)
    late_sum = jnp.concatenate([late_sum, vector], axis=1)
    back_blocks = [back_first] + back_blocks[1:]
    early = trade(early.astype(F32).sum(axis=0))
    got, early, output = after(exchange(late_sum), early, output)
    own, shared = total_of(got, states)
    own, back_blocks = after(own, back_blocks)
    own = trade(own)

    shared = [
        permute(shared, lambda xh, xl, core, a=a, b=b: (core, xl ^ b, xh ^ a)) for a, b in TURNS
    ]
    input_grad = finish_input(meta, back_blocks, hidden_in, cotangent, gain)
    norm_grad, x_grad, bc_grad, dt_grad, conv_x_grad, conv_bc_grad, head_part, gate_part = deliver(
        own, shared, block, heads
    )
    return (
        output,
        input_grad,
        norm_grad,
        early[0],
        x_grad,
        bc_grad,
        dt_grad.T,
        conv_x_grad,
        conv_bc_grad,
        head_part,
        gate_part,
        early[1].T,
    )


def solution(mesh):
    fine = Mesh(mesh.devices.reshape(2, 4, 4, 2, 2), AXES)
    rows, both, lanes = P(AXES, None), P(DP, TN), P(None, TN)
    return jax.shard_map(
        on_device,
        mesh=fine,
        in_specs=(rows, rows, P(), both, both, P(DP, None), both, lanes, P(), lanes, P(TN), P(TN, DP)),
        out_specs=(
            rows, rows, P(), both, both, P(DP, None), both, lanes, P(), lanes, P(TN), P(TN, DP)
        ),
        check_vma=False,
    )
```

```python
import functools
import jax
import jax.numpy as jnp
from jax import lax
from jax.experimental import pallas as pl
from jax.experimental.pallas import tpu as pltpu
from jax.sharding import Mesh, PartitionSpec as P

EPS = 1e-05
AXES = ("xh", "y", "z", "xl", "core")
DP = ("xh", "y", "z")
TN = ("xl", "core")
GROUP = ("xh", "xl", "core")
PLANE = ("y", "z")
BF = jnp.bfloat16
F32 = jnp.float32
SPAN = 128
LIMIT = 36


def near(value):
    return pltpu.with_memory_space_constraint(value, pltpu.VMEM)


def far(value):
    return pltpu.with_memory_space_constraint(value, pltpu.HBM)


ROWS = 512
SCALE = 1.15e9


def nn(left, right):
    return lax.dot_general(left, right, (((1,), (0,)), ((), ())), preferred_element_type=F32)


def nt(left, right):
    return lax.dot_general(left, right, (((1,), (1,)), ((), ())), preferred_element_type=F32)


def halves(value):
    high = value.astype(BF)
    low = (value - high.astype(F32)).astype(BF)
    return high, low


def running(mask, value):
    high, low = halves(value)
    return nn(jnp.concatenate([mask, mask], axis=1), jnp.concatenate([high, low], axis=0))


def close_nt(left, right):
    left_high, left_low = halves(left)
    right_high, right_low = halves(right)
    return nt(
        jnp.concatenate([left_high, left_high, left_low], axis=1),
        jnp.concatenate([right_high, right_low, right_high], axis=1),
    )


def expand(value, spread):
    high, low = halves(value)
    return nn(jnp.concatenate([high, low], axis=1), spread)


def by_head(value, spread):
    width = spread.shape[0] // 2
    high, low = halves(value)
    return nt(high, spread[:width]) + nt(low, spread[:width])


def logistic(value):
    return 1.0 / (1.0 + jnp.exp(-value))


def sigmoid(value):
    return 0.5 * jnp.tanh(0.5 * value) + 0.5


def softplus(value):
    return jnp.maximum(value, 0.0) + jnp.log1p(jnp.exp(-jnp.abs(value)))


def conv_rows(ext_ref, taps):
    total = taps[4:5] + ext_ref[5 : 5 + SPAN] * taps[0:1]
    for k in range(1, 4):
        total = total + ext_ref[5 + k : 5 + k + SPAN] * taps[k : k + 1]
    return total


def scan_parts(conv, pre_dt, head, spread, tri):
    sig = sigmoid(conv)
    xbc = conv * sig
    raw = pre_dt + head[1:2]
    step = softplus(raw)
    decay = running(tri, step * head[0:1])
    last = decay[SPAN - 1 : SPAN]
    grown = expand(jnp.concatenate([step, jnp.exp(decay), jnp.exp(last - decay)], axis=0), spread)
    step_x, start_x, end_x = grown[:SPAN], grown[SPAN : 2 * SPAN], grown[2 * SPAN :]
    return sig, xbc, raw, step, decay, step_x, start_x, end_x


def forward_kernel(
    pre_ref, taps_ref, head_ref, skip_ref, spread_ref, y_ref, kept_ref, conv_ref, ext_ref, state_ref
):
    inner = y_ref.shape[1]
    both = ext_ref.shape[1]

    @pl.when(pl.program_id(0) == 0)
    def _():
        ext_ref[0:8] = jnp.zeros((8, both), F32)
        state_ref[...] = jnp.zeros_like(state_ref)

    ext_ref[8 : 8 + SPAN] = pre_ref[:, :both]
    rows = lax.broadcasted_iota(jnp.int32, (SPAN, SPAN), 0)
    cols = lax.broadcasted_iota(jnp.int32, (SPAN, SPAN), 1)
    keep = rows >= cols
    tri = jnp.where(keep, 1.0, 0.0).astype(BF)
    spread = spread_ref[...]
    conv = conv_rows(ext_ref, taps_ref[...])
    conv_ref[...] = conv
    sig, xbc, raw, step, decay, step_x, start_x, end_x = scan_parts(
        conv, pre_ref[:, both:], head_ref[...], spread, tri
    )
    ext_ref[0:8] = ext_ref[SPAN : SPAN + 8]
    state_width = (both - inner) // 2
    x = xbc[:, :inner]
    b = xbc[:, inner : inner + state_width]
    c = xbc[:, inner + state_width :]
    decay_t = decay.T
    scaled = x * step_x
    low = scaled.astype(BF)
    scores = close_nt(c, b)
    state = state_ref[...]
    state_low = state.astype(BF)
    kept_ref[...] = state_low
    carried = nn(c.astype(BF), state_low) * start_x + x * skip_ref[...]
    left = cols < 64
    for pair in range(inner // 128):
        at = slice(128 * pair, 128 * pair + 128)
        x_pair = low[:, at]
        found = []
        for h in (2 * pair, 2 * pair + 1):
            gap = decay[:, h : h + 1] - decay_t[h : h + 1]
            weight = jnp.exp(jnp.where(keep, gap, -1e30)) * scores
            found.append(nn(weight.astype(BF), x_pair))
        y_ref[:, at] = jnp.where(left, found[0], found[1]) + carried[:, at]
    state_ref[...] = state * start_x[SPAN - 1 : SPAN] + nn(
        b.T.astype(BF), (scaled * end_x).astype(BF)
    )


def backward_kernel(
    pre_ref, conv_ref, dy_ref, kept_ref, taps_ref, head_ref, skip_ref, spread_ref,
    late_ref, conv_grad_ref, head_grad_ref,
    dext_ref, dstate_ref, skip_sum_ref,
):
    inner = dy_ref.shape[1]
    both = dext_ref.shape[1]
    steps = pl.num_programs(0)
    at_step = pl.program_id(0)

    @pl.when(at_step == 0)
    def _():
        dext_ref[SPAN : SPAN + 8] = jnp.zeros((8, both), F32)
        dstate_ref[...] = jnp.zeros_like(dstate_ref)
        skip_sum_ref[...] = jnp.zeros_like(skip_sum_ref)
        conv_grad_ref[...] = jnp.zeros_like(conv_grad_ref)
        head_grad_ref[...] = jnp.zeros_like(head_grad_ref)

    rows = lax.broadcasted_iota(jnp.int32, (SPAN, SPAN), 0)
    cols = lax.broadcasted_iota(jnp.int32, (SPAN, SPAN), 1)
    tri = jnp.where(rows >= cols, 1.0, 0.0).astype(BF)
    upper = jnp.where(cols >= rows, 1.0, 0.0).astype(BF)
    keep = cols >= rows
    spread = spread_ref[...]
    taps = taps_ref[...]
    head = head_ref[...]
    conv = conv_ref[...]
    sig, xbc, raw, step, decay, step_x, start_x, end_x = scan_parts(
        conv, pre_ref[:, both:], head, spread, tri
    )
    state_width = (both - inner) // 2
    x = xbc[:, :inner]
    b = xbc[:, inner : inner + state_width]
    c = xbc[:, inner + state_width :]
    b_low, c_low = b.astype(BF), c.astype(BF)
    decay_t = decay.T
    scaled = x * step_x
    low = scaled.astype(BF)
    scores = close_nt(b, c)
    dy = dy_ref[...].astype(F32)
    dy_low = dy.astype(BF)
    kept = kept_ref[...]
    dstate = dstate_ref[...]
    dstate_low = dstate.astype(BF)
    left = cols < 64
    wide_rows = lax.broadcasted_iota(jnp.int32, (SPAN, SPAN), 0)
    d_scores = jnp.zeros((SPAN, SPAN), F32)
    into = jnp.zeros((SPAN, SPAN), F32)
    out_of = jnp.zeros((SPAN, SPAN), F32)
    pieces = []
    none = jnp.zeros((SPAN, 128), BF)
    for pair in range(inner // 128):
        at = slice(128 * pair, 128 * pair + 128)
        x_pair = low[:, at]
        dy_pair = dy_low[:, at]
        found = []
        for side, h in enumerate((2 * pair, 2 * pair + 1)):
            gap = decay_t[h : h + 1] - decay[:, h : h + 1]
            fall = jnp.exp(jnp.where(keep, gap, -1e30))
            mine = jnp.where(left if side == 0 else ~left, dy_pair, none)
            back = nt(x_pair, mine) * fall
            d_scores = d_scores + back
            both_ways = back * scores
            into = jnp.where(wide_rows == h, jnp.sum(both_ways, axis=0, keepdims=True), into)
            out_of = jnp.where(cols == h, jnp.sum(both_ways, axis=1, keepdims=True), out_of)
            found.append(nn((fall * scores).astype(BF), dy_pair))
        pieces.append(jnp.where(left, found[0], found[1]))
    inside = jnp.concatenate(pieces, axis=1)
    dy_start = dy * start_x
    dy_start_low = dy_start.astype(BF)
    from_state = nn(c_low, kept)
    scaled_end = scaled * end_x
    d_end = nn(b_low, dstate_low)
    d_scaled = inside + d_end * end_x
    pair_start = by_head(dy_start * from_state, spread)
    pair_end = by_head(scaled_end * d_end, spread)
    d_scores_low = d_scores.astype(BF)
    d_c = nn(d_scores.T.astype(BF), b_low) + nt(dy_start_low, kept)
    d_b = nn(d_scores_low, c_low) + nt(scaled_end.astype(BF), dstate_low)
    through = jnp.sum(kept.astype(F32) * dstate, axis=0, keepdims=True)
    through = by_head(jnp.broadcast_to(through * start_x[SPAN - 1 : SPAN], (8, inner)), spread)[0:1]
    at_end = jnp.sum(pair_end, axis=0, keepdims=True) + through
    d_decay = into.T - out_of + pair_start - pair_end
    d_decay = d_decay + jnp.where(rows == SPAN - 1, at_end, 0.0)
    d_log = running(upper, d_decay)
    d_step = by_head(d_scaled * x, spread) + d_log * head[0:1]
    d_raw = d_step * logistic(raw)
    dstate_ref[...] = dstate * start_x[SPAN - 1 : SPAN] + nn(c.T.astype(BF), dy_start_low)
    late_ref[:, both:] = d_raw.astype(BF)
    head_grad_ref[0:1] += jnp.sum(d_log * step, axis=0, keepdims=True) * head[0:1]
    head_grad_ref[1:2] += jnp.sum(d_raw, axis=0, keepdims=True)
    skip_sum_ref[0:1] += jnp.sum(dy * x, axis=0, keepdims=True)
    dx = d_scaled * step_x + dy * skip_ref[...]
    d_conv = jnp.concatenate([dx, d_b, d_c], axis=1) * (sig * (1.0 + conv * (1.0 - sig)))
    dext_ref[0:SPAN] = d_conv
    values = pre_ref[:, :both]
    d_pre = d_conv * taps[3:4]
    conv_grad_ref[3:4] += jnp.sum(d_conv * values, axis=0, keepdims=True)
    for k in range(3):
        moved = dext_ref[3 - k : 3 - k + SPAN]
        d_pre = d_pre + moved * taps[k : k + 1]
        conv_grad_ref[k : k + 1] += jnp.sum(moved * values, axis=0, keepdims=True)
    conv_grad_ref[4:5] += jnp.sum(d_conv, axis=0, keepdims=True)
    dext_ref[SPAN : SPAN + 8] = dext_ref[0:8]
    late_ref[:, :both] = d_pre.astype(BF)

    @pl.when(at_step == steps - 1)
    def _():
        head_grad_ref[2:3] += by_head(
            jnp.broadcast_to(skip_sum_ref[0:1], (8, inner)), spread
        )[0:1]


def whole(shape):
    return pl.BlockSpec(shape, lambda *_: (0,) * len(shape))


def column(rows, width, shift=0):
    return pl.BlockSpec((rows, width), lambda j, *_: (0, j + shift))


def shape_of(shape, dtype):
    return jax.ShapeDtypeStruct(shape, dtype)


def stored(shape, dtype):
    return pltpu.HBM(shape, dtype)


def held_near(shape, dtype):
    return pltpu.VMEM(shape, dtype)


def params(limit, *semantics):
    return pltpu.CompilerParams(
        dimension_semantics=semantics or None, vmem_limit_bytes=LIMIT * 1024 * 1024
    )


def lasting(us):
    return pl.CostEstimate(flops=int(us * SCALE), bytes_accessed=1024, transcendentals=0)


def place_kernel(normalise, meta_ref, gain_ref, *refs):
    blocks, out_ref, flip_ref = refs[:4], refs[4], refs[5]
    rows, width = blocks[0].shape
    half = width // 2
    core = meta_ref[4]
    first = pl.multiple_of(core * half, 128)
    second = pl.multiple_of((1 - core) * half, 128)
    for k, block in enumerate(blocks):
        at = pl.multiple_of(meta_ref[k] * rows, rows)
        value = block[...].astype(F32)
        if normalise:
            scale = lax.rsqrt(jnp.mean(value * value, axis=1, keepdims=True) + EPS)
            value = value * scale * gain_ref[...]
        low = value.astype(BF)
        out_ref[pl.ds(at, rows), pl.ds(first, half)] = low[:, :half]
        out_ref[pl.ds(at, rows), pl.ds(second, half)] = low[:, half:]
        flip = value.T.astype(BF)
        flip_ref[pl.ds(first, half), pl.ds(at, rows)] = flip[:half]
        flip_ref[pl.ds(second, half), pl.ds(at, rows)] = flip[half:]


def place(meta, gain, blocks, normalise):
    rows, width = blocks[0].shape
    vmem = pl.BlockSpec()
    return pl.pallas_call(
        functools.partial(place_kernel, normalise),
        in_specs=[pl.BlockSpec(memory_space=pltpu.SMEM)] + [vmem] * 5,
        out_specs=[vmem, vmem],
        out_shape=[
            (stored if normalise else shape_of)((4 * rows, width), BF),
            shape_of((width, 4 * rows), BF),
        ],
        compiler_params=params(24),
        cost_estimate=lasting(6),
        name="place_normed" if normalise else "place_cotangent",
    )(meta, gain, *[far(block) for block in blocks])


def project_kernel(tokens_ref, xm_ref, xo_ref, zm_ref, zo_ref, pre_ref, z_ref):
    half = xm_ref.shape[0]
    for first, second, out in ((xm_ref, xo_ref, pre_ref), (zm_ref, zo_ref, z_ref)):
        out[...] = nn(tokens_ref[:, :half], first[...]) + nn(tokens_ref[:, half:], second[...])


def project(tokens, mine, other, inner):
    half = mine.shape[0]
    length = tokens.shape[0]
    columns = mine.shape[1] - 2 * inner
    rows = ROWS

    def part(width, shift):
        return pl.BlockSpec(
            (pl.Element(half), pl.Element(width)),
            lambda i: (0, shift),
            pipeline_mode=pl.Buffered(1),
        )

    return pl.pallas_call(
        project_kernel,
        grid=(length // rows,),
        in_specs=[pl.BlockSpec((rows, 2 * half), lambda i: (i, 0))]
        + [part(columns, 2 * inner)] * 2
        + [part(inner, 0)] * 2,
        out_specs=[
            pl.BlockSpec((rows, columns), lambda i: (i, 0)),
            pl.BlockSpec((rows, inner), lambda i: (i, 0)),
        ],
        out_shape=[shape_of((length, columns), F32), shape_of((length, inner), F32)],
        compiler_params=params(20, "arbitrary"),
        cost_estimate=lasting(6),
        name="project_in",
    )(far(tokens), far(mine), other, far(mine), other)


def gate_sums_kernel(
    cot_ref, om_ref, oo_ref, y_ref, z_ref, gain_ref, dy_ref, sums_ref
):
    half = om_ref.shape[0]
    z = z_ref[...]
    dy = nn(cot_ref[:, :half], om_ref[...]) + nn(cot_ref[:, half:], oo_ref[...])
    dy_ref[...] = dy
    gated = y_ref[...] * (z * sigmoid(z))
    ones = jnp.ones((8, z.shape[1]), BF)
    found = []
    for value in (gated * gated, gated * (dy * gain_ref[...])):
        high, low = halves(value)
        found.append(nt(ones, high) + nt(ones, low))
    row = lax.broadcasted_iota(jnp.int32, found[0].shape, 0)
    total = jnp.where(row == 0, found[0], found[1])

    @pl.when(pl.program_id(0) == 0)
    def _():
        sums_ref[...] = total

    @pl.when(pl.program_id(0) > 0)
    def _():
        sums_ref[...] += total


def gate_sums(cot, mine, other, y, z, gain):
    length, inner = y.shape
    half = mine.shape[0]
    tile = 256
    steps = inner // tile
    return pl.pallas_call(
        gate_sums_kernel,
        grid=(steps,),
        in_specs=[
            whole(cot.shape),
            column(half, tile, steps),
            column(half, tile, steps),
            column(length, tile),
            column(length, tile),
            column(1, tile),
        ],
        out_specs=[column(length, tile), whole((8, length))],
        out_shape=[shape_of((length, inner), F32), shape_of((8, length), F32)],
        compiler_params=params(36, "arbitrary"),
        cost_estimate=lasting(6),
        name="gate_sums",
    )(near(cot), far(mine), far(other), near(y), near(z), gain)


def gate_back_kernel(
    width_all, s0, s1, s2, s3, z_ref, dy_ref, y_ref, gain_ref, tokens_t_ref, cot_t_ref,
    normed_ref, gate_ref, dscan_ref, gain_grad_ref, keep_ref, send_ref,
):
    sums = (s0[...] + s1[...]) + (s2[...] + s3[...])
    flat = sums.T
    rms = lax.rsqrt(flat[:, 0:1] / width_all + EPS)
    inner = flat[:, 1:2] * (rms * rms * rms / width_all)
    z = z_ref[...]
    y = y_ref[...]
    dy = dy_ref[...]
    gain = gain_ref[...]
    sig = sigmoid(z)
    act = z * sig
    gated = y * act
    unit = gated * rms
    normed = (unit * gain).astype(BF)
    normed_ref[...] = normed
    gain_grad_ref[...] = jnp.broadcast_to(
        jnp.sum(dy * unit, axis=0, keepdims=True), gain_grad_ref.shape
    )
    d_gated = rms * (dy * gain) - gated * inner
    dscan_ref[...] = d_gated * act
    gate = (d_gated * y * (sig * (1.0 + z * (1.0 - sig)))).astype(BF)
    gate_ref[...] = gate
    half = tokens_t_ref.shape[0] // 2
    for side, (left, right) in enumerate(((tokens_t_ref, gate), (cot_t_ref, normed))):
        for out, at in ((keep_ref, slice(0, half)), (send_ref, slice(half, 2 * half))):
            found = nn(left[at], right).astype(BF)
            out[:, side] = found.reshape(out.shape[0], out.shape[2], found.shape[1])


def gate_back(block, width_all, sums, z, dy, y, gain, tokens_t, cot_t):
    length, inner = y.shape
    half = tokens_t.shape[0] // 2
    tile = 256
    pile = pl.BlockSpec((half // block, 2, block, tile), lambda j: (0, 0, 0, j))
    return pl.pallas_call(
        functools.partial(gate_back_kernel, width_all),
        grid=(inner // tile,),
        in_specs=[whole((8, length))] * 4
        + [column(length, tile)] * 3
        + [column(1, tile), whole(tokens_t.shape), whole(cot_t.shape)],
        out_specs=[column(length, tile)] * 3 + [column(8, tile), pile, pile],
        out_shape=[
            stored((length, inner), BF),
            stored((length, inner), BF),
            stored((length, inner), F32),
            shape_of((8, inner), F32),
            shape_of((half // block, 2, block, inner), BF),
            shape_of((half // block, 2, block, inner), BF),
        ],
        compiler_params=params(44, "arbitrary"),
        cost_estimate=lasting(12),
        name="gate_back",
    )(*sums, near(z), near(dy), near(y), gain, near(tokens_t), near(cot_t))


def scatter_rows(meta_ref, found, scratch, outs):
    rows = outs[0].shape[0]
    scratch[...] = found
    for k, out in enumerate(outs):
        out[...] = scratch[pl.ds(pl.multiple_of(meta_ref[k] * rows, rows), rows), :].astype(BF)


def project_out_kernel(meta_ref, normed_ref, om_ref, oo_ref, *refs):
    outs, scratch = refs[:4], refs[4]

    def step(right):
        scatter_rows(meta_ref, nt(normed_ref[...], right[...]), scratch, outs)

    first = pl.program_id(0) < pl.num_programs(0) // 2
    pl.when(first)(lambda: step(om_ref))
    pl.when(jnp.logical_not(first))(lambda: step(oo_ref))


def sides(tile, columns, shift, per):
    return [
        pl.BlockSpec(
            (pl.Element(tile), pl.Element(columns)),
            lambda j: (jnp.minimum(j, per - 1) * tile, shift),
        ),
        pl.BlockSpec(
            (pl.Element(tile), pl.Element(columns)),
            lambda j: (jnp.maximum(j - per, 0) * tile, shift),
        ),
    ]


def project_out(meta, normed_y, mine, other):
    length, inner = normed_y.shape
    half = mine.shape[0]
    rows = length // 4
    per = 3
    tile = half // per
    return pl.pallas_call(
        project_out_kernel,
        grid=(2 * per,),
        in_specs=[pl.BlockSpec(memory_space=pltpu.SMEM), whole(normed_y.shape)]
        + sides(tile, inner, inner, per),
        out_specs=[column(rows, tile)] * 4,
        out_shape=[stored((rows, 2 * half), BF)] * 4,
        scratch_shapes=[pltpu.VMEM((length, tile), F32)],
        compiler_params=params(24, "arbitrary"),
        cost_estimate=lasting(6),
        name="project_out",
    )(meta, far(normed_y), far(mine), far(other))


def project_back_kernel(
    meta_ref, late_ref, gate_ref, xm_ref, xo_ref, zm_ref, zo_ref, tokens_ref, gain_ref, *refs
):
    outs, grad_ref, scratch = refs[:4], refs[4], refs[5]
    tile = scratch.shape[1]
    j = pl.program_id(0)
    per = pl.num_programs(0) // 2
    side, within = j // per, j % per
    core = meta_ref[4]

    def step(x_ref, z_ref):
        found = nt(late_ref[...], x_ref[...]) + nt(gate_ref[...], z_ref[...])
        total = jnp.sum(found * tokens_ref[...].astype(F32), axis=0, keepdims=True)
        owner = side + core - 2 * side * core
        place = pl.ds(pl.multiple_of((per * owner + within) * tile, 128), tile)
        grad_ref[:, place] = jnp.broadcast_to(total / gain_ref[:, place], (8, tile))
        scatter_rows(meta_ref, found, scratch, outs)

    pl.when(side == 0)(lambda: step(xm_ref, zm_ref))
    pl.when(side == 1)(lambda: step(xo_ref, zo_ref))


def project_back(meta, late, gate, mine1, other1, mine2, other2, tokens, gain):
    length, columns = late.shape
    inner = gate.shape[1]
    half = mine1.shape[0]
    rows = length // 4
    per = 3
    tile = half // per
    return pl.pallas_call(
        project_back_kernel,
        grid=(2 * per,),
        in_specs=[pl.BlockSpec(memory_space=pltpu.SMEM), whole(late.shape), whole(gate.shape)]
        + sides(tile, columns, 2 * inner, per)
        + sides(tile, inner, 0, per)
        + [column(length, tile), whole(gain.shape)],
        out_specs=[column(rows, tile)] * 4 + [whole((8, 2 * half))],
        out_shape=[stored((rows, 2 * half), BF)] * 4 + [shape_of((8, 2 * half), F32)],
        scratch_shapes=[pltpu.VMEM((length, tile), F32)],
        compiler_params=params(32, "arbitrary"),
        cost_estimate=lasting(0.5),
        name="project_back",
    )(
        meta, near(late), far(gate), far(mine1), far(other1), far(mine2), far(other2), far(tokens), gain
    )


def weight_grad_kernel(tokens_t_ref, late_ref, vector_ref, keep_ref, send_ref):
    half = keep_ref.shape[0]
    late = late_ref[...]
    keep_ref[...] = nn(tokens_t_ref[:half], late)
    send_ref[:half] = nn(tokens_t_ref[half:], late).astype(BF)
    send_ref[half:] = vector_ref[...].astype(BF)


def weight_grad(tokens_t, late, vector):
    length, columns = late.shape
    half = tokens_t.shape[0] // 2
    rows = half + vector.shape[0]
    tile = 384
    return pl.pallas_call(
        weight_grad_kernel,
        grid=(columns // tile,),
        in_specs=[whole(tokens_t.shape), column(length, tile), column(vector.shape[0], tile)],
        out_specs=[column(half, tile), column(rows, tile)],
        out_shape=[stored((half, columns), F32), stored((rows, columns), BF)],
        compiler_params=params(24, "arbitrary"),
        cost_estimate=lasting(0.5),
        name="weight_grad",
    )(far(tokens_t), near(late), vector)


def pack_kernel(z_ref, out_ref, x_ref, bc_ref, dt_ref, packed_ref):
    at = 0
    for ref in (z_ref, out_ref, x_ref, bc_ref):
        packed_ref[:, at : at + ref.shape[1]] = ref[...]
        at += ref.shape[1]
    heads, rows = dt_ref.shape
    tall = jnp.concatenate([dt_ref[...].astype(F32), jnp.zeros((128 - heads, rows), F32)], axis=0)
    packed_ref[:, at:] = tall.T.astype(BF)


def pack(*parts):
    vmem = pl.BlockSpec()
    return pl.pallas_call(
        pack_kernel,
        in_specs=[vmem] * 5,
        out_specs=vmem,
        out_shape=shape_of(
            (parts[0].shape[0], sum(part.shape[1] for part in parts[:4]) + 128), BF
        ),
        compiler_params=params(8),
        cost_estimate=lasting(1),
        name="pack_weights",
    )(*[far(part) for part in parts])


def total_kernel(states, got_ref, own_ref, shared_ref):
    total = jnp.sum(got_ref[...].astype(F32), axis=0)
    rows = total.shape[0]
    inner = own_ref.shape[1] - 128
    both = inner + states
    own_ref[:, :inner] = total[:, :inner]
    own_ref[:, inner:] = total[:, both:]
    shared_ref[:rows] = total[:, inner:both]
    per = inner // states
    for k in range(2 * per):
        line = rows - 3 + k // per
        at = states * (k % per)
        shared_ref[rows + k : rows + k + 1] = total[line : line + 1, at : at + states]


def total_of(got, states):
    count, rows, columns = got.shape
    vmem = pl.BlockSpec()
    extra = rows + 2 * ((columns - states - 128) // states)
    return pl.pallas_call(
        functools.partial(total_kernel, states),
        in_specs=[vmem],
        out_specs=[vmem, vmem],
        out_shape=[shape_of((rows, columns - states), F32), shape_of((extra, states), F32)],
        compiler_params=params(16),
        cost_estimate=lasting(3),
        name="late_total",
    )(got)


def deliver_kernel(
    own_ref, s0, s1, s2, s3,
    norm_ref, x_ref, bc_ref, dt_ref, conv_x_ref, conv_bc_ref, head_ref, gate_ref,
):
    shared = (s0[...] + s1[...]) + (s2[...] + s3[...])
    own = own_ref[...]
    block, inner = x_ref.shape
    heads = dt_ref.shape[0]
    x_ref[...] = own[:block, :inner]
    dt_ref[...] = own[:block, inner:].T[:heads]
    conv_x_ref[...] = own[block : block + 5, :inner]
    head_ref[...] = own[block : block + 3, inner : inner + heads]
    gate_ref[...] = own[block + 7, :inner]
    bc_ref[...] = shared[:block]
    conv_bc_ref[...] = shared[block : block + 5]
    states = bc_ref.shape[1]
    for k in range(norm_ref.shape[0] // states):
        norm_ref[states * k : states * k + states] = shared[block + 8 + k]


def deliver(own, shared, block, heads):
    vmem = pl.BlockSpec()
    inner = own.shape[1] - 128
    states = shared[0].shape[1]
    shapes = [
        (2 * inner,), (block, inner), (block, states), (heads, block),
        (5, inner), (5, states), (3, heads), (inner,),
    ]
    return pl.pallas_call(
        deliver_kernel,
        in_specs=[vmem] * 5,
        out_specs=[vmem] * 8,
        out_shape=[shape_of(shape, F32) for shape in shapes],
        compiler_params=params(16),
        cost_estimate=lasting(2),
        name="deliver_late",
    )(own, *shared)


def owner_total(xh_ref, blocks):
    total = sum(block[...].astype(F32) for block in blocks)
    half = total.shape[1] // 2
    turned = jnp.concatenate([total[:, half:], total[:, :half]], axis=1)
    return jnp.where(xh_ref[5] == 0, total, turned)


def output_kernel(meta_ref, b0, b1, b2, b3, hidden_ref, out_ref):
    mixed = owner_total(meta_ref, (b0, b1, b2, b3))
    out_ref[...] = (hidden_ref[...].astype(F32) + mixed).astype(BF)


def finish_output(meta, blocks, hidden):
    vmem = pl.BlockSpec()
    return pl.pallas_call(
        output_kernel,
        in_specs=[pl.BlockSpec(memory_space=pltpu.SMEM)] + [vmem] * 5,
        out_specs=vmem,
        out_shape=shape_of(hidden.shape, BF),
        compiler_params=params(16),
        cost_estimate=lasting(3),
        name="finish_output",
    )(meta, *[far(block) for block in blocks], far(hidden))


def input_kernel(meta_ref, b0, b1, b2, b3, hidden_ref, cot_ref, gain_ref, out_ref):
    scaled = owner_total(meta_ref, (b0, b1, b2, b3)) * gain_ref[...]
    resid = hidden_ref[...].astype(F32)
    inv = lax.rsqrt(jnp.mean(resid * resid, axis=1, keepdims=True) + EPS)
    along = jnp.mean(resid * scaled, axis=1, keepdims=True) * (inv * inv * inv)
    out_ref[...] = inv * scaled - resid * along + cot_ref[...].astype(F32)


def finish_input(meta, blocks, hidden, cot, gain):
    vmem = pl.BlockSpec()
    return pl.pallas_call(
        input_kernel,
        in_specs=[pl.BlockSpec(memory_space=pltpu.SMEM)] + [vmem] * 7,
        out_specs=vmem,
        out_shape=shape_of(hidden.shape, F32),
        compiler_params=params(16),
        cost_estimate=lasting(3),
        name="finish_input",
    )(meta, *blocks, far(hidden), far(cot), gain)


def mixer_tables(conv_x, conv_bc, head_params):
    heads = head_params.shape[1]
    inner = conv_x.shape[1]
    taps = jnp.pad(jnp.concatenate([conv_x, conv_bc], axis=1), ((0, 3), (0, 0)))
    head = jnp.stack([-jnp.exp(head_params[0]), head_params[1]])
    head = jnp.pad(head, ((0, 6), (0, 128 - heads)))
    skip = jnp.repeat(head_params[2], inner // heads)[None]
    owner = lax.broadcasted_iota(jnp.int32, (256, inner), 1) // (inner // heads)
    one = owner == lax.broadcasted_iota(jnp.int32, (256, inner), 0) % 128
    return taps, head, skip, one.astype(BF)


def mixer_forward(pre, taps, head, skip, spread):
    length, columns = pre.shape
    both = taps.shape[1]
    inner = skip.shape[1]
    steps = length // SPAN
    return pl.pallas_call(
        forward_kernel,
        grid=(steps,),
        in_specs=[
            pl.BlockSpec((SPAN, columns), lambda i: (i, 0)),
            whole(taps.shape), whole(head.shape), whole(skip.shape), whole(spread.shape),
        ],
        out_specs=[
            pl.BlockSpec((SPAN, inner), lambda i: (i, 0)),
            pl.BlockSpec((128, inner), lambda i: (i, 0)),
            pl.BlockSpec((SPAN, both), lambda i: (i, 0)),
        ],
        out_shape=[
            shape_of((length, inner), F32),
            stored((steps * 128, inner), BF),
            stored((length, both), F32),
        ],
        scratch_shapes=[pltpu.VMEM((SPAN + 8, both), F32), pltpu.VMEM((128, inner), F32)],
        compiler_params=params(20, "arbitrary"),
        cost_estimate=lasting(13),
        name="mixer_forward",
    )(near(pre), taps, head, skip, spread)


def mixer_backward(pre, conv, dy, kept, taps, head, skip, spread):
    length, columns = pre.shape
    both = taps.shape[1]
    inner = skip.shape[1]
    steps = length // SPAN
    last = steps - 1
    return pl.pallas_call(
        backward_kernel,
        grid=(steps,),
        in_specs=[
            pl.BlockSpec((SPAN, columns), lambda i: (last - i, 0)),
            pl.BlockSpec((SPAN, both), lambda i: (last - i, 0)),
            pl.BlockSpec((SPAN, inner), lambda i: (last - i, 0)),
            pl.BlockSpec((128, inner), lambda i: (last - i, 0)),
            whole(taps.shape), whole(head.shape), whole(skip.shape), whole(spread.shape),
        ],
        out_specs=[
            pl.BlockSpec((SPAN, columns), lambda i: (last - i, 0)),
            whole((8, both)),
            whole((8, 128)),
        ],
        out_shape=[
            held_near((length, columns), BF),
            shape_of((8, both), F32),
            shape_of((8, 128), F32),
        ],
        scratch_shapes=[
            pltpu.VMEM((SPAN + 8, both), F32),
            pltpu.VMEM((128, inner), F32),
            pltpu.VMEM((8, inner), F32),
        ],
        compiler_params=params(24, "arbitrary"),
        cost_estimate=lasting(30),
        name="mixer_backward",
    )(far(pre), far(conv), far(dy), far(kept), taps, head, skip, spread)


CELLS = [(xh, xl, core) for xh in range(2) for xl in range(2) for core in range(2)]
TURNS = [(a, b) for a in range(2) for b in range(2)]


def moves(rule):
    return [(4 * c[0] + 2 * c[1] + c[2], 4 * d[0] + 2 * d[1] + d[2]) for c in CELLS for d in [rule(*c)]]


def permute(value, rule):
    return lax.ppermute(value, GROUP, moves(rule))


def trade(value):
    return permute(
        value, lambda xh, xl, core: (xh, xl, core) if xh == core else (1 - xh, xl, 1 - core)
    )


def swap_core(value):
    return lax.ppermute(value, "core", [(0, 1), (1, 0)])


def to_workers(value):
    return [
        permute(value, lambda xh, xl, core, a=a, b=b: (core ^ a, xl ^ b, xh)) for a, b in TURNS
    ]


def to_owners(blocks):
    return [
        permute(block, lambda xh, xl, core, a=a, b=b: (core, xl ^ b, xh ^ a))
        for block, (a, b) in zip(blocks, TURNS)
    ]


def around(value):
    return [value] + [
        permute(value, lambda xh, xl, core, a=a, b=b: (xh ^ a, xl ^ b, core)) for a, b in TURNS[1:]
    ]


def gather_plane(shard):
    count = lax.axis_size(PLANE)
    spread = jnp.broadcast_to(shard[None], (count,) + shard.shape)
    got = lax.all_to_all(spread, PLANE, 0, 0, tiled=True)
    return got.reshape((count * shard.shape[0],) + shard.shape[1:])


def exchange(blocks):
    return lax.all_to_all(blocks, PLANE, 0, 0, tiled=True)


def after(*values):
    return lax.optimization_barrier(values)


def on_device(
    hidden_in,
    cotangent,
    norm_gain,
    w_z,
    w_x,
    w_bc,
    w_dt,
    conv_x,
    conv_bc,
    head_params,
    gate_gain,
    w_out,
):
    block, wide = w_x.shape
    states = w_bc.shape[1]
    heads = w_dt.shape[1]
    both = wide + states
    xh, xl, core = (lax.axis_index(axis) for axis in GROUP)
    meta = jnp.stack([(xl ^ b) * 2 + (xh ^ a) for a, b in TURNS] + [core, xh]).astype(jnp.int32)
    gain = norm_gain[None]

    weights = trade(pack(w_z, w_out.T, w_x, w_bc, w_dt.T))
    small = jnp.concatenate(
        [conv_x, gate_gain[None], jnp.pad(head_params, ((0, 0), (0, wide - heads)))[:2]]
    )
    small = jnp.concatenate([small, jnp.pad(head_params[2:], ((0, 7), (0, wide - heads)))])
    small, weights = after(small, weights)
    small = jnp.where(core == xh, small, swap_core(small))

    mine = gather_plane(weights)
    hidden, weights = after(hidden_in, weights)
    hidden_blocks = to_workers(hidden)
    conv_x, gate_row, head_params = small[:5], small[5:6], small[6:9, :heads]
    taps, head, skip, spread = mixer_tables(conv_x, conv_bc, head_params)
    first_half, cot, taps, head, skip, spread, gate_row, meta, gain = after(
        hidden_blocks[:2], cotangent, taps, head, skip, spread, gate_row, meta, gain
    )
    hidden_blocks = first_half + hidden_blocks[2:]
    cot_blocks = to_workers(cot)
    tokens, tokens_t = place(meta, gain, hidden_blocks, True)
    tokens, mine, cot_first = after(tokens, mine, cot_blocks[0])
    cot_blocks = [cot_first] + cot_blocks[1:]
    other = swap_core(mine)

    pre, z = project(tokens, mine, other, wide)
    y, kept, conv = mixer_forward(pre, taps, head, skip, spread)
    y, cot_blocks = after(y, cot_blocks)
    cot, cot_t = place(meta, gain, cot_blocks, False)
    dy, sums = gate_sums(cot, mine, other, y, z, gate_row)
    normed_y, gate, dscan, gain_grad, keep, send = gate_back(
        block, 4.0 * wide, around(sums), z, dy, y, gate_row, tokens_t, cot_t
    )

    early = (keep.astype(F32) + swap_core(send).astype(F32)).astype(BF)
    out_blocks = project_out(meta, normed_y, mine, other)
    dscan, early, out_blocks = after(dscan, early, out_blocks)
    early = exchange(early)
    out_blocks = to_owners(out_blocks)
    late, conv_grad, head_grad = mixer_backward(pre, conv, dscan, kept, taps, head, skip, spread)
    *back_blocks, norm_part = project_back(
        meta, late, gate, mine, other, mine, other, tokens, gain
    )
    late, back_blocks, out_blocks = after(late, back_blocks, out_blocks)
    back_blocks = to_owners(back_blocks)

    rest = jnp.pad(
        jnp.concatenate([norm_part[:1, :wide], norm_part[:1, wide:], gain_grad[:1]]),
        ((0, 0), (0, states)),
    )
    vector = jnp.concatenate([jnp.concatenate([conv_grad[:5], rest]), head_grad], axis=1)
    vector = jnp.pad(vector, ((0, 8), (0, 0)))
    keep, send = weight_grad(tokens_t, late, vector)
    send, early, back_first = after(send, early, back_blocks[0])
    output = finish_output(meta, out_blocks, hidden_in)
    got = swap_core(send).astype(F32)
    half = keep.shape[0]
    late_sum = (keep + got[:half]).astype(BF).reshape(-1, block, both + 128)
    vector = (vector[:8] + got[half : half + 8]).astype(BF)
    vector = jnp.broadcast_to(vector[None], (late_sum.shape[0],) + vector.shape)
    late_sum = jnp.concatenate([late_sum, vector], axis=1)
    back_blocks = [back_first] + back_blocks[1:]
    early = trade(early.astype(F32).sum(axis=0))
    got, early, output = after(exchange(late_sum), early, output)
    own, shared = total_of(got, states)
    own, back_blocks = after(own, back_blocks)
    own = trade(own)

    shared = [
        permute(shared, lambda xh, xl, core, a=a, b=b: (core, xl ^ b, xh ^ a)) for a, b in TURNS
    ]
    input_grad = finish_input(meta, back_blocks, hidden_in, cotangent, gain)
    norm_grad, x_grad, bc_grad, dt_grad, conv_x_grad, conv_bc_grad, head_part, gate_part = deliver(
        own, shared, block, heads
    )
    return (
        output,
        input_grad,
        norm_grad,
        early[0],
        x_grad,
        bc_grad,
        dt_grad.T,
        conv_x_grad,
        conv_bc_grad,
        head_part,
        gate_part,
        early[1].T,
    )


def solution(mesh):
    fine = Mesh(mesh.devices.reshape(2, 4, 4, 2, 2), AXES)
    rows, both, lanes = P(AXES, None), P(DP, TN), P(None, TN)
    return jax.shard_map(
        on_device,
        mesh=fine,
        in_specs=(rows, rows, P(), both, both, P(DP, None), both, lanes, P(), lanes, P(TN), P(TN, DP)),
        out_specs=(
            rows, rows, P(), both, both, P(DP, None), both, lanes, P(), lanes, P(TN), P(TN, DP)
        ),
        check_vma=False,
    )
```

```python
import functools
import jax
import jax.numpy as jnp
from jax import lax
from jax.experimental import pallas as pl
from jax.experimental.pallas import tpu as pltpu
from jax.sharding import Mesh, PartitionSpec as P

EPS = 1e-05
AXES = ("xh", "y", "z", "xl", "core")
DP = ("xh", "y", "z")
TN = ("xl", "core")
GROUP = ("xh", "xl", "core")
PLANE = ("y", "z")
BF = jnp.bfloat16
F32 = jnp.float32
SPAN = 128
LIMIT = 36


def near(value):
    return pltpu.with_memory_space_constraint(value, pltpu.VMEM)


def far(value):
    return pltpu.with_memory_space_constraint(value, pltpu.HBM)


ROWS = 512
SCALE = 1.15e9


def nn(left, right):
    return lax.dot_general(left, right, (((1,), (0,)), ((), ())), preferred_element_type=F32)


def nt(left, right):
    return lax.dot_general(left, right, (((1,), (1,)), ((), ())), preferred_element_type=F32)


def halves(value):
    high = value.astype(BF)
    low = (value - high.astype(F32)).astype(BF)
    return high, low


def running(mask, value):
    high, low = halves(value)
    return nn(jnp.concatenate([mask, mask], axis=1), jnp.concatenate([high, low], axis=0))


def close_nt(left, right):
    left_high, left_low = halves(left)
    right_high, right_low = halves(right)
    return nt(
        jnp.concatenate([left_high, left_high, left_low], axis=1),
        jnp.concatenate([right_high, right_low, right_high], axis=1),
    )


def expand(value, spread):
    high, low = halves(value)
    return nn(jnp.concatenate([high, low], axis=1), spread)


def by_head(value, spread):
    width = spread.shape[0] // 2
    high, low = halves(value)
    return nt(high, spread[:width]) + nt(low, spread[:width])


def logistic(value):
    return 1.0 / (1.0 + jnp.exp(-value))


def sigmoid(value):
    return 0.5 * jnp.tanh(0.5 * value) + 0.5


def softplus(value):
    return jnp.maximum(value, 0.0) + jnp.log1p(jnp.exp(-jnp.abs(value)))


def conv_rows(ext_ref, taps):
    total = taps[4:5] + ext_ref[5 : 5 + SPAN] * taps[0:1]
    for k in range(1, 4):
        total = total + ext_ref[5 + k : 5 + k + SPAN] * taps[k : k + 1]
    return total


def scan_parts(conv, pre_dt, head, spread, tri):
    sig = sigmoid(conv)
    xbc = conv * sig
    raw = pre_dt + head[1:2]
    step = softplus(raw)
    decay = running(tri, step * head[0:1])
    last = decay[SPAN - 1 : SPAN]
    grown = expand(jnp.concatenate([step, jnp.exp(decay), jnp.exp(last - decay)], axis=0), spread)
    step_x, start_x, end_x = grown[:SPAN], grown[SPAN : 2 * SPAN], grown[2 * SPAN :]
    return sig, xbc, raw, step, decay, step_x, start_x, end_x


def forward_kernel(
    pre_ref, taps_ref, head_ref, skip_ref, spread_ref, y_ref, kept_ref, conv_ref, ext_ref, state_ref
):
    inner = y_ref.shape[1]
    both = ext_ref.shape[1]

    @pl.when(pl.program_id(0) == 0)
    def _():
        ext_ref[0:8] = jnp.zeros((8, both), F32)
        state_ref[...] = jnp.zeros_like(state_ref)

    ext_ref[8 : 8 + SPAN] = pre_ref[:, :both]
    rows = lax.broadcasted_iota(jnp.int32, (SPAN, SPAN), 0)
    cols = lax.broadcasted_iota(jnp.int32, (SPAN, SPAN), 1)
    keep = rows >= cols
    tri = jnp.where(keep, 1.0, 0.0).astype(BF)
    spread = spread_ref[...]
    conv = conv_rows(ext_ref, taps_ref[...])
    conv_ref[...] = conv
    sig, xbc, raw, step, decay, step_x, start_x, end_x = scan_parts(
        conv, pre_ref[:, both:], head_ref[...], spread, tri
    )
    ext_ref[0:8] = ext_ref[SPAN : SPAN + 8]
    state_width = (both - inner) // 2
    x = xbc[:, :inner]
    b = xbc[:, inner : inner + state_width]
    c = xbc[:, inner + state_width :]
    decay_t = decay.T
    scaled = x * step_x
    low = scaled.astype(BF)
    scores = close_nt(c, b)
    state = state_ref[...]
    state_low = state.astype(BF)
    kept_ref[...] = state_low
    carried = nn(c.astype(BF), state_low) * start_x + x * skip_ref[...]
    left = cols < 64
    for pair in range(inner // 128):
        at = slice(128 * pair, 128 * pair + 128)
        x_pair = low[:, at]
        found = []
        for h in (2 * pair, 2 * pair + 1):
            gap = decay[:, h : h + 1] - decay_t[h : h + 1]
            weight = jnp.exp(jnp.where(keep, gap, -1e30)) * scores
            found.append(nn(weight.astype(BF), x_pair))
        y_ref[:, at] = jnp.where(left, found[0], found[1]) + carried[:, at]
    state_ref[...] = state * start_x[SPAN - 1 : SPAN] + nn(
        b.T.astype(BF), (scaled * end_x).astype(BF)
    )


def backward_kernel(
    pre_ref, conv_ref, dy_ref, kept_ref, taps_ref, head_ref, skip_ref, spread_ref,
    late_ref, conv_grad_ref, head_grad_ref,
    dext_ref, dstate_ref, skip_sum_ref,
):
    inner = dy_ref.shape[1]
    both = dext_ref.shape[1]
    steps = pl.num_programs(0)
    at_step = pl.program_id(0)

    @pl.when(at_step == 0)
    def _():
        dext_ref[SPAN : SPAN + 8] = jnp.zeros((8, both), F32)
        dstate_ref[...] = jnp.zeros_like(dstate_ref)
        skip_sum_ref[...] = jnp.zeros_like(skip_sum_ref)
        conv_grad_ref[...] = jnp.zeros_like(conv_grad_ref)
        head_grad_ref[...] = jnp.zeros_like(head_grad_ref)

    rows = lax.broadcasted_iota(jnp.int32, (SPAN, SPAN), 0)
    cols = lax.broadcasted_iota(jnp.int32, (SPAN, SPAN), 1)
    tri = jnp.where(rows >= cols, 1.0, 0.0).astype(BF)
    upper = jnp.where(cols >= rows, 1.0, 0.0).astype(BF)
    keep = cols >= rows
    spread = spread_ref[...]
    taps = taps_ref[...]
    head = head_ref[...]
    conv = conv_ref[...]
    sig, xbc, raw, step, decay, step_x, start_x, end_x = scan_parts(
        conv, pre_ref[:, both:], head, spread, tri
    )
    state_width = (both - inner) // 2
    x = xbc[:, :inner]
    b = xbc[:, inner : inner + state_width]
    c = xbc[:, inner + state_width :]
    b_low, c_low = b.astype(BF), c.astype(BF)
    decay_t = decay.T
    scaled = x * step_x
    low = scaled.astype(BF)
    scores = close_nt(b, c)
    dy = dy_ref[...].astype(F32)
    dy_low = dy.astype(BF)
    kept = kept_ref[...]
    dstate = dstate_ref[...]
    dstate_low = dstate.astype(BF)
    left = cols < 64
    wide_rows = lax.broadcasted_iota(jnp.int32, (SPAN, SPAN), 0)
    d_scores = jnp.zeros((SPAN, SPAN), F32)
    into = jnp.zeros((SPAN, SPAN), F32)
    out_of = jnp.zeros((SPAN, SPAN), F32)
    pieces = []
    none = jnp.zeros((SPAN, 128), BF)
    for pair in range(inner // 128):
        at = slice(128 * pair, 128 * pair + 128)
        x_pair = low[:, at]
        dy_pair = dy_low[:, at]
        found = []
        for side, h in enumerate((2 * pair, 2 * pair + 1)):
            gap = decay_t[h : h + 1] - decay[:, h : h + 1]
            fall = jnp.exp(jnp.where(keep, gap, -1e30))
            mine = jnp.where(left if side == 0 else ~left, dy_pair, none)
            back = nt(x_pair, mine) * fall
            d_scores = d_scores + back
            both_ways = back * scores
            into = jnp.where(wide_rows == h, jnp.sum(both_ways, axis=0, keepdims=True), into)
            out_of = jnp.where(cols == h, jnp.sum(both_ways, axis=1, keepdims=True), out_of)
            found.append(nn((fall * scores).astype(BF), dy_pair))
        pieces.append(jnp.where(left, found[0], found[1]))
    inside = jnp.concatenate(pieces, axis=1)
    dy_start = dy * start_x
    dy_start_low = dy_start.astype(BF)
    from_state = nn(c_low, kept)
    scaled_end = scaled * end_x
    d_end = nn(b_low, dstate_low)
    d_scaled = inside + d_end * end_x
    pair_start = by_head(dy_start * from_state, spread)
    pair_end = by_head(scaled_end * d_end, spread)
    d_scores_low = d_scores.astype(BF)
    d_c = nn(d_scores.T.astype(BF), b_low) + nt(dy_start_low, kept)
    d_b = nn(d_scores_low, c_low) + nt(scaled_end.astype(BF), dstate_low)
    through = jnp.sum(kept.astype(F32) * dstate, axis=0, keepdims=True)
    through = by_head(jnp.broadcast_to(through * start_x[SPAN - 1 : SPAN], (8, inner)), spread)[0:1]
    at_end = jnp.sum(pair_end, axis=0, keepdims=True) + through
    d_decay = into.T - out_of + pair_start - pair_end
    d_decay = d_decay + jnp.where(rows == SPAN - 1, at_end, 0.0)
    d_log = running(upper, d_decay)
    d_step = by_head(d_scaled * x, spread) + d_log * head[0:1]
    d_raw = d_step * logistic(raw)
    dstate_ref[...] = dstate * start_x[SPAN - 1 : SPAN] + nn(c.T.astype(BF), dy_start_low)
    late_ref[:, both:] = d_raw.astype(BF)
    head_grad_ref[0:1] += jnp.sum(d_log * step, axis=0, keepdims=True) * head[0:1]
    head_grad_ref[1:2] += jnp.sum(d_raw, axis=0, keepdims=True)
    skip_sum_ref[0:1] += jnp.sum(dy * x, axis=0, keepdims=True)
    dx = d_scaled * step_x + dy * skip_ref[...]
    d_conv = jnp.concatenate([dx, d_b, d_c], axis=1) * (sig * (1.0 + conv * (1.0 - sig)))
    dext_ref[0:SPAN] = d_conv
    values = pre_ref[:, :both]
    d_pre = d_conv * taps[3:4]
    conv_grad_ref[3:4] += jnp.sum(d_conv * values, axis=0, keepdims=True)
    for k in range(3):
        moved = dext_ref[3 - k : 3 - k + SPAN]
        d_pre = d_pre + moved * taps[k : k + 1]
        conv_grad_ref[k : k + 1] += jnp.sum(moved * values, axis=0, keepdims=True)
    conv_grad_ref[4:5] += jnp.sum(d_conv, axis=0, keepdims=True)
    dext_ref[SPAN : SPAN + 8] = dext_ref[0:8]
    late_ref[:, :both] = d_pre.astype(BF)

    @pl.when(at_step == steps - 1)
    def _():
        head_grad_ref[2:3] += by_head(
            jnp.broadcast_to(skip_sum_ref[0:1], (8, inner)), spread
        )[0:1]


def whole(shape):
    return pl.BlockSpec(shape, lambda *_: (0,) * len(shape))


def column(rows, width, shift=0):
    return pl.BlockSpec((rows, width), lambda j, *_: (0, j + shift))


def shape_of(shape, dtype):
    return jax.ShapeDtypeStruct(shape, dtype)


def stored(shape, dtype):
    return pltpu.HBM(shape, dtype)


def held_near(shape, dtype):
    return pltpu.VMEM(shape, dtype)


def params(limit, *semantics):
    return pltpu.CompilerParams(
        dimension_semantics=semantics or None, vmem_limit_bytes=LIMIT * 1024 * 1024
    )


def lasting(us):
    return pl.CostEstimate(flops=int(us * SCALE), bytes_accessed=1024, transcendentals=0)


def place_kernel(normalise, meta_ref, gain_ref, *refs):
    blocks, out_ref, flip_ref = refs[:4], refs[4], refs[5]
    rows, width = blocks[0].shape
    half = width // 2
    core = meta_ref[4]
    first = pl.multiple_of(core * half, 128)
    second = pl.multiple_of((1 - core) * half, 128)
    for k, block in enumerate(blocks):
        at = pl.multiple_of(meta_ref[k] * rows, rows)
        value = block[...].astype(F32)
        if normalise:
            scale = lax.rsqrt(jnp.mean(value * value, axis=1, keepdims=True) + EPS)
            value = value * scale * gain_ref[...]
        low = value.astype(BF)
        out_ref[pl.ds(at, rows), pl.ds(first, half)] = low[:, :half]
        out_ref[pl.ds(at, rows), pl.ds(second, half)] = low[:, half:]
        flip = value.T.astype(BF)
        flip_ref[pl.ds(first, half), pl.ds(at, rows)] = flip[:half]
        flip_ref[pl.ds(second, half), pl.ds(at, rows)] = flip[half:]


def place(meta, gain, blocks, normalise):
    rows, width = blocks[0].shape
    vmem = pl.BlockSpec()
    return pl.pallas_call(
        functools.partial(place_kernel, normalise),
        in_specs=[pl.BlockSpec(memory_space=pltpu.SMEM)] + [vmem] * 5,
        out_specs=[vmem, vmem],
        out_shape=[
            (stored if normalise else shape_of)((4 * rows, width), BF),
            shape_of((width, 4 * rows), BF),
        ],
        compiler_params=params(24),
        cost_estimate=lasting(6),
        name="place_normed" if normalise else "place_cotangent",
    )(meta, gain, *[far(block) for block in blocks])


def project_kernel(tokens_ref, xm_ref, xo_ref, zm_ref, zo_ref, pre_ref, z_ref):
    half = xm_ref.shape[0]
    for first, second, out in ((xm_ref, xo_ref, pre_ref), (zm_ref, zo_ref, z_ref)):
        out[...] = nn(tokens_ref[:, :half], first[...]) + nn(tokens_ref[:, half:], second[...])


def project(tokens, mine, other, inner):
    half = mine.shape[0]
    length = tokens.shape[0]
    columns = mine.shape[1] - 2 * inner
    rows = ROWS

    def part(width, shift):
        return pl.BlockSpec(
            (pl.Element(half), pl.Element(width)),
            lambda i: (0, shift),
            pipeline_mode=pl.Buffered(1),
        )

    return pl.pallas_call(
        project_kernel,
        grid=(length // rows,),
        in_specs=[pl.BlockSpec((rows, 2 * half), lambda i: (i, 0))]
        + [part(columns, 2 * inner)] * 2
        + [part(inner, 0)] * 2,
        out_specs=[
            pl.BlockSpec((rows, columns), lambda i: (i, 0)),
            pl.BlockSpec((rows, inner), lambda i: (i, 0)),
        ],
        out_shape=[shape_of((length, columns), F32), shape_of((length, inner), F32)],
        compiler_params=params(20, "arbitrary"),
        cost_estimate=lasting(6),
        name="project_in",
    )(far(tokens), far(mine), other, far(mine), other)


def gate_sums_kernel(
    cot_ref, om_ref, oo_ref, y_ref, z_ref, gain_ref, dy_ref, sums_ref
):
    half = om_ref.shape[0]
    z = z_ref[...]
    dy = nn(cot_ref[:, :half], om_ref[...]) + nn(cot_ref[:, half:], oo_ref[...])
    dy_ref[...] = dy
    gated = y_ref[...] * (z * sigmoid(z))
    ones = jnp.ones((8, z.shape[1]), BF)
    found = []
    for value in (gated * gated, gated * (dy * gain_ref[...])):
        high, low = halves(value)
        found.append(nt(ones, high) + nt(ones, low))
    row = lax.broadcasted_iota(jnp.int32, found[0].shape, 0)
    total = jnp.where(row == 0, found[0], found[1])

    @pl.when(pl.program_id(0) == 0)
    def _():
        sums_ref[...] = total

    @pl.when(pl.program_id(0) > 0)
    def _():
        sums_ref[...] += total


def gate_sums(cot, mine, other, y, z, gain):
    length, inner = y.shape
    half = mine.shape[0]
    tile = 256
    steps = inner // tile
    return pl.pallas_call(
        gate_sums_kernel,
        grid=(steps,),
        in_specs=[
            whole(cot.shape),
            column(half, tile, steps),
            column(half, tile, steps),
            column(length, tile),
            column(length, tile),
            column(1, tile),
        ],
        out_specs=[column(length, tile), whole((8, length))],
        out_shape=[shape_of((length, inner), F32), shape_of((8, length), F32)],
        compiler_params=params(36, "arbitrary"),
        cost_estimate=lasting(6),
        name="gate_sums",
    )(near(cot), far(mine), far(other), near(y), near(z), gain)


def gate_back_kernel(
    width_all, s0, s1, s2, s3, z_ref, dy_ref, y_ref, gain_ref, tokens_t_ref, cot_t_ref,
    normed_ref, gate_ref, dscan_ref, gain_grad_ref, keep_ref, send_ref,
):
    sums = (s0[...] + s1[...]) + (s2[...] + s3[...])
    flat = sums.T
    rms = lax.rsqrt(flat[:, 0:1] / width_all + EPS)
    inner = flat[:, 1:2] * (rms * rms * rms / width_all)
    z = z_ref[...]
    y = y_ref[...]
    dy = dy_ref[...]
    gain = gain_ref[...]
    sig = sigmoid(z)
    act = z * sig
    gated = y * act
    unit = gated * rms
    normed = (unit * gain).astype(BF)
    normed_ref[...] = normed
    gain_grad_ref[...] = jnp.broadcast_to(
        jnp.sum(dy * unit, axis=0, keepdims=True), gain_grad_ref.shape
    )
    d_gated = rms * (dy * gain) - gated * inner
    dscan_ref[...] = d_gated * act
    gate = (d_gated * y * (sig * (1.0 + z * (1.0 - sig)))).astype(BF)
    gate_ref[...] = gate
    half = tokens_t_ref.shape[0] // 2
    for side, (left, right) in enumerate(((tokens_t_ref, gate), (cot_t_ref, normed))):
        for out, at in ((keep_ref, slice(0, half)), (send_ref, slice(half, 2 * half))):
            found = nn(left[at], right).astype(BF)
            out[:, side] = found.reshape(out.shape[0], out.shape[2], found.shape[1])


def gate_back(block, width_all, sums, z, dy, y, gain, tokens_t, cot_t):
    length, inner = y.shape
    half = tokens_t.shape[0] // 2
    tile = 256
    pile = pl.BlockSpec((half // block, 2, block, tile), lambda j: (0, 0, 0, j))
    return pl.pallas_call(
        functools.partial(gate_back_kernel, width_all),
        grid=(inner // tile,),
        in_specs=[whole((8, length))] * 4
        + [column(length, tile)] * 3
        + [column(1, tile), whole(tokens_t.shape), whole(cot_t.shape)],
        out_specs=[column(length, tile)] * 3 + [column(8, tile), pile, pile],
        out_shape=[
            stored((length, inner), BF),
            stored((length, inner), BF),
            stored((length, inner), F32),
            shape_of((8, inner), F32),
            shape_of((half // block, 2, block, inner), BF),
            shape_of((half // block, 2, block, inner), BF),
        ],
        compiler_params=params(44, "arbitrary"),
        cost_estimate=lasting(12),
        name="gate_back",
    )(*sums, near(z), near(dy), near(y), gain, near(tokens_t), near(cot_t))


def scatter_rows(meta_ref, found, scratch, outs):
    rows = outs[0].shape[0]
    scratch[...] = found
    for k, out in enumerate(outs):
        out[...] = scratch[pl.ds(pl.multiple_of(meta_ref[k] * rows, rows), rows), :].astype(BF)


def project_out_kernel(meta_ref, normed_ref, om_ref, oo_ref, *refs):
    outs, scratch = refs[:4], refs[4]

    def step(right):
        scatter_rows(meta_ref, nt(normed_ref[...], right[...]), scratch, outs)

    first = pl.program_id(0) < pl.num_programs(0) // 2
    pl.when(first)(lambda: step(om_ref))
    pl.when(jnp.logical_not(first))(lambda: step(oo_ref))


def sides(tile, columns, shift, per):
    return [
        pl.BlockSpec(
            (pl.Element(tile), pl.Element(columns)),
            lambda j: (jnp.minimum(j, per - 1) * tile, shift),
        ),
        pl.BlockSpec(
            (pl.Element(tile), pl.Element(columns)),
            lambda j: (jnp.maximum(j - per, 0) * tile, shift),
        ),
    ]


def project_out(meta, normed_y, mine, other):
    length, inner = normed_y.shape
    half = mine.shape[0]
    rows = length // 4
    per = 3
    tile = half // per
    return pl.pallas_call(
        project_out_kernel,
        grid=(2 * per,),
        in_specs=[pl.BlockSpec(memory_space=pltpu.SMEM), whole(normed_y.shape)]
        + sides(tile, inner, inner, per),
        out_specs=[column(rows, tile)] * 4,
        out_shape=[stored((rows, 2 * half), BF)] * 4,
        scratch_shapes=[pltpu.VMEM((length, tile), F32)],
        compiler_params=params(24, "arbitrary"),
        cost_estimate=lasting(6),
        name="project_out",
    )(meta, far(normed_y), far(mine), far(other))


def project_back_kernel(
    meta_ref, late_ref, gate_ref, xm_ref, xo_ref, zm_ref, zo_ref, tokens_ref, gain_ref, *refs
):
    outs, grad_ref, scratch = refs[:4], refs[4], refs[5]
    tile = scratch.shape[1]
    j = pl.program_id(0)
    per = pl.num_programs(0) // 2
    side, within = j // per, j % per
    core = meta_ref[4]

    def step(x_ref, z_ref):
        found = nt(late_ref[...], x_ref[...]) + nt(gate_ref[...], z_ref[...])
        total = jnp.sum(found * tokens_ref[...].astype(F32), axis=0, keepdims=True)
        owner = side + core - 2 * side * core
        place = pl.ds(pl.multiple_of((per * owner + within) * tile, 128), tile)
        grad_ref[:, place] = jnp.broadcast_to(total / gain_ref[:, place], (8, tile))
        scatter_rows(meta_ref, found, scratch, outs)

    pl.when(side == 0)(lambda: step(xm_ref, zm_ref))
    pl.when(side == 1)(lambda: step(xo_ref, zo_ref))


def project_back(meta, late, gate, mine1, other1, mine2, other2, tokens, gain):
    length, columns = late.shape
    inner = gate.shape[1]
    half = mine1.shape[0]
    rows = length // 4
    per = 3
    tile = half // per
    return pl.pallas_call(
        project_back_kernel,
        grid=(2 * per,),
        in_specs=[pl.BlockSpec(memory_space=pltpu.SMEM), whole(late.shape), whole(gate.shape)]
        + sides(tile, columns, 2 * inner, per)
        + sides(tile, inner, 0, per)
        + [column(length, tile), whole(gain.shape)],
        out_specs=[column(rows, tile)] * 4 + [whole((8, 2 * half))],
        out_shape=[stored((rows, 2 * half), BF)] * 4 + [shape_of((8, 2 * half), F32)],
        scratch_shapes=[pltpu.VMEM((length, tile), F32)],
        compiler_params=params(32, "arbitrary"),
        cost_estimate=lasting(0.5),
        name="project_back",
    )(
        meta, near(late), far(gate), far(mine1), far(other1), far(mine2), far(other2), far(tokens), gain
    )


def weight_grad_kernel(tokens_t_ref, late_ref, vector_ref, keep_ref, send_ref):
    half = keep_ref.shape[0]
    late = late_ref[...]
    keep_ref[...] = nn(tokens_t_ref[:half], late)
    send_ref[:half] = nn(tokens_t_ref[half:], late).astype(BF)
    send_ref[half:] = vector_ref[...].astype(BF)


def weight_grad(tokens_t, late, vector):
    length, columns = late.shape
    half = tokens_t.shape[0] // 2
    rows = half + vector.shape[0]
    tile = 384
    return pl.pallas_call(
        weight_grad_kernel,
        grid=(columns // tile,),
        in_specs=[whole(tokens_t.shape), column(length, tile), column(vector.shape[0], tile)],
        out_specs=[column(half, tile), column(rows, tile)],
        out_shape=[stored((half, columns), F32), stored((rows, columns), BF)],
        compiler_params=params(24, "arbitrary"),
        cost_estimate=lasting(0.5),
        name="weight_grad",
    )(far(tokens_t), near(late), vector)


def pack_kernel(z_ref, out_ref, x_ref, bc_ref, dt_ref, packed_ref):
    at = 0
    for ref in (z_ref, out_ref, x_ref, bc_ref):
        packed_ref[:, at : at + ref.shape[1]] = ref[...]
        at += ref.shape[1]
    heads, rows = dt_ref.shape
    tall = jnp.concatenate([dt_ref[...].astype(F32), jnp.zeros((128 - heads, rows), F32)], axis=0)
    packed_ref[:, at:] = tall.T.astype(BF)


def pack(*parts):
    vmem = pl.BlockSpec()
    return pl.pallas_call(
        pack_kernel,
        in_specs=[vmem] * 5,
        out_specs=vmem,
        out_shape=shape_of(
            (parts[0].shape[0], sum(part.shape[1] for part in parts[:4]) + 128), BF
        ),
        compiler_params=params(8),
        cost_estimate=lasting(1),
        name="pack_weights",
    )(*[far(part) for part in parts])


def total_kernel(states, got_ref, joint_ref, shared_ref):
    total = jnp.sum(got_ref[...].astype(F32), axis=0)
    rows = total.shape[0]
    inner = joint_ref.shape[1] - 128 - states
    both = inner + states
    joint_ref[...] = jnp.zeros_like(joint_ref)
    joint_ref[:rows, :inner] = total[:, :inner]
    joint_ref[:rows, inner : inner + 128] = total[:, both:]
    shared_ref[:rows] = total[:, inner:both]
    per = inner // states
    for k in range(2 * per):
        line = rows - 3 + k // per
        at = states * (k % per)
        shared_ref[rows + k : rows + k + 1] = total[line : line + 1, at : at + states]
    joint_ref[:, inner + 128 :] = shared_ref[...]


def total_of(got, states):
    count, rows, columns = got.shape
    vmem = pl.BlockSpec()
    extra = rows + 2 * ((columns - states - 128) // states)
    return pl.pallas_call(
        functools.partial(total_kernel, states),
        in_specs=[vmem],
        out_specs=[vmem, vmem],
        out_shape=[shape_of((extra, columns), F32), shape_of((extra, states), F32)],
        compiler_params=params(16),
        cost_estimate=lasting(3),
        name="late_total",
    )(got)


def deliver_kernel(
    joint_ref, s1, s2, s3,
    norm_ref, x_ref, bc_ref, dt_ref, conv_x_ref, conv_bc_ref, head_ref, gate_ref,
):
    block, inner = x_ref.shape
    own = joint_ref[:, : inner + 128]
    shared = (joint_ref[:, inner + 128 :] + s1[...]) + (s2[...] + s3[...])
    heads = dt_ref.shape[0]
    x_ref[...] = own[:block, :inner]
    dt_ref[...] = own[:block, inner:].T[:heads]
    conv_x_ref[...] = own[block : block + 5, :inner]
    head_ref[...] = own[block : block + 3, inner : inner + heads]
    gate_ref[...] = own[block + 7, :inner]
    bc_ref[...] = shared[:block]
    conv_bc_ref[...] = shared[block : block + 5]
    states = bc_ref.shape[1]
    for k in range(norm_ref.shape[0] // states):
        norm_ref[states * k : states * k + states] = shared[block + 8 + k]


def deliver(own, shared, block, heads):
    vmem = pl.BlockSpec()
    states = shared[0].shape[1]
    inner = own.shape[1] - 128 - states
    shapes = [
        (2 * inner,), (block, inner), (block, states), (heads, block),
        (5, inner), (5, states), (3, heads), (inner,),
    ]
    return pl.pallas_call(
        deliver_kernel,
        in_specs=[vmem] * 4,
        out_specs=[vmem] * 8,
        out_shape=[shape_of(shape, F32) for shape in shapes],
        compiler_params=params(16),
        cost_estimate=lasting(2),
        name="deliver_late",
    )(own, *shared)


def owner_total(xh_ref, blocks):
    total = sum(block[...].astype(F32) for block in blocks)
    half = total.shape[1] // 2
    turned = jnp.concatenate([total[:, half:], total[:, :half]], axis=1)
    return jnp.where(xh_ref[5] == 0, total, turned)


def output_kernel(meta_ref, b0, b1, b2, b3, hidden_ref, out_ref):
    mixed = owner_total(meta_ref, (b0, b1, b2, b3))
    out_ref[...] = (hidden_ref[...].astype(F32) + mixed).astype(BF)


def finish_output(meta, blocks, hidden):
    vmem = pl.BlockSpec()
    return pl.pallas_call(
        output_kernel,
        in_specs=[pl.BlockSpec(memory_space=pltpu.SMEM)] + [vmem] * 5,
        out_specs=vmem,
        out_shape=shape_of(hidden.shape, BF),
        compiler_params=params(16),
        cost_estimate=lasting(3),
        name="finish_output",
    )(meta, *[far(block) for block in blocks], far(hidden))


def input_kernel(meta_ref, b0, b1, b2, b3, hidden_ref, cot_ref, gain_ref, out_ref):
    scaled = owner_total(meta_ref, (b0, b1, b2, b3)) * gain_ref[...]
    resid = hidden_ref[...].astype(F32)
    inv = lax.rsqrt(jnp.mean(resid * resid, axis=1, keepdims=True) + EPS)
    along = jnp.mean(resid * scaled, axis=1, keepdims=True) * (inv * inv * inv)
    out_ref[...] = inv * scaled - resid * along + cot_ref[...].astype(F32)


def finish_input(meta, blocks, hidden, cot, gain):
    vmem = pl.BlockSpec()
    return pl.pallas_call(
        input_kernel,
        in_specs=[pl.BlockSpec(memory_space=pltpu.SMEM)] + [vmem] * 7,
        out_specs=vmem,
        out_shape=shape_of(hidden.shape, F32),
        compiler_params=params(16),
        cost_estimate=lasting(3),
        name="finish_input",
    )(meta, *blocks, far(hidden), far(cot), gain)


def mixer_tables(conv_x, conv_bc, head_params):
    heads = head_params.shape[1]
    inner = conv_x.shape[1]
    taps = jnp.pad(jnp.concatenate([conv_x, conv_bc], axis=1), ((0, 3), (0, 0)))
    head = jnp.stack([-jnp.exp(head_params[0]), head_params[1]])
    head = jnp.pad(head, ((0, 6), (0, 128 - heads)))
    skip = jnp.repeat(head_params[2], inner // heads)[None]
    owner = lax.broadcasted_iota(jnp.int32, (256, inner), 1) // (inner // heads)
    one = owner == lax.broadcasted_iota(jnp.int32, (256, inner), 0) % 128
    return taps, head, skip, one.astype(BF)


def mixer_forward(pre, taps, head, skip, spread):
    length, columns = pre.shape
    both = taps.shape[1]
    inner = skip.shape[1]
    steps = length // SPAN
    return pl.pallas_call(
        forward_kernel,
        grid=(steps,),
        in_specs=[
            pl.BlockSpec((SPAN, columns), lambda i: (i, 0)),
            whole(taps.shape), whole(head.shape), whole(skip.shape), whole(spread.shape),
        ],
        out_specs=[
            pl.BlockSpec((SPAN, inner), lambda i: (i, 0)),
            pl.BlockSpec((128, inner), lambda i: (i, 0)),
            pl.BlockSpec((SPAN, both), lambda i: (i, 0)),
        ],
        out_shape=[
            shape_of((length, inner), F32),
            stored((steps * 128, inner), BF),
            stored((length, both), F32),
        ],
        scratch_shapes=[pltpu.VMEM((SPAN + 8, both), F32), pltpu.VMEM((128, inner), F32)],
        compiler_params=params(20, "arbitrary"),
        cost_estimate=lasting(13),
        name="mixer_forward",
    )(near(pre), taps, head, skip, spread)


def mixer_backward(pre, conv, dy, kept, taps, head, skip, spread):
    length, columns = pre.shape
    both = taps.shape[1]
    inner = skip.shape[1]
    steps = length // SPAN
    last = steps - 1
    return pl.pallas_call(
        backward_kernel,
        grid=(steps,),
        in_specs=[
            pl.BlockSpec((SPAN, columns), lambda i: (last - i, 0)),
            pl.BlockSpec((SPAN, both), lambda i: (last - i, 0)),
            pl.BlockSpec((SPAN, inner), lambda i: (last - i, 0)),
            pl.BlockSpec((128, inner), lambda i: (last - i, 0)),
            whole(taps.shape), whole(head.shape), whole(skip.shape), whole(spread.shape),
        ],
        out_specs=[
            pl.BlockSpec((SPAN, columns), lambda i: (last - i, 0)),
            whole((8, both)),
            whole((8, 128)),
        ],
        out_shape=[
            held_near((length, columns), BF),
            shape_of((8, both), F32),
            shape_of((8, 128), F32),
        ],
        scratch_shapes=[
            pltpu.VMEM((SPAN + 8, both), F32),
            pltpu.VMEM((128, inner), F32),
            pltpu.VMEM((8, inner), F32),
        ],
        compiler_params=params(24, "arbitrary"),
        cost_estimate=lasting(30),
        name="mixer_backward",
    )(far(pre), far(conv), far(dy), far(kept), taps, head, skip, spread)


CELLS = [(xh, xl, core) for xh in range(2) for xl in range(2) for core in range(2)]
TURNS = [(a, b) for a in range(2) for b in range(2)]


def moves(rule):
    return [(4 * c[0] + 2 * c[1] + c[2], 4 * d[0] + 2 * d[1] + d[2]) for c in CELLS for d in [rule(*c)]]


def permute(value, rule):
    return lax.ppermute(value, GROUP, moves(rule))


def trade(value):
    return permute(
        value, lambda xh, xl, core: (xh, xl, core) if xh == core else (1 - xh, xl, 1 - core)
    )


def swap_core(value):
    return lax.ppermute(value, "core", [(0, 1), (1, 0)])


def to_workers(value):
    return [
        permute(value, lambda xh, xl, core, a=a, b=b: (core ^ a, xl ^ b, xh)) for a, b in TURNS
    ]


def to_owners(blocks):
    return [
        permute(block, lambda xh, xl, core, a=a, b=b: (core, xl ^ b, xh ^ a))
        for block, (a, b) in zip(blocks, TURNS)
    ]


def around(value):
    return [value] + [
        permute(value, lambda xh, xl, core, a=a, b=b: (xh ^ a, xl ^ b, core)) for a, b in TURNS[1:]
    ]


def gather_plane(shard):
    count = lax.axis_size(PLANE)
    spread = jnp.broadcast_to(shard[None], (count,) + shard.shape)
    got = lax.all_to_all(spread, PLANE, 0, 0, tiled=True)
    return got.reshape((count * shard.shape[0],) + shard.shape[1:])


def exchange(blocks):
    return lax.all_to_all(blocks, PLANE, 0, 0, tiled=True)


def after(*values):
    return lax.optimization_barrier(values)


def on_device(
    hidden_in,
    cotangent,
    norm_gain,
    w_z,
    w_x,
    w_bc,
    w_dt,
    conv_x,
    conv_bc,
    head_params,
    gate_gain,
    w_out,
):
    block, wide = w_x.shape
    states = w_bc.shape[1]
    heads = w_dt.shape[1]
    both = wide + states
    xh, xl, core = (lax.axis_index(axis) for axis in GROUP)
    meta = jnp.stack([(xl ^ b) * 2 + (xh ^ a) for a, b in TURNS] + [core, xh]).astype(jnp.int32)
    gain = norm_gain[None]

    weights = trade(pack(w_z, w_out.T, w_x, w_bc, w_dt.T))
    small = jnp.concatenate(
        [conv_x, gate_gain[None], jnp.pad(head_params, ((0, 0), (0, wide - heads)))[:2]]
    )
    small = jnp.concatenate([small, jnp.pad(head_params[2:], ((0, 7), (0, wide - heads)))])
    small, weights = after(small, weights)
    small = jnp.where(core == xh, small, swap_core(small))

    mine = gather_plane(weights)
    hidden, weights = after(hidden_in, weights)
    hidden_blocks = to_workers(hidden)
    conv_x, gate_row, head_params = small[:5], small[5:6], small[6:9, :heads]
    taps, head, skip, spread = mixer_tables(conv_x, conv_bc, head_params)
    first_half, cot, taps, head, skip, spread, gate_row, meta, gain = after(
        hidden_blocks[:2], cotangent, taps, head, skip, spread, gate_row, meta, gain
    )
    hidden_blocks = first_half + hidden_blocks[2:]
    cot_blocks = to_workers(cot)
    tokens, tokens_t = place(meta, gain, hidden_blocks, True)
    tokens, mine, cot_first = after(tokens, mine, cot_blocks[0])
    cot_blocks = [cot_first] + cot_blocks[1:]
    other = swap_core(mine)

    pre, z = project(tokens, mine, other, wide)
    y, kept, conv = mixer_forward(pre, taps, head, skip, spread)
    y, cot_blocks = after(y, cot_blocks)
    cot, cot_t = place(meta, gain, cot_blocks, False)
    dy, sums = gate_sums(cot, mine, other, y, z, gate_row)
    normed_y, gate, dscan, gain_grad, keep, send = gate_back(
        block, 4.0 * wide, around(sums), z, dy, y, gate_row, tokens_t, cot_t
    )

    early = (keep.astype(F32) + swap_core(send).astype(F32)).astype(BF)
    out_blocks = project_out(meta, normed_y, mine, other)
    dscan, early, out_blocks = after(dscan, early, out_blocks)
    early = exchange(early)
    out_blocks = to_owners(out_blocks)
    late, conv_grad, head_grad = mixer_backward(pre, conv, dscan, kept, taps, head, skip, spread)
    *back_blocks, norm_part = project_back(
        meta, late, gate, mine, other, mine, other, tokens, gain
    )
    late, back_blocks, out_blocks = after(late, back_blocks, out_blocks)
    back_blocks = to_owners(back_blocks)

    rest = jnp.pad(
        jnp.concatenate([norm_part[:1, :wide], norm_part[:1, wide:], gain_grad[:1]]),
        ((0, 0), (0, states)),
    )
    vector = jnp.concatenate([jnp.concatenate([conv_grad[:5], rest]), head_grad], axis=1)
    vector = jnp.pad(vector, ((0, 8), (0, 0)))
    keep, send = weight_grad(tokens_t, late, vector)
    send, early, back_first = after(send, early, back_blocks[0])
    output = finish_output(meta, out_blocks, hidden_in)
    got = swap_core(send).astype(F32)
    half = keep.shape[0]
    late_sum = (keep + got[:half]).astype(BF).reshape(-1, block, both + 128)
    vector = (vector[:8] + got[half : half + 8]).astype(BF)
    vector = jnp.broadcast_to(vector[None], (late_sum.shape[0],) + vector.shape)
    late_sum = jnp.concatenate([late_sum, vector], axis=1)
    back_blocks = [back_first] + back_blocks[1:]
    early = trade(early.astype(F32).sum(axis=0))
    got, early, output = after(exchange(late_sum), early, output)
    own, shared = total_of(got, states)
    own, back_blocks = after(own, back_blocks)

    own, *shared = to_owners([own] + [shared] * 3)
    input_grad = finish_input(meta, back_blocks, hidden_in, cotangent, gain)
    norm_grad, x_grad, bc_grad, dt_grad, conv_x_grad, conv_bc_grad, head_part, gate_part = deliver(
        own, shared, block, heads
    )
    return (
        output,
        input_grad,
        norm_grad,
        early[0],
        x_grad,
        bc_grad,
        dt_grad.T,
        conv_x_grad,
        conv_bc_grad,
        head_part,
        gate_part,
        early[1].T,
    )


def solution(mesh):
    fine = Mesh(mesh.devices.reshape(2, 4, 4, 2, 2), AXES)
    rows, both, lanes = P(AXES, None), P(DP, TN), P(None, TN)
    return jax.shard_map(
        on_device,
        mesh=fine,
        in_specs=(rows, rows, P(), both, both, P(DP, None), both, lanes, P(), lanes, P(TN), P(TN, DP)),
        out_specs=(
            rows, rows, P(), both, both, P(DP, None), both, lanes, P(), lanes, P(TN), P(TN, DP)
        ),
        check_vma=False,
    )
```

```python
import functools
import jax
import jax.numpy as jnp
from jax import lax
from jax.experimental import pallas as pl
from jax.experimental.pallas import tpu as pltpu
from jax.sharding import Mesh, PartitionSpec as P

EPS = 1e-05
AXES = ("xh", "y", "z", "xl", "core")
DP = ("xh", "y", "z")
TN = ("xl", "core")
GROUP = ("xh", "xl", "core")
PLANE = ("y", "z")
BF = jnp.bfloat16
F32 = jnp.float32
SPAN = 128
LIMIT = 36


def near(value):
    return pltpu.with_memory_space_constraint(value, pltpu.VMEM)


def far(value):
    return pltpu.with_memory_space_constraint(value, pltpu.HBM)


ROWS = 512
SCALE = 1.15e9


def nn(left, right):
    return lax.dot_general(left, right, (((1,), (0,)), ((), ())), preferred_element_type=F32)


def nt(left, right):
    return lax.dot_general(left, right, (((1,), (1,)), ((), ())), preferred_element_type=F32)


def halves(value):
    high = value.astype(BF)
    low = (value - high.astype(F32)).astype(BF)
    return high, low


def running(mask, value):
    high, low = halves(value)
    return nn(jnp.concatenate([mask, mask], axis=1), jnp.concatenate([high, low], axis=0))


def close_nt(left, right):
    left_high, left_low = halves(left)
    right_high, right_low = halves(right)
    return nt(
        jnp.concatenate([left_high, left_high, left_low], axis=1),
        jnp.concatenate([right_high, right_low, right_high], axis=1),
    )


def expand(value, spread):
    high, low = halves(value)
    return nn(jnp.concatenate([high, low], axis=1), spread)


def by_head(value, spread):
    width = spread.shape[0] // 2
    high, low = halves(value)
    one = spread[:width]
    return nt(jnp.concatenate([high, low], axis=1), jnp.concatenate([one, one], axis=1))


def logistic(value):
    return 1.0 / (1.0 + jnp.exp(-value))


def sigmoid(value):
    return 0.5 * jnp.tanh(0.5 * value) + 0.5


def softplus(value):
    return jnp.maximum(value, 0.0) + jnp.log1p(jnp.exp(-jnp.abs(value)))


def conv_rows(ext_ref, taps):
    total = taps[4:5] + ext_ref[5 : 5 + SPAN] * taps[0:1]
    for k in range(1, 4):
        total = total + ext_ref[5 + k : 5 + k + SPAN] * taps[k : k + 1]
    return total


def scan_parts(conv, pre_dt, head, spread, tri):
    sig = sigmoid(conv)
    xbc = conv * sig
    raw = pre_dt + head[1:2]
    step = softplus(raw)
    decay = running(tri, step * head[0:1])
    last = decay[SPAN - 1 : SPAN]
    grown = expand(jnp.concatenate([step, jnp.exp(decay), jnp.exp(last - decay)], axis=0), spread)
    step_x, start_x, end_x = grown[:SPAN], grown[SPAN : 2 * SPAN], grown[2 * SPAN :]
    return sig, xbc, raw, step, decay, step_x, start_x, end_x


def forward_kernel(
    pre_ref, taps_ref, head_ref, skip_ref, spread_ref, y_ref, kept_ref, conv_ref, ext_ref, state_ref
):
    inner = y_ref.shape[1]
    both = ext_ref.shape[1]

    @pl.when(pl.program_id(0) == 0)
    def _():
        ext_ref[0:8] = jnp.zeros((8, both), F32)
        state_ref[...] = jnp.zeros_like(state_ref)

    ext_ref[8 : 8 + SPAN] = pre_ref[:, :both]
    rows = lax.broadcasted_iota(jnp.int32, (SPAN, SPAN), 0)
    cols = lax.broadcasted_iota(jnp.int32, (SPAN, SPAN), 1)
    keep = rows >= cols
    tri = jnp.where(keep, 1.0, 0.0).astype(BF)
    spread = spread_ref[...]
    conv = conv_rows(ext_ref, taps_ref[...])
    conv_ref[...] = conv
    sig, xbc, raw, step, decay, step_x, start_x, end_x = scan_parts(
        conv, pre_ref[:, both:], head_ref[...], spread, tri
    )
    ext_ref[0:8] = ext_ref[SPAN : SPAN + 8]
    state_width = (both - inner) // 2
    x = xbc[:, :inner]
    b = xbc[:, inner : inner + state_width]
    c = xbc[:, inner + state_width :]
    decay_t = decay.T
    scaled = x * step_x
    low = scaled.astype(BF)
    scores = close_nt(c, b)
    state = state_ref[...]
    state_low = state.astype(BF)
    kept_ref[...] = state_low
    carried = nn(c.astype(BF), state_low) * start_x + x * skip_ref[...]
    left = cols < 64
    for pair in range(inner // 128):
        at = slice(128 * pair, 128 * pair + 128)
        x_pair = low[:, at]
        found = []
        for h in (2 * pair, 2 * pair + 1):
            gap = decay[:, h : h + 1] - decay_t[h : h + 1]
            weight = jnp.exp(jnp.where(keep, gap, -1e30)) * scores
            found.append(nn(weight.astype(BF), x_pair))
        y_ref[:, at] = jnp.where(left, found[0], found[1]) + carried[:, at]
    state_ref[...] = state * start_x[SPAN - 1 : SPAN] + nn(
        b.T.astype(BF), (scaled * end_x).astype(BF)
    )


def backward_kernel(
    pre_ref, conv_ref, dy_ref, kept_ref, taps_ref, head_ref, skip_ref, spread_ref,
    late_ref, conv_grad_ref, head_grad_ref,
    dext_ref, dstate_ref, skip_sum_ref,
):
    inner = dy_ref.shape[1]
    both = dext_ref.shape[1]
    steps = pl.num_programs(0)
    at_step = pl.program_id(0)

    @pl.when(at_step == 0)
    def _():
        dext_ref[SPAN : SPAN + 8] = jnp.zeros((8, both), F32)
        dstate_ref[...] = jnp.zeros_like(dstate_ref)
        skip_sum_ref[...] = jnp.zeros_like(skip_sum_ref)
        conv_grad_ref[...] = jnp.zeros_like(conv_grad_ref)
        head_grad_ref[...] = jnp.zeros_like(head_grad_ref)

    rows = lax.broadcasted_iota(jnp.int32, (SPAN, SPAN), 0)
    cols = lax.broadcasted_iota(jnp.int32, (SPAN, SPAN), 1)
    tri = jnp.where(rows >= cols, 1.0, 0.0).astype(BF)
    upper = jnp.where(cols >= rows, 1.0, 0.0).astype(BF)
    keep = cols >= rows
    spread = spread_ref[...]
    taps = taps_ref[...]
    head = head_ref[...]
    conv = conv_ref[...]
    sig, xbc, raw, step, decay, step_x, start_x, end_x = scan_parts(
        conv, pre_ref[:, both:], head, spread, tri
    )
    state_width = (both - inner) // 2
    x = xbc[:, :inner]
    b = xbc[:, inner : inner + state_width]
    c = xbc[:, inner + state_width :]
    b_low, c_low = b.astype(BF), c.astype(BF)
    decay_t = decay.T
    scaled = x * step_x
    low = scaled.astype(BF)
    scores = close_nt(b, c)
    dy = dy_ref[...].astype(F32)
    dy_low = dy.astype(BF)
    kept = kept_ref[...]
    dstate = dstate_ref[...]
    dstate_low = dstate.astype(BF)
    left = cols < 64
    wide_rows = lax.broadcasted_iota(jnp.int32, (SPAN, SPAN), 0)
    d_scores = jnp.zeros((SPAN, SPAN), F32)
    into = jnp.zeros((SPAN, SPAN), F32)
    out_of = jnp.zeros((SPAN, SPAN), F32)
    pieces = []
    none = jnp.zeros((SPAN, 128), BF)
    for pair in range(inner // 128):
        at = slice(128 * pair, 128 * pair + 128)
        x_pair = low[:, at]
        dy_pair = dy_low[:, at]
        found = []
        for side, h in enumerate((2 * pair, 2 * pair + 1)):
            gap = decay_t[h : h + 1] - decay[:, h : h + 1]
            fall = jnp.exp(jnp.where(keep, gap, -1e30))
            mine = jnp.where(left if side == 0 else ~left, dy_pair, none)
            back = nt(x_pair, mine) * fall
            d_scores = d_scores + back
            both_ways = back * scores
            into = jnp.where(wide_rows == h, jnp.sum(both_ways, axis=0, keepdims=True), into)
            out_of = jnp.where(cols == h, jnp.sum(both_ways, axis=1, keepdims=True), out_of)
            found.append(nn((fall * scores).astype(BF), dy_pair))
        pieces.append(jnp.where(left, found[0], found[1]))
    inside = jnp.concatenate(pieces, axis=1)
    dy_start = dy * start_x
    dy_start_low = dy_start.astype(BF)
    from_state = nn(c_low, kept)
    scaled_end = scaled * end_x
    d_end = nn(b_low, dstate_low)
    d_scaled = inside + d_end * end_x
    pair_start = by_head(dy_start * from_state, spread)
    pair_end = by_head(scaled_end * d_end, spread)
    d_scores_low = d_scores.astype(BF)
    d_c = nn(d_scores.T.astype(BF), b_low) + nt(dy_start_low, kept)
    d_b = nn(d_scores_low, c_low) + nt(scaled_end.astype(BF), dstate_low)
    through = jnp.sum(kept.astype(F32) * dstate, axis=0, keepdims=True)
    through = by_head(jnp.broadcast_to(through * start_x[SPAN - 1 : SPAN], (8, inner)), spread)[0:1]
    at_end = jnp.sum(pair_end, axis=0, keepdims=True) + through
    d_decay = into.T - out_of + pair_start - pair_end
    d_decay = d_decay + jnp.where(rows == SPAN - 1, at_end, 0.0)
    d_log = running(upper, d_decay)
    d_step = by_head(d_scaled * x, spread) + d_log * head[0:1]
    d_raw = d_step * logistic(raw)
    dstate_ref[...] = dstate * start_x[SPAN - 1 : SPAN] + nn(c.T.astype(BF), dy_start_low)
    late_ref[:, both:] = d_raw.astype(BF)
    head_grad_ref[0:1] += jnp.sum(d_log * step, axis=0, keepdims=True) * head[0:1]
    head_grad_ref[1:2] += jnp.sum(d_raw, axis=0, keepdims=True)
    skip_sum_ref[0:1] += jnp.sum(dy * x, axis=0, keepdims=True)
    dx = d_scaled * step_x + dy * skip_ref[...]
    d_conv = jnp.concatenate([dx, d_b, d_c], axis=1) * (sig * (1.0 + conv * (1.0 - sig)))
    dext_ref[0:SPAN] = d_conv
    values = pre_ref[:, :both]
    d_pre = d_conv * taps[3:4]
    conv_grad_ref[3:4] += jnp.sum(d_conv * values, axis=0, keepdims=True)
    for k in range(3):
        moved = dext_ref[3 - k : 3 - k + SPAN]
        d_pre = d_pre + moved * taps[k : k + 1]
        conv_grad_ref[k : k + 1] += jnp.sum(moved * values, axis=0, keepdims=True)
    conv_grad_ref[4:5] += jnp.sum(d_conv, axis=0, keepdims=True)
    dext_ref[SPAN : SPAN + 8] = dext_ref[0:8]
    late_ref[:, :both] = d_pre.astype(BF)

    @pl.when(at_step == steps - 1)
    def _():
        head_grad_ref[2:3] += by_head(
            jnp.broadcast_to(skip_sum_ref[0:1], (8, inner)), spread
        )[0:1]


def whole(shape):
    return pl.BlockSpec(shape, lambda *_: (0,) * len(shape))


def column(rows, width, shift=0):
    return pl.BlockSpec((rows, width), lambda j, *_: (0, j + shift))


def shape_of(shape, dtype):
    return jax.ShapeDtypeStruct(shape, dtype)


def stored(shape, dtype):
    return pltpu.HBM(shape, dtype)


def held_near(shape, dtype):
    return pltpu.VMEM(shape, dtype)


def params(limit, *semantics):
    return pltpu.CompilerParams(
        dimension_semantics=semantics or None, vmem_limit_bytes=LIMIT * 1024 * 1024
    )


def lasting(us):
    return pl.CostEstimate(flops=int(us * SCALE), bytes_accessed=1024, transcendentals=0)


def place_kernel(normalise, meta_ref, gain_ref, *refs):
    blocks, out_ref, flip_ref = refs[:4], refs[4], refs[5]
    rows, width = blocks[0].shape
    half = width // 2
    core = meta_ref[4]
    first = pl.multiple_of(core * half, 128)
    second = pl.multiple_of((1 - core) * half, 128)
    for k, block in enumerate(blocks):
        at = pl.multiple_of(meta_ref[k] * rows, rows)
        value = block[...].astype(F32)
        if normalise:
            scale = lax.rsqrt(jnp.mean(value * value, axis=1, keepdims=True) + EPS)
            value = value * scale * gain_ref[...]
        low = value.astype(BF)
        out_ref[pl.ds(at, rows), pl.ds(first, half)] = low[:, :half]
        out_ref[pl.ds(at, rows), pl.ds(second, half)] = low[:, half:]
        flip = value.T.astype(BF)
        flip_ref[pl.ds(first, half), pl.ds(at, rows)] = flip[:half]
        flip_ref[pl.ds(second, half), pl.ds(at, rows)] = flip[half:]


def place(meta, gain, blocks, normalise):
    rows, width = blocks[0].shape
    vmem = pl.BlockSpec()
    return pl.pallas_call(
        functools.partial(place_kernel, normalise),
        in_specs=[pl.BlockSpec(memory_space=pltpu.SMEM)] + [vmem] * 5,
        out_specs=[vmem, vmem],
        out_shape=[
            (stored if normalise else shape_of)((4 * rows, width), BF),
            shape_of((width, 4 * rows), BF),
        ],
        compiler_params=params(24),
        cost_estimate=lasting(6),
        name="place_normed" if normalise else "place_cotangent",
    )(meta, gain, *[far(block) for block in blocks])


def project_kernel(tokens_ref, xm_ref, xo_ref, zm_ref, zo_ref, pre_ref, z_ref):
    half = xm_ref.shape[0]
    for first, second, out in ((xm_ref, xo_ref, pre_ref), (zm_ref, zo_ref, z_ref)):
        out[...] = nn(tokens_ref[:, :half], first[...]) + nn(tokens_ref[:, half:], second[...])


def project(tokens, mine, other, inner):
    half = mine.shape[0]
    length = tokens.shape[0]
    columns = mine.shape[1] - 2 * inner
    rows = ROWS

    def part(width, shift):
        return pl.BlockSpec(
            (pl.Element(half), pl.Element(width)),
            lambda i: (0, shift),
            pipeline_mode=pl.Buffered(1),
        )

    return pl.pallas_call(
        project_kernel,
        grid=(length // rows,),
        in_specs=[pl.BlockSpec((rows, 2 * half), lambda i: (i, 0))]
        + [part(columns, 2 * inner)] * 2
        + [part(inner, 0)] * 2,
        out_specs=[
            pl.BlockSpec((rows, columns), lambda i: (i, 0)),
            pl.BlockSpec((rows, inner), lambda i: (i, 0)),
        ],
        out_shape=[shape_of((length, columns), F32), shape_of((length, inner), F32)],
        compiler_params=params(20, "arbitrary"),
        cost_estimate=lasting(6),
        name="project_in",
    )(far(tokens), far(mine), other, far(mine), other)


def gate_sums_kernel(
    cot_ref, om_ref, oo_ref, y_ref, z_ref, gain_ref, dy_ref, sums_ref
):
    half = om_ref.shape[0]
    z = z_ref[...]
    dy = nn(cot_ref[:, :half], om_ref[...]) + nn(cot_ref[:, half:], oo_ref[...])
    dy_ref[...] = dy
    gated = y_ref[...] * (z * sigmoid(z))
    ones = jnp.ones((8, z.shape[1]), BF)
    found = []
    for value in (gated * gated, gated * (dy * gain_ref[...])):
        high, low = halves(value)
        found.append(nt(ones, high) + nt(ones, low))
    row = lax.broadcasted_iota(jnp.int32, found[0].shape, 0)
    total = jnp.where(row == 0, found[0], found[1])

    @pl.when(pl.program_id(0) == 0)
    def _():
        sums_ref[...] = total

    @pl.when(pl.program_id(0) > 0)
    def _():
        sums_ref[...] += total


def gate_sums(cot, mine, other, y, z, gain):
    length, inner = y.shape
    half = mine.shape[0]
    tile = 256
    steps = inner // tile
    return pl.pallas_call(
        gate_sums_kernel,
        grid=(steps,),
        in_specs=[
            whole(cot.shape),
            column(half, tile, steps),
            column(half, tile, steps),
            column(length, tile),
            column(length, tile),
            column(1, tile),
        ],
        out_specs=[column(length, tile), whole((8, length))],
        out_shape=[shape_of((length, inner), F32), shape_of((8, length), F32)],
        compiler_params=params(36, "arbitrary"),
        cost_estimate=lasting(6),
        name="gate_sums",
    )(near(cot), far(mine), far(other), near(y), near(z), gain)


def gate_back_kernel(
    width_all, s0, s1, s2, s3, z_ref, dy_ref, y_ref, gain_ref, tokens_t_ref, cot_t_ref,
    normed_ref, gate_ref, dscan_ref, gain_grad_ref, keep_ref, send_ref,
):
    sums = (s0[...] + s1[...]) + (s2[...] + s3[...])
    flat = sums.T
    rms = lax.rsqrt(flat[:, 0:1] / width_all + EPS)
    inner = flat[:, 1:2] * (rms * rms * rms / width_all)
    z = z_ref[...]
    y = y_ref[...]
    dy = dy_ref[...]
    gain = gain_ref[...]
    sig = sigmoid(z)
    act = z * sig
    gated = y * act
    unit = gated * rms
    normed = (unit * gain).astype(BF)
    normed_ref[...] = normed
    gain_grad_ref[...] = jnp.broadcast_to(
        jnp.sum(dy * unit, axis=0, keepdims=True), gain_grad_ref.shape
    )
    d_gated = rms * (dy * gain) - gated * inner
    dscan_ref[...] = d_gated * act
    gate = (d_gated * y * (sig * (1.0 + z * (1.0 - sig)))).astype(BF)
    gate_ref[...] = gate
    half = tokens_t_ref.shape[0] // 2
    for side, (left, right) in enumerate(((tokens_t_ref, gate), (cot_t_ref, normed))):
        for out, at in ((keep_ref, slice(0, half)), (send_ref, slice(half, 2 * half))):
            found = nn(left[at], right).astype(BF)
            out[:, side] = found.reshape(out.shape[0], out.shape[2], found.shape[1])


def gate_back(block, width_all, sums, z, dy, y, gain, tokens_t, cot_t):
    length, inner = y.shape
    half = tokens_t.shape[0] // 2
    tile = 256
    pile = pl.BlockSpec((half // block, 2, block, tile), lambda j: (0, 0, 0, j))
    return pl.pallas_call(
        functools.partial(gate_back_kernel, width_all),
        grid=(inner // tile,),
        in_specs=[whole((8, length))] * 4
        + [column(length, tile)] * 3
        + [column(1, tile), whole(tokens_t.shape), whole(cot_t.shape)],
        out_specs=[column(length, tile)] * 3 + [column(8, tile), pile, pile],
        out_shape=[
            stored((length, inner), BF),
            stored((length, inner), BF),
            stored((length, inner), F32),
            shape_of((8, inner), F32),
            shape_of((half // block, 2, block, inner), BF),
            shape_of((half // block, 2, block, inner), BF),
        ],
        compiler_params=params(44, "arbitrary"),
        cost_estimate=lasting(12),
        name="gate_back",
    )(*sums, near(z), near(dy), near(y), gain, near(tokens_t), near(cot_t))


def scatter_rows(meta_ref, found, scratch, outs):
    rows = outs[0].shape[0]
    scratch[...] = found
    for k, out in enumerate(outs):
        out[...] = scratch[pl.ds(pl.multiple_of(meta_ref[k] * rows, rows), rows), :].astype(BF)


def project_out_kernel(meta_ref, normed_ref, om_ref, oo_ref, *refs):
    outs, scratch = refs[:4], refs[4]

    def step(right):
        scatter_rows(meta_ref, nt(normed_ref[...], right[...]), scratch, outs)

    first = pl.program_id(0) < pl.num_programs(0) // 2
    pl.when(first)(lambda: step(om_ref))
    pl.when(jnp.logical_not(first))(lambda: step(oo_ref))


def sides(tile, columns, shift, per):
    return [
        pl.BlockSpec(
            (pl.Element(tile), pl.Element(columns)),
            lambda j: (jnp.minimum(j, per - 1) * tile, shift),
        ),
        pl.BlockSpec(
            (pl.Element(tile), pl.Element(columns)),
            lambda j: (jnp.maximum(j - per, 0) * tile, shift),
        ),
    ]


def project_out(meta, normed_y, mine, other):
    length, inner = normed_y.shape
    half = mine.shape[0]
    rows = length // 4
    per = 3
    tile = half // per
    return pl.pallas_call(
        project_out_kernel,
        grid=(2 * per,),
        in_specs=[pl.BlockSpec(memory_space=pltpu.SMEM), whole(normed_y.shape)]
        + sides(tile, inner, inner, per),
        out_specs=[column(rows, tile)] * 4,
        out_shape=[stored((rows, 2 * half), BF)] * 4,
        scratch_shapes=[pltpu.VMEM((length, tile), F32)],
        compiler_params=params(24, "arbitrary"),
        cost_estimate=lasting(6),
        name="project_out",
    )(meta, far(normed_y), far(mine), far(other))


def project_back_kernel(
    meta_ref, late_ref, gate_ref, xm_ref, xo_ref, zm_ref, zo_ref, tokens_ref, gain_ref, *refs
):
    outs, grad_ref, scratch = refs[:4], refs[4], refs[5]
    tile = scratch.shape[1]
    j = pl.program_id(0)
    per = pl.num_programs(0) // 2
    side, within = j // per, j % per
    core = meta_ref[4]

    def step(x_ref, z_ref):
        found = nt(late_ref[...], x_ref[...]) + nt(gate_ref[...], z_ref[...])
        total = jnp.sum(found * tokens_ref[...].astype(F32), axis=0, keepdims=True)
        owner = side + core - 2 * side * core
        place = pl.ds(pl.multiple_of((per * owner + within) * tile, 128), tile)
        grad_ref[:, place] = jnp.broadcast_to(total / gain_ref[:, place], (8, tile))
        scatter_rows(meta_ref, found, scratch, outs)

    pl.when(side == 0)(lambda: step(xm_ref, zm_ref))
    pl.when(side == 1)(lambda: step(xo_ref, zo_ref))


def project_back(meta, late, gate, mine1, other1, mine2, other2, tokens, gain):
    length, columns = late.shape
    inner = gate.shape[1]
    half = mine1.shape[0]
    rows = length // 4
    per = 3
    tile = half // per
    return pl.pallas_call(
        project_back_kernel,
        grid=(2 * per,),
        in_specs=[pl.BlockSpec(memory_space=pltpu.SMEM), whole(late.shape), whole(gate.shape)]
        + sides(tile, columns, 2 * inner, per)
        + sides(tile, inner, 0, per)
        + [column(length, tile), whole(gain.shape)],
        out_specs=[column(rows, tile)] * 4 + [whole((8, 2 * half))],
        out_shape=[stored((rows, 2 * half), BF)] * 4 + [shape_of((8, 2 * half), F32)],
        scratch_shapes=[pltpu.VMEM((length, tile), F32)],
        compiler_params=params(32, "arbitrary"),
        cost_estimate=lasting(0.5),
        name="project_back",
    )(
        meta, near(late), far(gate), far(mine1), far(other1), far(mine2), far(other2), far(tokens), gain
    )


def weight_grad_kernel(tokens_t_ref, late_ref, vector_ref, keep_ref, send_ref):
    half = keep_ref.shape[0]
    late = late_ref[...]
    keep_ref[...] = nn(tokens_t_ref[:half], late)
    send_ref[:half] = nn(tokens_t_ref[half:], late).astype(BF)
    send_ref[half:] = vector_ref[...].astype(BF)


def weight_grad(tokens_t, late, vector):
    length, columns = late.shape
    half = tokens_t.shape[0] // 2
    rows = half + vector.shape[0]
    tile = 384
    return pl.pallas_call(
        weight_grad_kernel,
        grid=(columns // tile,),
        in_specs=[whole(tokens_t.shape), column(length, tile), column(vector.shape[0], tile)],
        out_specs=[column(half, tile), column(rows, tile)],
        out_shape=[stored((half, columns), F32), stored((rows, columns), BF)],
        compiler_params=params(24, "arbitrary"),
        cost_estimate=lasting(0.5),
        name="weight_grad",
    )(far(tokens_t), near(late), vector)


def pack_kernel(z_ref, out_ref, x_ref, bc_ref, dt_ref, packed_ref):
    at = 0
    for ref in (z_ref, out_ref, x_ref, bc_ref):
        packed_ref[:, at : at + ref.shape[1]] = ref[...]
        at += ref.shape[1]
    heads, rows = dt_ref.shape
    tall = jnp.concatenate([dt_ref[...].astype(F32), jnp.zeros((128 - heads, rows), F32)], axis=0)
    packed_ref[:, at:] = tall.T.astype(BF)


def pack(*parts):
    vmem = pl.BlockSpec()
    return pl.pallas_call(
        pack_kernel,
        in_specs=[vmem] * 5,
        out_specs=vmem,
        out_shape=shape_of(
            (parts[0].shape[0], sum(part.shape[1] for part in parts[:4]) + 128), BF
        ),
        compiler_params=params(8),
        cost_estimate=lasting(1),
        name="pack_weights",
    )(*[far(part) for part in parts])


def total_kernel(states, got_ref, joint_ref, shared_ref):
    total = jnp.sum(got_ref[...].astype(F32), axis=0)
    rows = total.shape[0]
    inner = joint_ref.shape[1] - 128 - states
    both = inner + states
    joint_ref[...] = jnp.zeros_like(joint_ref)
    joint_ref[:rows, :inner] = total[:, :inner]
    joint_ref[:rows, inner : inner + 128] = total[:, both:]
    shared_ref[:rows] = total[:, inner:both]
    per = inner // states
    for k in range(2 * per):
        line = rows - 3 + k // per
        at = states * (k % per)
        shared_ref[rows + k : rows + k + 1] = total[line : line + 1, at : at + states]
    joint_ref[:, inner + 128 :] = shared_ref[...]


def total_of(got, states):
    count, rows, columns = got.shape
    vmem = pl.BlockSpec()
    extra = rows + 2 * ((columns - states - 128) // states)
    return pl.pallas_call(
        functools.partial(total_kernel, states),
        in_specs=[vmem],
        out_specs=[vmem, vmem],
        out_shape=[shape_of((extra, columns), F32), shape_of((extra, states), F32)],
        compiler_params=params(16),
        cost_estimate=lasting(3),
        name="late_total",
    )(got)


def deliver_kernel(
    joint_ref, s1, s2, s3,
    norm_ref, x_ref, bc_ref, dt_ref, conv_x_ref, conv_bc_ref, head_ref, gate_ref,
):
    block, inner = x_ref.shape
    own = joint_ref[:, : inner + 128]
    shared = (joint_ref[:, inner + 128 :] + s1[...]) + (s2[...] + s3[...])
    heads = dt_ref.shape[0]
    x_ref[...] = own[:block, :inner]
    dt_ref[...] = own[:block, inner:].T[:heads]
    conv_x_ref[...] = own[block : block + 5, :inner]
    head_ref[...] = own[block : block + 3, inner : inner + heads]
    gate_ref[...] = own[block + 7, :inner]
    bc_ref[...] = shared[:block]
    conv_bc_ref[...] = shared[block : block + 5]
    states = bc_ref.shape[1]
    for k in range(norm_ref.shape[0] // states):
        norm_ref[states * k : states * k + states] = shared[block + 8 + k]


def deliver(own, shared, block, heads):
    vmem = pl.BlockSpec()
    states = shared[0].shape[1]
    inner = own.shape[1] - 128 - states
    shapes = [
        (2 * inner,), (block, inner), (block, states), (heads, block),
        (5, inner), (5, states), (3, heads), (inner,),
    ]
    return pl.pallas_call(
        deliver_kernel,
        in_specs=[vmem] * 4,
        out_specs=[vmem] * 8,
        out_shape=[shape_of(shape, F32) for shape in shapes],
        compiler_params=params(16),
        cost_estimate=lasting(2),
        name="deliver_late",
    )(own, *shared)


def owner_total(xh_ref, blocks):
    total = sum(block[...].astype(F32) for block in blocks)
    half = total.shape[1] // 2
    turned = jnp.concatenate([total[:, half:], total[:, :half]], axis=1)
    return jnp.where(xh_ref[5] == 0, total, turned)


def output_kernel(meta_ref, b0, b1, b2, b3, hidden_ref, out_ref):
    mixed = owner_total(meta_ref, (b0, b1, b2, b3))
    out_ref[...] = (hidden_ref[...].astype(F32) + mixed).astype(BF)


def finish_output(meta, blocks, hidden):
    vmem = pl.BlockSpec()
    return pl.pallas_call(
        output_kernel,
        in_specs=[pl.BlockSpec(memory_space=pltpu.SMEM)] + [vmem] * 5,
        out_specs=vmem,
        out_shape=shape_of(hidden.shape, BF),
        compiler_params=params(16),
        cost_estimate=lasting(3),
        name="finish_output",
    )(meta, *[far(block) for block in blocks], far(hidden))


def input_kernel(meta_ref, b0, b1, b2, b3, hidden_ref, cot_ref, gain_ref, out_ref):
    scaled = owner_total(meta_ref, (b0, b1, b2, b3)) * gain_ref[...]
    resid = hidden_ref[...].astype(F32)
    inv = lax.rsqrt(jnp.mean(resid * resid, axis=1, keepdims=True) + EPS)
    along = jnp.mean(resid * scaled, axis=1, keepdims=True) * (inv * inv * inv)
    out_ref[...] = inv * scaled - resid * along + cot_ref[...].astype(F32)


def finish_input(meta, blocks, hidden, cot, gain):
    vmem = pl.BlockSpec()
    return pl.pallas_call(
        input_kernel,
        in_specs=[pl.BlockSpec(memory_space=pltpu.SMEM)] + [vmem] * 7,
        out_specs=vmem,
        out_shape=shape_of(hidden.shape, F32),
        compiler_params=params(16),
        cost_estimate=lasting(3),
        name="finish_input",
    )(meta, *blocks, far(hidden), far(cot), gain)


def mixer_tables(conv_x, conv_bc, head_params):
    heads = head_params.shape[1]
    inner = conv_x.shape[1]
    taps = jnp.pad(jnp.concatenate([conv_x, conv_bc], axis=1), ((0, 3), (0, 0)))
    head = jnp.stack([-jnp.exp(head_params[0]), head_params[1]])
    head = jnp.pad(head, ((0, 6), (0, 128 - heads)))
    skip = jnp.repeat(head_params[2], inner // heads)[None]
    owner = lax.broadcasted_iota(jnp.int32, (256, inner), 1) // (inner // heads)
    one = owner == lax.broadcasted_iota(jnp.int32, (256, inner), 0) % 128
    return taps, head, skip, one.astype(BF)


def mixer_forward(pre, taps, head, skip, spread):
    length, columns = pre.shape
    both = taps.shape[1]
    inner = skip.shape[1]
    steps = length // SPAN
    return pl.pallas_call(
        forward_kernel,
        grid=(steps,),
        in_specs=[
            pl.BlockSpec((SPAN, columns), lambda i: (i, 0)),
            whole(taps.shape), whole(head.shape), whole(skip.shape), whole(spread.shape),
        ],
        out_specs=[
            pl.BlockSpec((SPAN, inner), lambda i: (i, 0)),
            pl.BlockSpec((128, inner), lambda i: (i, 0)),
            pl.BlockSpec((SPAN, both), lambda i: (i, 0)),
        ],
        out_shape=[
            shape_of((length, inner), F32),
            stored((steps * 128, inner), BF),
            stored((length, both), F32),
        ],
        scratch_shapes=[pltpu.VMEM((SPAN + 8, both), F32), pltpu.VMEM((128, inner), F32)],
        compiler_params=params(20, "arbitrary"),
        cost_estimate=lasting(13),
        name="mixer_forward",
    )(near(pre), taps, head, skip, spread)


def mixer_backward(pre, conv, dy, kept, taps, head, skip, spread):
    length, columns = pre.shape
    both = taps.shape[1]
    inner = skip.shape[1]
    steps = length // SPAN
    last = steps - 1
    return pl.pallas_call(
        backward_kernel,
        grid=(steps,),
        in_specs=[
            pl.BlockSpec((SPAN, columns), lambda i: (last - i, 0)),
            pl.BlockSpec((SPAN, both), lambda i: (last - i, 0)),
            pl.BlockSpec((SPAN, inner), lambda i: (last - i, 0)),
            pl.BlockSpec((128, inner), lambda i: (last - i, 0)),
            whole(taps.shape), whole(head.shape), whole(skip.shape), whole(spread.shape),
        ],
        out_specs=[
            pl.BlockSpec((SPAN, columns), lambda i: (last - i, 0)),
            whole((8, both)),
            whole((8, 128)),
        ],
        out_shape=[
            held_near((length, columns), BF),
            shape_of((8, both), F32),
            shape_of((8, 128), F32),
        ],
        scratch_shapes=[
            pltpu.VMEM((SPAN + 8, both), F32),
            pltpu.VMEM((128, inner), F32),
            pltpu.VMEM((8, inner), F32),
        ],
        compiler_params=params(24, "arbitrary"),
        cost_estimate=lasting(30),
        name="mixer_backward",
    )(far(pre), far(conv), far(dy), far(kept), taps, head, skip, spread)


CELLS = [(xh, xl, core) for xh in range(2) for xl in range(2) for core in range(2)]
TURNS = [(a, b) for a in range(2) for b in range(2)]


def moves(rule):
    return [(4 * c[0] + 2 * c[1] + c[2], 4 * d[0] + 2 * d[1] + d[2]) for c in CELLS for d in [rule(*c)]]


def permute(value, rule):
    return lax.ppermute(value, GROUP, moves(rule))


def trade(value):
    return permute(
        value, lambda xh, xl, core: (xh, xl, core) if xh == core else (1 - xh, xl, 1 - core)
    )


def swap_core(value):
    return lax.ppermute(value, "core", [(0, 1), (1, 0)])


def to_workers(value):
    return [
        permute(value, lambda xh, xl, core, a=a, b=b: (core ^ a, xl ^ b, xh)) for a, b in TURNS
    ]


def to_owners(blocks):
    return [
        permute(block, lambda xh, xl, core, a=a, b=b: (core, xl ^ b, xh ^ a))
        for block, (a, b) in zip(blocks, TURNS)
    ]


def around(value):
    return [value] + [
        permute(value, lambda xh, xl, core, a=a, b=b: (xh ^ a, xl ^ b, core)) for a, b in TURNS[1:]
    ]


def gather_plane(shard):
    count = lax.axis_size(PLANE)
    spread = jnp.broadcast_to(shard[None], (count,) + shard.shape)
    got = lax.all_to_all(spread, PLANE, 0, 0, tiled=True)
    return got.reshape((count * shard.shape[0],) + shard.shape[1:])


def exchange(blocks):
    return lax.all_to_all(blocks, PLANE, 0, 0, tiled=True)


def after(*values):
    return lax.optimization_barrier(values)


def on_device(
    hidden_in,
    cotangent,
    norm_gain,
    w_z,
    w_x,
    w_bc,
    w_dt,
    conv_x,
    conv_bc,
    head_params,
    gate_gain,
    w_out,
):
    block, wide = w_x.shape
    states = w_bc.shape[1]
    heads = w_dt.shape[1]
    both = wide + states
    xh, xl, core = (lax.axis_index(axis) for axis in GROUP)
    meta = jnp.stack([(xl ^ b) * 2 + (xh ^ a) for a, b in TURNS] + [core, xh]).astype(jnp.int32)
    gain = norm_gain[None]

    weights = trade(pack(w_z, w_out.T, w_x, w_bc, w_dt.T))
    small = jnp.concatenate(
        [conv_x, gate_gain[None], jnp.pad(head_params, ((0, 0), (0, wide - heads)))[:2]]
    )
    small = jnp.concatenate([small, jnp.pad(head_params[2:], ((0, 7), (0, wide - heads)))])
    small, weights = after(small, weights)
    small = jnp.where(core == xh, small, swap_core(small))

    mine = gather_plane(weights)
    hidden, weights = after(hidden_in, weights)
    hidden_blocks = to_workers(hidden)
    conv_x, gate_row, head_params = small[:5], small[5:6], small[6:9, :heads]
    taps, head, skip, spread = mixer_tables(conv_x, conv_bc, head_params)
    first_half, cot, taps, head, skip, spread, gate_row, meta, gain = after(
        hidden_blocks[:2], cotangent, taps, head, skip, spread, gate_row, meta, gain
    )
    hidden_blocks = first_half + hidden_blocks[2:]
    cot_blocks = to_workers(cot)
    tokens, tokens_t = place(meta, gain, hidden_blocks, True)
    tokens, mine, cot_first = after(tokens, mine, cot_blocks[0])
    cot_blocks = [cot_first] + cot_blocks[1:]
    other = swap_core(mine)

    pre, z = project(tokens, mine, other, wide)
    y, kept, conv = mixer_forward(pre, taps, head, skip, spread)
    y, cot_blocks = after(y, cot_blocks)
    cot, cot_t = place(meta, gain, cot_blocks, False)
    dy, sums = gate_sums(cot, mine, other, y, z, gate_row)
    normed_y, gate, dscan, gain_grad, keep, send = gate_back(
        block, 4.0 * wide, around(sums), z, dy, y, gate_row, tokens_t, cot_t
    )

    early = (keep.astype(F32) + swap_core(send).astype(F32)).astype(BF)
    out_blocks = project_out(meta, normed_y, mine, other)
    dscan, early, out_blocks = after(dscan, early, out_blocks)
    early = exchange(early)
    out_blocks = to_owners(out_blocks)
    late, conv_grad, head_grad = mixer_backward(pre, conv, dscan, kept, taps, head, skip, spread)
    *back_blocks, norm_part = project_back(
        meta, late, gate, mine, other, mine, other, tokens, gain
    )
    late, back_blocks, out_blocks = after(late, back_blocks, out_blocks)
    back_blocks = to_owners(back_blocks)

    rest = jnp.pad(
        jnp.concatenate([norm_part[:1, :wide], norm_part[:1, wide:], gain_grad[:1]]),
        ((0, 0), (0, states)),
    )
    vector = jnp.concatenate([jnp.concatenate([conv_grad[:5], rest]), head_grad], axis=1)
    vector = jnp.pad(vector, ((0, 8), (0, 0)))
    keep, send = weight_grad(tokens_t, late, vector)
    send, early, back_first = after(send, early, back_blocks[0])
    output = finish_output(meta, out_blocks, hidden_in)
    got = swap_core(send).astype(F32)
    half = keep.shape[0]
    late_sum = (keep + got[:half]).astype(BF).reshape(-1, block, both + 128)
    vector = (vector[:8] + got[half : half + 8]).astype(BF)
    vector = jnp.broadcast_to(vector[None], (late_sum.shape[0],) + vector.shape)
    late_sum = jnp.concatenate([late_sum, vector], axis=1)
    back_blocks = [back_first] + back_blocks[1:]
    early = trade(early.astype(F32).sum(axis=0))
    got, early, output = after(exchange(late_sum), early, output)
    own, shared = total_of(got, states)
    own, back_blocks = after(own, back_blocks)

    own, *shared = to_owners([own] + [shared] * 3)
    input_grad = finish_input(meta, back_blocks, hidden_in, cotangent, gain)
    norm_grad, x_grad, bc_grad, dt_grad, conv_x_grad, conv_bc_grad, head_part, gate_part = deliver(
        own, shared, block, heads
    )
    return (
        output,
        input_grad,
        norm_grad,
        early[0],
        x_grad,
        bc_grad,
        dt_grad.T,
        conv_x_grad,
        conv_bc_grad,
        head_part,
        gate_part,
        early[1].T,
    )


def solution(mesh):
    fine = Mesh(mesh.devices.reshape(2, 4, 4, 2, 2), AXES)
    rows, both, lanes = P(AXES, None), P(DP, TN), P(None, TN)
    return jax.shard_map(
        on_device,
        mesh=fine,
        in_specs=(rows, rows, P(), both, both, P(DP, None), both, lanes, P(), lanes, P(TN), P(TN, DP)),
        out_specs=(
            rows, rows, P(), both, both, P(DP, None), both, lanes, P(), lanes, P(TN), P(TN, DP)
        ),
        check_vma=False,
    )
```
